128 devices in a mesh: orb: 32 (over z_hi, x, y), slab: 4 (over z_lo, core).
Axes of the slice: x: 4, y: 4, z: 4 (z_hi: 2, z_lo: 2; z = z_hi * 2 + z_lo), core: 2. Of those that a mesh axis runs over, the one named last changes fastest.
Arguments:
- orbitals: float32 [32, 2, 128, 32, 128], P('orb', None, None, 'slab'), may hold values from -7 to 7, as said below
- potential: float32 [128, 32, 128], P(None, 'slab'), may hold values from 0 to 2
- occupation: float32 [32], P('orb'), may hold values from 0.5 to 2
- e_field: float32 [3, 128, 32, 128], P(None, 'orb', 'slab'), may hold values from -3 to 3
- a_field: float32 [3, 128, 32, 128], P(None, 'orb', 'slab'), may hold values from -1.8 to 1.8
Outputs:
- orbitals_next: float32 [32, 2, 128, 32, 128], P('orb', None, None, 'slab')
- electric_field: float32 [3, 128, 32, 128], P(None, 'orb', 'slab')
- vector_potential: float32 [3, 128, 32, 128], P(None, 'orb', 'slab')
The draws below stay inside these ranges and needn't reach their ends.
Inputs may be any that keep to these rules, and one draw needn't show every extreme that they name: `orbitals`: real and imaginary parts of each orbital at each cell.
All inputs are finite; a program needn't handle non-finite values.
Results may differ from the reference program's by a relative error of at most 0.0003.
Values sent between devices are 32-bit elements; how exact they have to be, the bound alone decides.
No kernel may reach another device: no remote copies, remote signals or barrier semaphores. Data moves between devices by JAX's collectives and lax.ppermute only.
A program may use at most 64 MiB of HBM per device.

```python
import math
import jax
import jax.numpy as jnp
from jax import lax

ORBS = 32
NX = 128
NY = 128
NZ = 32
TERMS = 4
STEPS = 2


def draw_orbitals(key, part):
    depth = jnp.arange(NZ).astype(jnp.float32) / (NZ - 1)
    shape = (ORBS, 2, NX, NZ, NY)
    values = jnp.clip(jax.random.normal(key, shape, jnp.float32), -4.0, 4.0)
    ramp = jnp.sqrt(1.0 + 2.0 * depth)
    return values * ramp[None, None, None, :, None]


def levels(key, shape, pieces, least, high):
    gain, own = 1.0, jax.random.fold_in(key, 6)
    for dim, shards_of in pieces:
        heights = jnp.exp(jax.random.uniform(jax.random.fold_in(own, dim), (shards_of,), jnp.float32, least / len(pieces), high / len(pieces)))
        gain = gain * jnp.repeat(heights, shape[dim] // shards_of).reshape([-1 if axis == dim else 1 for axis in range(len(shape))])
    return gain


def centred(own_key, shape, width, reach, split=(), held_as=jnp.bfloat16):
    drawn = width * jax.random.normal(own_key, shape, jnp.float32)
    if split:
        drawn = drawn * levels(own_key, shape, split, -0.22, 0.18)
    return jnp.clip(drawn, -reach, reach).astype(held_as)


def setup_inputs(seed: int = 0) -> dict:
    splits = jax.random.split(jax.random.key(seed), 6)
    return {
        "orbitals": draw_orbitals(jax.random.fold_in(splits[5], 71), 0),
        "potential": jnp.clip(2.0 * jax.random.uniform(splits[1], (NX, NZ, NY), jnp.float32) ** levels(splits[1], (NX, NZ, NY), ((1, 4),), -0.2, 0.2), 0.0, 2.0),
        "occupation": jnp.clip(jnp.exp(math.log(2.0) - 1.3862944 * jax.random.uniform(splits[2], (ORBS,), jnp.float32) ** levels(splits[2], (ORBS,), ((0, 32),), -0.2, 0.2)), 0.5, 2.0),
        "e_field": centred(splits[3], (3, NX, NZ, NY), 0.5, 3.0, ((1, 32), (2, 4)), jnp.float32),
        "a_field": centred(splits[4], (3, NX, NZ, NY), 0.3, 1.8, ((1, 32), (2, 4)), jnp.float32),
    }


time_step = 0.3
wave_step = 0.5
epsilon = 1e-06

def trim_axis(array, axis, start, stop):
    return lax.slice_in_dim(array, start, array.shape[axis] + stop, axis=axis)

def forward(field, axis):
    diff = trim_axis(field, axis, 1, 0) - trim_axis(field, axis, 0, -1)
    for other in (0, 1, 2):
        if other != axis:
            diff = trim_axis(diff, other, 0, -1)
    return diff

def backward(field, axis):
    diff = trim_axis(field, axis, 1, 0) - trim_axis(field, axis, 0, -1)
    for other in (0, 1, 2):
        if other != axis:
            diff = trim_axis(diff, other, 1, 0)
    return diff

def curl_of(field, differ):
    comp_x, comp_y, comp_z = (field[0], field[1], field[2])
    out_x = differ(comp_z, 2) - differ(comp_y, 1)
    out_y = differ(comp_x, 1) - differ(comp_z, 0)
    out_z = differ(comp_y, 0) - differ(comp_x, 2)
    return jnp.stack([out_x, out_y, out_z])

def double_curl(padded):
    return curl_of(curl_of(padded, forward), backward)

def neighbours(padded):
    center = padded[:, :, 1:-1, 1:-1, 1:-1]
    x_plus = padded[:, :, 2:, 1:-1, 1:-1]
    x_minus = padded[:, :, :-2, 1:-1, 1:-1]
    z_plus = padded[:, :, 1:-1, 2:, 1:-1]
    z_minus = padded[:, :, 1:-1, :-2, 1:-1]
    y_plus = padded[:, :, 1:-1, 1:-1, 2:]
    y_minus = padded[:, :, 1:-1, 1:-1, :-2]
    return (center, (x_plus, x_minus), (y_plus, y_minus), (z_plus, z_minus))

def hamiltonian(padded, field, weight):
    center, along_x, along_y, along_z = neighbours(padded)
    laplace = along_x[0] + along_x[1] + along_y[0] + along_y[1] + along_z[0] + along_z[1] - 6.0 * center
    drift = 0.5 * (field[0] * (along_x[0] - along_x[1]) + field[1] * (along_y[0] - along_y[1]) + field[2] * (along_z[0] - along_z[1]))
    real_h = -0.5 * laplace[:, 0] + drift[:, 1] + weight * center[:, 0]
    imag_h = -0.5 * laplace[:, 1] - drift[:, 0] + weight * center[:, 1]
    return (real_h, imag_h)

def taylor_term(real_h, imag_h, order):
    factor = time_step / order
    return jnp.stack([factor * imag_h, -factor * real_h], axis=1)

def current_density(padded, field, weights):
    center, along_x, along_y, along_z = neighbours(padded)
    real_c = center[:, 0]
    imag_c = center[:, 1]
    density = real_c * real_c + imag_c * imag_c
    parts = []
    for pair, comp in ((along_x, 0), (along_y, 1), (along_z, 2)):
        grad_r = 0.5 * (pair[0][:, 0] - pair[1][:, 0])
        grad_i = 0.5 * (pair[0][:, 1] - pair[1][:, 1])
        flow = real_c * grad_i - imag_c * grad_r + field[comp] * density
        parts.append(lax.optimization_barrier(jnp.sum(weights[:, None, None, None] * flow, axis=0)))
    return jnp.stack(parts)

def pad_all(array):
    return jnp.pad(array, ((0, 0), (0, 0), (1, 1), (1, 1), (1, 1)))

def reference(orbitals, potential, occupation, e_field, a_field):
    cells = NX * NZ * NY
    e_state = e_field
    a_state = a_field
    for step in range(STEPS):
        field = a_state
        weight = potential + 0.5 * lax.optimization_barrier(jnp.sum(field * field, axis=0))

        def advance(flow, item):
            orbital, occ = item
            block = orbital[None]
            total = block
            term = block
            for order in range(1, TERMS + 1):
                real_h, imag_h = hamiltonian(pad_all(term), field, weight)
                term = taylor_term(real_h, imag_h, order)
                total = total + term
            norm = jnp.sum(total * total)
            scale = 1.0 / jnp.sqrt(norm / cells + epsilon)
            normed = total * scale
            weights = (occ * (1.0 / ORBS))[None]
            flow = flow + current_density(pad_all(normed), field, weights)
            return (flow, normed[0])
        start = jnp.zeros((3, NX, NZ, NY), jnp.float32)
        flow, orbitals = lax.scan(advance, start, (orbitals, occupation))
        padded = jnp.pad(a_state, ((0, 0), (1, 1), (1, 1), (1, 1)))
        e_state = e_state + wave_step * (double_curl(padded) - flow)
        a_state = a_state - wave_step * e_state
    return (orbitals, e_state, a_state)
```

```python
import functools

import jax
import jax.numpy as jnp
from jax import lax
from jax.experimental import pallas as pl
from jax.experimental.pallas import tpu as pltpu
from jax.sharding import PartitionSpec as P

TERMS = 4
STEPS = 2
TIME_STEP = 0.3
WAVE_STEP = 0.5
EPSILON = 1e-06

NX = 128
NY = 128
NZ = 32
ORBS = 32
SLABS = 4
CELLS = NX * NY * NZ
DEPTH = NZ // SLABS
ROWS = NX // ORBS
HALO = TERMS + 1
MARGIN = TERMS
WIDE = DEPTH + 2 * HALO
PAD = 8
XP = NX + 2 * PAD
PACK = 3 * DEPTH * ROWS
CHUNK = 32
F32 = jnp.float32

CORE_PAIRS = [(0, 1), (1, 0), (2, 3), (3, 2)]
CHIP_PAIRS = [(1, 2), (2, 1)]


def vmem():
    return pl.BlockSpec(memory_space=pltpu.VMEM)


def smem():
    return pl.BlockSpec(memory_space=pltpu.SMEM)


def call(body, outs, ins, scratch=(), flops=1000000, limit=40):
    shapes = [jax.ShapeDtypeStruct(s, F32) for s in outs]
    size = sum(4 * s.size for s in shapes)
    return pl.pallas_call(
        body,
        out_shape=shapes,
        in_specs=ins,
        out_specs=[vmem()] * len(outs),
        scratch_shapes=list(scratch),
        compiler_params=pltpu.CompilerParams(vmem_limit_bytes=limit * 1024 * 1024),
        cost_estimate=pl.CostEstimate(flops=flops, bytes_accessed=2 * size, transcendentals=0),
    )


def core_index():
    return lax.rem(lax.axis_index("slab"), 2)


def lane_shifts(value):
    lane = lax.broadcasted_iota(jnp.int32, value.shape, value.ndim - 1)
    plus = jnp.where(lane == NY - 1, 0.0, pltpu.roll(value, NY - 1, value.ndim - 1))
    minus = jnp.where(lane == 0, 0.0, pltpu.roll(value, 1, value.ndim - 1))
    return plus, minus


def half_rows(shape):
    return lax.broadcasted_iota(jnp.int32, shape, len(shape) - 2) % 8 < 4


def prepare_body(orb_ref, pot_ref, wide_ref, weight_ref, core_ref, chip_ref):
    core = core_index()
    for z in range(DEPTH):
        for part in range(2):
            wide_ref[z + 1, part, PAD : PAD + NX, :] = orb_ref[part, pl.ds(z, NX, stride=DEPTH), :]
        weight_ref[z] = 2.0 * pot_ref[pl.ds(z, NX, stride=DEPTH), :] + 6.0
    to_core = 1 + (1 - core) * (DEPTH - HALO)
    to_chip = 1 + core * (DEPTH - HALO)
    for i in range(HALO):
        for part in range(2):
            core_ref[2 * i + part] = wide_ref[to_core + i, part, PAD : PAD + NX, :]
            chip_ref[2 * i + part] = wide_ref[to_chip + i, part, PAD : PAD + NX, :]
    for i in range(MARGIN):
        core_ref[2 * HALO + i] = weight_ref[(1 - core) * (DEPTH - MARGIN) + i]
        chip_ref[2 * HALO + i] = weight_ref[core * (DEPTH - MARGIN) + i]


def prepare(orbitals, potential):
    planes = 2 * HALO + MARGIN
    return call(
        prepare_body,
        [(DEPTH + 2, 2, XP, NY), (DEPTH, NX, NY), (planes, NX, NY), (planes, NX, NY)],
        [vmem(), vmem()],
    )(orbitals.reshape(2, NX * DEPTH, NY), potential.reshape(NX * DEPTH, NY))


def rims_body(wide_ref, core_ref, chip_ref):
    core = core_index()
    to_core = 1 + (1 - core) * (DEPTH - HALO)
    to_chip = 1 + core * (DEPTH - HALO)
    for i in range(HALO):
        for part in range(2):
            core_ref[2 * i + part] = wide_ref[to_core + i, part, PAD : PAD + NX, :]
            chip_ref[2 * i + part] = wide_ref[to_chip + i, part, PAD : PAD + NX, :]


def rims(wide):
    return call(rims_body, [(2 * HALO, NX, NY)] * 2, [vmem()])(wide)


def spread_body(a_ref, e_ref, copies_ref, a_rows_ref, e_rows_ref):
    for comp in range(3):
        for z in range(DEPTH):
            rows = pl.ds((comp * DEPTH + z) * ROWS, ROWS)
            a_rows_ref[rows, :] = a_ref[comp, pl.ds(z, ROWS, stride=DEPTH), :]
            e_rows_ref[rows, :] = e_ref[comp, pl.ds(z, ROWS, stride=DEPTH), :]
    value = a_rows_ref[...]
    for i in range(ORBS):
        copies_ref[i] = value


def spread(a_field, e_field):
    flat = (3, ROWS * DEPTH, NY)
    return call(spread_body, [(ORBS, PACK, NY), (PACK, NY), (PACK, NY)], [vmem(), vmem()])(
        a_field.reshape(flat), e_field.reshape(flat)
    )


def assemble_body(got_ref, field_ref, core_ref, chip_ref):
    core = core_index()
    low = half_rows((ORBS // 2, 8, NY))
    for comp in range(3):
        for pair in range(DEPTH // 2):
            rows = pl.ds((comp * DEPTH + 2 * pair) * ROWS, 8)
            first = got_ref[:, 0, rows, :]
            second = got_ref[:, 1, rows, :]
            even = jnp.where(low, first, pltpu.roll(second, 4, 1))
            odd = jnp.where(low, pltpu.roll(first, 4, 1), second)
            field_ref[2 * pair, comp] = even.reshape(NX, NY)
            field_ref[2 * pair + 1, comp] = odd.reshape(NX, NY)
    for i in range(MARGIN):
        for comp in range(3):
            core_ref[i, comp] = field_ref[(1 - core) * (DEPTH - MARGIN) + i, comp]
            chip_ref[i, comp] = field_ref[core * (DEPTH - MARGIN) + i, comp]


def assemble(got):
    return call(
        assemble_body,
        [(DEPTH, 3, NX, NY), (MARGIN, 3, NX, NY), (MARGIN, 3, NX, NY)],
        [vmem()],
    )(got.reshape(ORBS // 2, 2, PACK, NY))


def propagate_body(
    scale_ref, wide_ref, hcore_ref, hchip_ref, weight_ref, vcore_ref, vchip_ref, field_ref, acore_ref, achip_ref,
    out_ref, norm_ref, ping_ref, pong_ref, w_ref, a_ref,
):
    core = core_index()
    scale = scale_ref[0:1, :]
    edge = jnp.zeros((PAD, NY), F32)

    def clear(ref, count):
        @pl.loop(0, count)
        def _(j):
            for part in range(2):
                ref[j, part, 0:PAD, :] = edge
                ref[j, part, PAD + NX : XP, :] = edge

    clear(ping_ref, WIDE)
    clear(pong_ref, WIDE)
    clear(out_ref, DEPTH + 2)

    def put_field(j, plane, base):
        total = base
        for comp in range(3):
            value = plane[comp]
            a_ref[j, comp] = value
            total = total + value * value
        w_ref[j] = total

    @pl.loop(0, DEPTH)
    def _(z):
        for part in range(2):
            ping_ref[z + HALO, part, PAD : PAD + NX, :] = wide_ref[z + 1, part, PAD : PAD + NX, :] * scale
        put_field(z + MARGIN, field_ref[z], weight_ref[z])

    def put_halo(start, width, orb_ref, pot_ref, fld_ref):
        @pl.loop(0, HALO)
        def _(i):
            for part in range(2):
                ping_ref[start * (DEPTH + HALO) + i, part, PAD : PAD + NX, :] = orb_ref[2 * i + part] * scale

        @pl.loop(0, MARGIN)
        def _(i):
            put_field(start * (DEPTH + MARGIN) + i, fld_ref[i], pot_ref[i])

    @pl.when(core == 1)
    def _():
        put_halo(0, 0, hcore_ref, vcore_ref, acore_ref)
        put_halo(1, 0, hchip_ref, vchip_ref, achip_ref)

    @pl.when(core == 0)
    def _():
        put_halo(1, 0, hcore_ref, vcore_ref, acore_ref)
        put_halo(0, 0, hchip_ref, vchip_ref, achip_ref)

    slab = lax.axis_index("slab")
    source, target = ping_ref, pong_ref
    norm_ref[...] = jnp.zeros((8, NY), F32)
    for order in range(1, TERMS + 1):

        @pl.loop(order, WIDE - order)
        def _(j, order=order, source=source, target=target):
            depth = slab * DEPTH + j - HALO
            inside = jnp.where((depth >= 0) & (depth < NZ), 1.0, 0.0).astype(F32)
            factor = inside * (0.5 * TIME_STEP / order)
            own = j - HALO + 1
            squares = jnp.zeros((8, NY), F32)
            for r in range(0, NX, CHUNK):
                here = pl.ds(PAD + r, CHUNK)
                centre, total, drift = [], [], []
                fields = [a_ref[j - 1, comp, r : r + CHUNK, :] for comp in range(3)]
                for part in range(2):
                    mid = source[j, part, here, :]
                    xp = source[j, part, pl.ds(PAD + r + 1, CHUNK), :]
                    xm = source[j, part, pl.ds(PAD + r - 1, CHUNK), :]
                    zp = source[j + 1, part, here, :]
                    zm = source[j - 1, part, here, :]
                    yp, ym = lane_shifts(mid)
                    centre.append(mid)
                    total.append((xp + xm) + (yp + ym) + (zp + zm))
                    drift.append(fields[0] * (xp - xm) + fields[1] * (yp - ym) + fields[2] * (zp - zm))
                weight = w_ref[j - 1, r : r + CHUNK, :]
                real_h = weight * centre[0] - total[0] + drift[1]
                imag_h = weight * centre[1] - total[1] - drift[0]
                new = (factor * imag_h, -factor * real_h)
                if order < TERMS:
                    for part in range(2):
                        target[j, part, here, :] = new[part]
                if order == 1:

                    @pl.when((own >= 0) & (own < DEPTH + 2))
                    def _():
                        for part in range(2):
                            out_ref[own, part, here, :] = centre[part] + new[part]
                elif order < TERMS:

                    @pl.when((own >= 0) & (own < DEPTH + 2))
                    def _():
                        for part in range(2):
                            out_ref[own, part, here, :] += new[part]
                else:
                    for part in range(2):
                        moved = out_ref[own, part, here, :] + new[part]
                        out_ref[own, part, here, :] = moved
                        squares = squares + (moved * moved).reshape(CHUNK // 8, 8, NY).sum(0)
            if order == TERMS:

                @pl.when((own >= 1) & (own < DEPTH + 1))
                def _():
                    norm_ref[...] += squares

        source, target = target, source


def propagate(scale, wide, hcore, hchip, weight, vcore, vchip, field, acore, achip):
    return call(
        propagate_body,
        [(DEPTH + 2, 2, XP, NY), (8, NY)],
        [vmem()] * 10,
        [
            pltpu.VMEM((WIDE, 2, XP, NY), F32),
            pltpu.VMEM((WIDE, 2, XP, NY), F32),
            pltpu.VMEM((DEPTH + 2 * MARGIN, NX, NY), F32),
            pltpu.VMEM((DEPTH + 2 * MARGIN, 3, NX, NY), F32),
        ],
        flops=60000000,
    )(scale, wide, hcore, hchip, weight, vcore, vchip, field, acore, achip)


def current_body(wide_ref, field_ref, flow_ref):
    low = half_rows((CHUNK // 8, 8, NY))

    @pl.loop(0, DEPTH // 2)
    def _(pair):
        for r in range(0, NX, CHUNK):
            both = []
            for z in range(2):
                j = 2 * pair + z + 1
                here = pl.ds(PAD + r, CHUNK)
                mids, grads = [], []
                for part in range(2):
                    mid = wide_ref[j, part, here, :]
                    yp, ym = lane_shifts(mid)
                    mids.append(mid)
                    grads.append(
                        (
                            wide_ref[j, part, pl.ds(PAD + r + 1, CHUNK), :]
                            - wide_ref[j, part, pl.ds(PAD + r - 1, CHUNK), :],
                            yp - ym,
                            wide_ref[j + 1, part, here, :] - wide_ref[j - 1, part, here, :],
                        )
                    )
                u, w = mids
                density = u * u + w * w
                both.append(
                    [
                        0.5 * (u * grads[1][comp] - w * grads[0][comp])
                        + field_ref[j - 1, comp, r : r + CHUNK, :] * density
                        for comp in range(3)
                    ]
                )
            tiles = pl.ds(r // 8, CHUNK // 8)
            for comp in range(3):
                even = both[0][comp].reshape(CHUNK // 8, 8, NY)
                odd = both[1][comp].reshape(CHUNK // 8, 8, NY)
                rows = pl.ds(pl.multiple_of((comp * DEPTH + 2 * pair) * ROWS, 8), 8)
                flow_ref[tiles, 0, rows, :] = jnp.where(low, even, pltpu.roll(odd, 4, 1))
                flow_ref[tiles, 1, rows, :] = jnp.where(low, pltpu.roll(even, 4, 1), odd)


def current(wide, field):
    return call(current_body, [(ORBS // 2, 2, PACK, NY)], [vmem(), vmem()], flops=10000000)(wide, field)[0]


def weigh_body(occ_ref, n0_ref, n1_ref, n2_ref, n3_ref, flow_ref, out_ref, scale_ref):
    sums = (n0_ref[...] + n1_ref[...]) + (n2_ref[...] + n3_ref[...])
    norm = jnp.sum(jnp.sum(sums, axis=1, keepdims=True), axis=0, keepdims=True)
    mean = norm * (1.0 / CELLS) + EPSILON
    scale = 1.0 / jnp.sqrt(mean)
    scale_ref[...] = jnp.broadcast_to(scale, (8, NY))
    weight = jnp.broadcast_to(scale * scale * (occ_ref[0] * (1.0 / ORBS)), (1, NY))

    @pl.loop(0, ORBS // 2)
    def _(i):
        for side in range(2):
            out_ref[i, side] = flow_ref[i, side] * weight


def weigh(occupation, norms, flow):
    return call(
        weigh_body, [(ORBS // 2, 2, PACK, NY), (8, NY)], [smem()] + [vmem()] * 5, flops=500000
    )(occupation, *norms, flow)


def curl_body(field_ref, acore_ref, achip_ref, out_ref):
    core = core_index()
    owner = lax.axis_index("orb")
    tile = owner // 2
    odd = lax.rem(owner, 2)
    row = lax.broadcasted_iota(jnp.int32, (8, NY), 0)
    keep = ((owner > 0) | (row != 0)) & ((owner < ORBS - 1) | (row != ROWS + 1))
    starts = [pl.multiple_of(8 * jnp.clip(tile + k, 0, NX // 8 - 1), 8) for k in (-1, 0, 1)]

    def window(load):
        before, middle, after = [load(pl.ds(s, 8)) for s in starts]
        first = jnp.where(odd == 1, middle, before)
        second = jnp.where(odd == 1, after, middle)
        shift_first = jnp.where(odd == 1, pltpu.roll(first, 5, 0), pltpu.roll(first, 1, 0))
        shift_second = jnp.where(odd == 1, pltpu.roll(second, 5, 0), pltpu.roll(second, 1, 0))
        split = jnp.where(odd == 1, 5, 1)
        return jnp.where(keep, jnp.where(row < split, shift_first, shift_second), 0.0)

    def x_plus(v):
        return pltpu.roll(v, 7, 0)

    def x_minus(v):
        return pltpu.roll(v, 1, 0)

    planes = []
    for z in range(-1, DEPTH + 1):
        comps = []
        for comp in range(3):
            if z < 0:
                value = jnp.where(
                    core == 1,
                    window(lambda r: acore_ref[MARGIN - 1, comp, r, :]),
                    window(lambda r: achip_ref[MARGIN - 1, comp, r, :]),
                )
            elif z < DEPTH:
                value = window(lambda r: field_ref[z, comp, r, :])
            else:
                value = jnp.where(
                    core == 0,
                    window(lambda r: acore_ref[0, comp, r, :]),
                    window(lambda r: achip_ref[0, comp, r, :]),
                )
            comps.append(value)
        planes.append(comps)
    for z in range(DEPTH):
        ax, ay, az = planes[z + 1]
        axm, aym, azm = planes[z]
        axp, ayp, azp = planes[z + 2]
        ax_up, ax_dn = lane_shifts(ax)
        ay_dn = lane_shifts(ay)[1]
        az_up, az_dn = lane_shifts(az)
        dy_ay = ay - ay_dn
        dx_ax = ax - x_minus(ax)
        inner_x = dy_ay + (az - azm)
        inner_y = dx_ax + (az - azm)
        inner_z = dx_ax + dy_ay
        up_inner_z = (axp - x_minus(axp)) + (ayp - lane_shifts(ayp)[1])
        out_x = (x_plus(inner_x) - inner_x) - (ax_up + ax_dn + axp + axm - 4.0 * ax)
        out_y = (lane_shifts(inner_y)[0] - inner_y) - (x_plus(ay) + x_minus(ay) + ayp + aym - 4.0 * ay)
        out_z = (up_inner_z - inner_z) - (x_plus(az) + x_minus(az) + az_up + az_dn - 4.0 * az)
        for comp, value in enumerate((out_x, out_y, out_z)):
            out_ref[pl.ds((comp * DEPTH + z) * ROWS, ROWS), :] = pltpu.roll(value, 7, 0)[0:ROWS]


def double_curl(field, acore, achip):
    return call(curl_body, [(PACK, NY)], [vmem()] * 3, flops=1000000)(field, acore, achip)[0]


def update_body(last, got_ref, curl_ref, e_ref, a_ref, *outs):
    total = got_ref[0]
    for i in range(1, ORBS):
        total = total + got_ref[i]
    e_new = e_ref[...] + WAVE_STEP * (curl_ref[...] - total)
    a_new = a_ref[...] - WAVE_STEP * e_new
    if last:
        for ref, value in zip(outs, (e_new, a_new)):
            for comp in range(3):
                for z in range(DEPTH):
                    start = (comp * DEPTH + z) * ROWS
                    ref[comp, pl.ds(z, ROWS, stride=DEPTH), :] = value[start : start + ROWS]
    else:
        copies_ref, a_out_ref, e_out_ref = outs
        a_out_ref[...] = a_new
        e_out_ref[...] = e_new
        for i in range(ORBS):
            copies_ref[i] = a_new


def update(last, got, curl, e_rows, a_rows):
    if last:
        outs = [(3, ROWS * DEPTH, NY)] * 2
    else:
        outs = [(ORBS, PACK, NY), (PACK, NY), (PACK, NY)]
    return call(functools.partial(update_body, last), outs, [vmem()] * 4, flops=500000)(got, curl, e_rows, a_rows)


def finish_body(scale_ref, wide_ref, out_ref):
    scale = scale_ref[0:1, :]
    for z in range(DEPTH):
        for part in range(2):
            out_ref[part, pl.ds(z, NX, stride=DEPTH), :] = wide_ref[z + 1, part, PAD : PAD + NX, :] * scale


def finish(scale, wide):
    return call(finish_body, [(2, NX * DEPTH, NY)], [vmem()] * 2)(scale, wide)[0]


def everyone(copies):
    return lax.all_to_all(copies, "orb", 0, 0, tiled=True)


def per_device(orbitals, potential, occupation, e_field, a_field):
    copies, a_rows, e_rows = spread(a_field, e_field)
    got = everyone(copies)
    wide, weight, core_send, chip_send = prepare(orbitals, potential)
    hcore = lax.ppermute(core_send, "slab", CORE_PAIRS)
    hchip = lax.ppermute(chip_send, "slab", CHIP_PAIRS)
    vcore, vchip = hcore[2 * HALO :], hchip[2 * HALO :]
    scale = jnp.ones((8, NY), F32)
    for step in range(STEPS):
        last = step == STEPS - 1
        field, acore_send, achip_send = assemble(got)
        acore = lax.ppermute(acore_send, "slab", CORE_PAIRS)
        achip = lax.ppermute(achip_send, "slab", CHIP_PAIRS)
        wide, norm = propagate(scale, wide, hcore, hchip, weight, vcore, vchip, field, acore, achip)
        norms = [norm] + [lax.ppermute(norm, "slab", [(i, i ^ k) for i in range(SLABS)]) for k in (1, 2, 3)]
        flow = current(wide, field)
        flow, scale = weigh(occupation, norms, flow)
        flows = everyone(flow.reshape(ORBS, PACK, NY))
        curl = double_curl(field, acore, achip)
        if not last:
            core_send, chip_send = rims(wide)
            hcore = lax.ppermute(core_send, "slab", CORE_PAIRS)
            hchip = lax.ppermute(chip_send, "slab", CHIP_PAIRS)
            copies, a_rows, e_rows = update(last, flows, curl, e_rows, a_rows)
            got = everyone(copies)
        else:
            e_new, a_new = update(last, flows, curl, e_rows, a_rows)
            orbitals = finish(scale, wide)
    return (
        orbitals.reshape(1, 2, NX, DEPTH, NY),
        e_new.reshape(3, ROWS, DEPTH, NY),
        a_new.reshape(3, ROWS, DEPTH, NY),
    )


def solution(mesh):
    return jax.shard_map(
        per_device,
        mesh=mesh,
        in_specs=(
            P("orb", None, None, "slab", None),
            P(None, "slab", None),
            P("orb"),
            P(None, "orb", "slab", None),
            P(None, "orb", "slab", None),
        ),
        out_specs=(
            P("orb", None, None, "slab", None),
            P(None, "orb", "slab", None),
            P(None, "orb", "slab", None),
        ),
        check_vma=False,
    )
```

```python
import functools

import jax
import jax.numpy as jnp
from jax import lax
from jax.experimental import pallas as pl
from jax.experimental.pallas import tpu as pltpu
from jax.sharding import PartitionSpec as P

TERMS = 4
STEPS = 2
TIME_STEP = 0.3
WAVE_STEP = 0.5
EPSILON = 1e-06

NX = 128
NY = 128
NZ = 32
ORBS = 32
SLABS = 4
CELLS = NX * NY * NZ
DEPTH = NZ // SLABS
ROWS = NX // ORBS
HALO = TERMS + 1
MARGIN = TERMS
WIDE = DEPTH + 2 * HALO
PAD = 8
XP = NX + 2 * PAD
PACK = 3 * DEPTH * ROWS
CHUNK = 16
F32 = jnp.float32

CORE_PAIRS = [(0, 1), (1, 0), (2, 3), (3, 2)]
CHIP_PAIRS = [(1, 2), (2, 1)]


def vmem():
    return pl.BlockSpec(memory_space=pltpu.VMEM)


def smem():
    return pl.BlockSpec(memory_space=pltpu.SMEM)


def call(name, body, outs, ins, scratch=(), flops=1000000, limit=8):
    shapes = [jax.ShapeDtypeStruct(s, F32) for s in outs]
    size = sum(4 * s.size for s in shapes)
    return pl.pallas_call(
        body,
        name=name,
        out_shape=shapes,
        in_specs=ins,
        out_specs=[vmem()] * len(outs),
        scratch_shapes=list(scratch),
        compiler_params=pltpu.CompilerParams(vmem_limit_bytes=limit * 1024 * 1024),
        cost_estimate=pl.CostEstimate(flops=flops, bytes_accessed=2 * size, transcendentals=0),
    )


def core_index():
    return lax.rem(lax.axis_index("slab"), 2)


def lane_shifts(value):
    lane = lax.broadcasted_iota(jnp.int32, value.shape, value.ndim - 1)
    plus = jnp.where(lane == NY - 1, 0.0, pltpu.roll(value, NY - 1, value.ndim - 1))
    minus = jnp.where(lane == 0, 0.0, pltpu.roll(value, 1, value.ndim - 1))
    return plus, minus


def half_rows(shape):
    return lax.broadcasted_iota(jnp.int32, shape, len(shape) - 2) % 8 < 4


def to_rows(ref, rows_ref):
    for comp in range(3):
        for z in range(DEPTH):
            rows_ref[pl.ds((comp * DEPTH + z) * ROWS, ROWS), :] = ref[comp, pl.ds(z, ROWS, stride=DEPTH), :]


def prepare_body(orb_ref, pot_ref, e_ref, wide_ref, weight_ref, core_ref, chip_ref, e_rows_ref):
    core = core_index()
    to_rows(e_ref, e_rows_ref)
    for z in range(DEPTH):
        for part in range(2):
            wide_ref[z + 1, part, PAD : PAD + NX, :] = orb_ref[part, pl.ds(z, NX, stride=DEPTH), :]
        weight_ref[z] = 2.0 * pot_ref[pl.ds(z, NX, stride=DEPTH), :] + 6.0
    to_core = 1 + (1 - core) * (DEPTH - HALO)
    to_chip = 1 + core * (DEPTH - HALO)
    for i in range(HALO):
        for part in range(2):
            core_ref[2 * i + part] = wide_ref[to_core + i, part, PAD : PAD + NX, :]
            chip_ref[2 * i + part] = wide_ref[to_chip + i, part, PAD : PAD + NX, :]
    for i in range(MARGIN):
        core_ref[2 * HALO + i] = weight_ref[(1 - core) * (DEPTH - MARGIN) + i]
        chip_ref[2 * HALO + i] = weight_ref[core * (DEPTH - MARGIN) + i]


def prepare(orbitals, potential, e_field):
    planes = 2 * HALO + MARGIN
    return call(
        "prepare",
        prepare_body,
        [(DEPTH + 2, 2, XP, NY), (DEPTH, NX, NY), (planes, NX, NY), (planes, NX, NY), (PACK, NY)],
        [vmem()] * 3,
        limit=12,
    )(
        orbitals.reshape(2, NX * DEPTH, NY),
        potential.reshape(NX * DEPTH, NY),
        e_field.reshape(3, ROWS * DEPTH, NY),
    )


def rims_body(wide_ref, core_ref, chip_ref):
    core = core_index()
    to_core = 1 + (1 - core) * (DEPTH - HALO)
    to_chip = 1 + core * (DEPTH - HALO)
    for i in range(HALO):
        for part in range(2):
            core_ref[2 * i + part] = wide_ref[to_core + i, part, PAD : PAD + NX, :]
            chip_ref[2 * i + part] = wide_ref[to_chip + i, part, PAD : PAD + NX, :]


def rims(wide):
    return call("rims", rims_body, [(2 * HALO, NX, NY)] * 2, [vmem()])(wide)


def spread_body(a_ref, copies_ref, a_rows_ref):
    to_rows(a_ref, a_rows_ref)
    value = a_rows_ref[...]
    for i in range(ORBS):
        copies_ref[i] = value


def spread(a_field):
    return call("spread", spread_body, [(ORBS, PACK, NY), (PACK, NY)], [vmem()])(
        a_field.reshape(3, ROWS * DEPTH, NY)
    )


def assemble_body(got_ref, field_ref, core_ref, chip_ref):
    core = core_index()
    low = half_rows((ORBS // 2, 8, NY))
    for comp in range(3):
        for pair in range(DEPTH // 2):
            rows = pl.ds((comp * DEPTH + 2 * pair) * ROWS, 8)
            first = got_ref[:, 0, rows, :]
            second = got_ref[:, 1, rows, :]
            even = jnp.where(low, first, pltpu.roll(second, 4, 1))
            odd = jnp.where(low, pltpu.roll(first, 4, 1), second)
            field_ref[2 * pair, comp] = even.reshape(NX, NY)
            field_ref[2 * pair + 1, comp] = odd.reshape(NX, NY)
    for i in range(MARGIN):
        for comp in range(3):
            core_ref[i, comp] = field_ref[(1 - core) * (DEPTH - MARGIN) + i, comp]
            chip_ref[i, comp] = field_ref[core * (DEPTH - MARGIN) + i, comp]


def assemble(got):
    return call(
        "assemble",
        assemble_body,
        [(DEPTH, 3, NX, NY), (MARGIN, 3, NX, NY), (MARGIN, 3, NX, NY)],
        [vmem()],
    )(got.reshape(ORBS // 2, 2, PACK, NY))


def propagate_body(
    scale_ref, wide_ref, hcore_ref, hchip_ref, weight_ref, vcore_ref, vchip_ref, field_ref, acore_ref, achip_ref,
    out_ref, norm_ref, base_ref, ping_ref, pong_ref, w_ref, a_ref,
):
    core = core_index()
    scale = scale_ref[0:1, :]
    edge = jnp.zeros((PAD, NY), F32)

    def clear(ref, count):
        @pl.loop(0, count)
        def _(j):
            for part in range(2):
                ref[j, part, 0:PAD, :] = edge
                ref[j, part, PAD + NX : XP, :] = edge

    clear(base_ref, WIDE)
    clear(ping_ref, WIDE)
    clear(pong_ref, WIDE)
    clear(out_ref, DEPTH + 2)

    def put_field(j, plane, base):
        total = base
        for comp in range(3):
            value = plane[comp]
            a_ref[j, comp] = value
            total = total + value * value
        w_ref[j] = total

    @pl.loop(0, DEPTH)
    def _(z):
        for part in range(2):
            base_ref[z + HALO, part, PAD : PAD + NX, :] = wide_ref[z + 1, part, PAD : PAD + NX, :] * scale
        put_field(z + MARGIN, field_ref[z], weight_ref[z])

    def put_halo(above, orb_ref, pot_ref, fld_ref):
        @pl.loop(0, HALO)
        def _(i):
            for part in range(2):
                base_ref[above * (DEPTH + HALO) + i, part, PAD : PAD + NX, :] = orb_ref[2 * i + part] * scale

        @pl.loop(0, MARGIN)
        def _(i):
            put_field(above * (DEPTH + MARGIN) + i, fld_ref[i], pot_ref[2 * HALO + i])

    @pl.when(core == 1)
    def _():
        put_halo(0, hcore_ref, vcore_ref, acore_ref)
        put_halo(1, hchip_ref, vchip_ref, achip_ref)

    @pl.when(core == 0)
    def _():
        put_halo(1, hcore_ref, vcore_ref, acore_ref)
        put_halo(0, hchip_ref, vchip_ref, achip_ref)

    first = lax.axis_index("slab") * DEPTH - HALO

    def plane(j, order, source, target, shift):
        depth = first + j
        inside = jnp.where((depth >= 0) & (depth < NZ), 1.0, 0.0).astype(F32)
        factor = inside * (0.5 * TIME_STEP / order)
        squares = jnp.zeros((8, NY), F32)
        for r in range(0, NX, CHUNK):
            here = pl.ds(PAD + r, CHUNK)
            centre, total, drift = [], [], []
            fields = [a_ref[j - 1, comp, r : r + CHUNK, :] for comp in range(3)]
            for part in range(2):
                mid = source[j, part, here, :]
                xp = source[j, part, pl.ds(PAD + r + 1, CHUNK), :]
                xm = source[j, part, pl.ds(PAD + r - 1, CHUNK), :]
                zp = source[j + 1, part, here, :]
                zm = source[j - 1, part, here, :]
                yp, ym = lane_shifts(mid)
                centre.append(mid)
                total.append((xp + xm) + (yp + ym) + (zp + zm))
                drift.append(fields[0] * (xp - xm) + fields[1] * (yp - ym) + fields[2] * (zp - zm))
            weight = w_ref[j - 1, r : r + CHUNK, :]
            real_h = weight * centre[0] - total[0] + drift[1]
            imag_h = weight * centre[1] - total[1] - drift[0]
            for part, change in enumerate((factor * imag_h, -factor * real_h)):
                value = base_ref[j, part, here, :] + change
                target[j + shift, part, here, :] = value
                if order == 1 and HALO <= j < HALO + DEPTH:
                    squares = squares + (value * value).reshape(CHUNK // 8, 8, NY).sum(0)
        return squares

    squares = jnp.zeros((8, NY), F32)
    source = base_ref
    for done, order in enumerate(range(TERMS, 0, -1)):
        target = out_ref if order == 1 else (ping_ref, pong_ref)[done % 2]
        for j in range(done + 1, WIDE - done - 1):
            squares = squares + plane(j, order, source, target, 1 - HALO if order == 1 else 0)
        source = target
    norm_ref[...] = squares


def propagate(scale, wide, hcore, hchip, weight, vcore, vchip, field, acore, achip):
    return call(
        "propagate",
        propagate_body,
        [(DEPTH + 2, 2, XP, NY), (8, NY)],
        [vmem()] * 10,
        [
            pltpu.VMEM((WIDE, 2, XP, NY), F32),
            pltpu.VMEM((WIDE, 2, XP, NY), F32),
            pltpu.VMEM((WIDE, 2, XP, NY), F32),
            pltpu.VMEM((DEPTH + 2 * MARGIN, NX, NY), F32),
            pltpu.VMEM((DEPTH + 2 * MARGIN, 3, NX, NY), F32),
        ],
        flops=60000000,
        limit=28,
    )(scale, wide, hcore, hchip, weight, vcore, vchip, field, acore, achip)


def current_body(wide_ref, field_ref, flow_ref):
    low = half_rows((CHUNK // 8, 8, NY))

    @pl.loop(0, DEPTH // 2)
    def _(pair):
        for r in range(0, NX, CHUNK):
            both = []
            for z in range(2):
                j = 2 * pair + z + 1
                here = pl.ds(PAD + r, CHUNK)
                mids, grads = [], []
                for part in range(2):
                    mid = wide_ref[j, part, here, :]
                    yp, ym = lane_shifts(mid)
                    mids.append(mid)
                    grads.append(
                        (
                            wide_ref[j, part, pl.ds(PAD + r + 1, CHUNK), :]
                            - wide_ref[j, part, pl.ds(PAD + r - 1, CHUNK), :],
                            yp - ym,
                            wide_ref[j + 1, part, here, :] - wide_ref[j - 1, part, here, :],
                        )
                    )
                u, w = mids
                density = u * u + w * w
                both.append(
                    [
                        0.5 * (u * grads[1][comp] - w * grads[0][comp])
                        + field_ref[j - 1, comp, r : r + CHUNK, :] * density
                        for comp in range(3)
                    ]
                )
            tiles = pl.ds(r // 8, CHUNK // 8)
            for comp in range(3):
                even = both[0][comp].reshape(CHUNK // 8, 8, NY)
                odd = both[1][comp].reshape(CHUNK // 8, 8, NY)
                rows = pl.ds(pl.multiple_of((comp * DEPTH + 2 * pair) * ROWS, 8), 8)
                flow_ref[tiles, 0, rows, :] = jnp.where(low, even, pltpu.roll(odd, 4, 1))
                flow_ref[tiles, 1, rows, :] = jnp.where(low, pltpu.roll(even, 4, 1), odd)


def current(wide, field):
    return call("current", current_body, [(ORBS // 2, 2, PACK, NY)], [vmem(), vmem()], flops=10000000, limit=10)(wide, field)[0]


def weigh_body(occ_ref, n0_ref, n1_ref, n2_ref, n3_ref, flow_ref, out_ref, scale_ref):
    sums = (n0_ref[...] + n1_ref[...]) + (n2_ref[...] + n3_ref[...])
    norm = jnp.sum(jnp.sum(sums, axis=1, keepdims=True), axis=0, keepdims=True)
    mean = norm * (1.0 / CELLS) + EPSILON
    scale = 1.0 / jnp.sqrt(mean)
    scale_ref[...] = jnp.broadcast_to(scale, (8, NY))
    weight = jnp.broadcast_to(scale * scale * (occ_ref[0] * (1.0 / ORBS)), (1, NY))

    @pl.loop(0, ORBS // 2)
    def _(i):
        for side in range(2):
            out_ref[i, side] = flow_ref[i, side] * weight


def weigh(occupation, norms, flow):
    return call(
        "weigh", weigh_body, [(ORBS // 2, 2, PACK, NY), (8, NY)], [smem()] + [vmem()] * 5, flops=500000
    )(occupation, *norms, flow)


def curl_body(field_ref, acore_ref, achip_ref, out_ref):
    core = core_index()
    owner = lax.axis_index("orb")
    tile = owner // 2
    odd = lax.rem(owner, 2)
    row = lax.broadcasted_iota(jnp.int32, (8, NY), 0)
    keep = ((owner > 0) | (row != 0)) & ((owner < ORBS - 1) | (row != ROWS + 1))
    starts = [pl.multiple_of(8 * jnp.clip(tile + k, 0, NX // 8 - 1), 8) for k in (-1, 0, 1)]

    def window(load):
        before, middle, after = [load(pl.ds(s, 8)) for s in starts]
        first = jnp.where(odd == 1, middle, before)
        second = jnp.where(odd == 1, after, middle)
        shift_first = jnp.where(odd == 1, pltpu.roll(first, 5, 0), pltpu.roll(first, 1, 0))
        shift_second = jnp.where(odd == 1, pltpu.roll(second, 5, 0), pltpu.roll(second, 1, 0))
        split = jnp.where(odd == 1, 5, 1)
        return jnp.where(keep, jnp.where(row < split, shift_first, shift_second), 0.0)

    def x_plus(v):
        return pltpu.roll(v, 7, 0)

    def x_minus(v):
        return pltpu.roll(v, 1, 0)

    planes = []
    for z in range(-1, DEPTH + 1):
        comps = []
        for comp in range(3):
            if z < 0:
                value = jnp.where(
                    core == 1,
                    window(lambda r: acore_ref[MARGIN - 1, comp, r, :]),
                    window(lambda r: achip_ref[MARGIN - 1, comp, r, :]),
                )
            elif z < DEPTH:
                value = window(lambda r: field_ref[z, comp, r, :])
            else:
                value = jnp.where(
                    core == 0,
                    window(lambda r: acore_ref[0, comp, r, :]),
                    window(lambda r: achip_ref[0, comp, r, :]),
                )
            comps.append(value)
        planes.append(comps)
    for z in range(DEPTH):
        ax, ay, az = planes[z + 1]
        axm, aym, azm = planes[z]
        axp, ayp, azp = planes[z + 2]
        ax_up, ax_dn = lane_shifts(ax)
        ay_dn = lane_shifts(ay)[1]
        az_up, az_dn = lane_shifts(az)
        dy_ay = ay - ay_dn
        dx_ax = ax - x_minus(ax)
        inner_x = dy_ay + (az - azm)
        inner_y = dx_ax + (az - azm)
        inner_z = dx_ax + dy_ay
        up_inner_z = (axp - x_minus(axp)) + (ayp - lane_shifts(ayp)[1])
        out_x = (x_plus(inner_x) - inner_x) - (ax_up + ax_dn + axp + axm - 4.0 * ax)
        out_y = (lane_shifts(inner_y)[0] - inner_y) - (x_plus(ay) + x_minus(ay) + ayp + aym - 4.0 * ay)
        out_z = (up_inner_z - inner_z) - (x_plus(az) + x_minus(az) + az_up + az_dn - 4.0 * az)
        for comp, value in enumerate((out_x, out_y, out_z)):
            out_ref[pl.ds((comp * DEPTH + z) * ROWS, ROWS), :] = pltpu.roll(value, 7, 0)[0:ROWS]


def double_curl(field, acore, achip):
    return call("double_curl", curl_body, [(PACK, NY)], [vmem()] * 3, flops=1000000)(field, acore, achip)[0]


def update_body(last, got_ref, curl_ref, e_ref, a_ref, *outs):
    total = got_ref[0]
    for i in range(1, ORBS):
        total = total + got_ref[i]
    e_new = e_ref[...] + WAVE_STEP * (curl_ref[...] - total)
    a_new = a_ref[...] - WAVE_STEP * e_new
    if last:
        for ref, value in zip(outs, (e_new, a_new)):
            for comp in range(3):
                for z in range(DEPTH):
                    start = (comp * DEPTH + z) * ROWS
                    ref[comp, pl.ds(z, ROWS, stride=DEPTH), :] = value[start : start + ROWS]
    else:
        copies_ref, a_out_ref, e_out_ref = outs
        a_out_ref[...] = a_new
        e_out_ref[...] = e_new
        for i in range(ORBS):
            copies_ref[i] = a_new


def update(last, got, curl, e_rows, a_rows):
    if last:
        outs = [(3, ROWS * DEPTH, NY)] * 2
    else:
        outs = [(ORBS, PACK, NY), (PACK, NY), (PACK, NY)]
    return call("update", functools.partial(update_body, last), outs, [vmem()] * 4, flops=500000)(got, curl, e_rows, a_rows)


def finish_body(scale_ref, wide_ref, out_ref):
    scale = scale_ref[0:1, :]
    for z in range(DEPTH):
        for part in range(2):
            out_ref[part, pl.ds(z, NX, stride=DEPTH), :] = wide_ref[z + 1, part, PAD : PAD + NX, :] * scale


def finish(scale, wide):
    return call("finish", finish_body, [(2, NX * DEPTH, NY)], [vmem()] * 2)(scale, wide)[0]


def everyone(copies):
    return lax.all_to_all(copies, "orb", 0, 0, tiled=True)


def per_device(orbitals, potential, occupation, e_field, a_field):
    copies, a_rows = spread(a_field)
    got = everyone(copies)
    wide, weight, core_send, chip_send, e_rows = prepare(orbitals, potential, e_field)
    hcore = lax.ppermute(core_send, "slab", CORE_PAIRS)
    hchip = lax.ppermute(chip_send, "slab", CHIP_PAIRS)
    vcore, vchip = hcore, hchip
    scale = jnp.ones((8, NY), F32)
    for step in range(STEPS):
        last = step == STEPS - 1
        field, acore_send, achip_send = assemble(got)
        acore = lax.ppermute(acore_send, "slab", CORE_PAIRS)
        achip = lax.ppermute(achip_send, "slab", CHIP_PAIRS)
        wide, norm = propagate(scale, wide, hcore, hchip, weight, vcore, vchip, field, acore, achip)
        norms = [norm] + [lax.ppermute(norm, "slab", [(i, i ^ k) for i in range(SLABS)]) for k in (1, 2, 3)]
        flow = current(wide, field)
        flow, scale = weigh(occupation, norms, flow)
        flows = everyone(flow.reshape(ORBS, PACK, NY))
        curl = double_curl(field, acore, achip)
        if not last:
            core_send, chip_send = rims(wide)
            hcore = lax.ppermute(core_send, "slab", CORE_PAIRS)
            hchip = lax.ppermute(chip_send, "slab", CHIP_PAIRS)
            flows, hcore, hchip = lax.optimization_barrier((flows, hcore, hchip))
            copies, a_rows, e_rows = update(last, flows, curl, e_rows, a_rows)
            got = everyone(copies)
        else:
            e_new, a_new = update(last, flows, curl, e_rows, a_rows)
            orbitals = finish(scale, wide)
    return (
        orbitals.reshape(1, 2, NX, DEPTH, NY),
        e_new.reshape(3, ROWS, DEPTH, NY),
        a_new.reshape(3, ROWS, DEPTH, NY),
    )


def solution(mesh):
    return jax.shard_map(
        per_device,
        mesh=mesh,
        in_specs=(
            P("orb", None, None, "slab", None),
            P(None, "slab", None),
            P("orb"),
            P(None, "orb", "slab", None),
            P(None, "orb", "slab", None),
        ),
        out_specs=(
            P("orb", None, None, "slab", None),
            P(None, "orb", "slab", None),
            P(None, "orb", "slab", None),
        ),
        check_vma=False,
    )
```

```python
import functools

import jax
import jax.numpy as jnp
from jax import lax
from jax.experimental import pallas as pl
from jax.experimental.pallas import tpu as pltpu
from jax.sharding import PartitionSpec as P

TERMS = 4
STEPS = 2
TIME_STEP = 0.3
WAVE_STEP = 0.5
EPSILON = 1e-06

NX = 128
NY = 128
NZ = 32
ORBS = 32
SLABS = 4
CELLS = NX * NY * NZ
DEPTH = NZ // SLABS
ROWS = NX // ORBS
HALO = TERMS + 1
MARGIN = TERMS
WIDE = DEPTH + 2 * HALO
PAD = 8
PACK = 3 * DEPTH * ROWS
CHUNK = 8
F32 = jnp.float32

HALF = NX // 2
LOCAL = HALF + 8
XL = LOCAL + 2 * PAD
GROUP = ORBS // 2
TILES = LOCAL // 8
ALL = ("orb", "slab")
MEETING = (1, 2)


def pairs(flip, move):
    found = []
    for orb in range(ORBS):
        for slab in range(SLABS):
            to = move(slab)
            if to is not None:
                found.append((orb * SLABS + slab, (orb ^ flip) * SLABS + to))
    return found


def over_core(slab):
    return slab ^ 1


def over_chip(slab):
    return 3 - slab if slab in MEETING else None


HALVES = pairs(GROUP, lambda slab: slab)
CORE = pairs(0, over_core)
CHIP = pairs(0, over_chip)
CORE_ACROSS = pairs(GROUP, over_core)
CHIP_ACROSS = pairs(GROUP, over_chip)
CHIP_SUM = pairs(0, lambda slab: slab ^ 2)
BOTH_SUM = pairs(GROUP, lambda slab: slab ^ 2)
GROUPS = [list(range(GROUP)), list(range(GROUP, ORBS))]


def send(value, table):
    return lax.ppermute(value, ALL, table)


def vmem():
    return pl.BlockSpec(memory_space=pltpu.VMEM)


def smem():
    return pl.BlockSpec(memory_space=pltpu.SMEM)


def call(name, body, outs, ins, scratch=(), flops=1000000, limit=8):
    shapes = [jax.ShapeDtypeStruct(s, F32) for s in outs]
    size = sum(4 * s.size for s in shapes)
    return pl.pallas_call(
        body,
        name=name,
        out_shape=shapes,
        in_specs=ins,
        out_specs=[vmem()] * len(outs),
        scratch_shapes=list(scratch),
        compiler_params=pltpu.CompilerParams(vmem_limit_bytes=limit * 1024 * 1024),
        cost_estimate=pl.CostEstimate(flops=flops, bytes_accessed=2 * size, transcendentals=0),
    )


def core_index():
    return lax.rem(lax.axis_index("slab"), 2)


def half_index():
    return lax.axis_index("orb") // GROUP


def split_rows(value, half):
    low, high = value[0:LOCAL], value[NX - LOCAL : NX]
    return jnp.where(half == 0, low, high), jnp.where(half == 0, high, low)


def own_rows(value, half):
    return jnp.where(half == 0, value[0:HALF], value[8 : 8 + HALF])


def lane_shifts(value):
    lane = lax.broadcasted_iota(jnp.int32, value.shape, value.ndim - 1)
    plus = jnp.where(lane == NY - 1, 0.0, pltpu.roll(value, NY - 1, value.ndim - 1))
    minus = jnp.where(lane == 0, 0.0, pltpu.roll(value, 1, value.ndim - 1))
    return plus, minus


def half_rows(shape):
    return lax.broadcasted_iota(jnp.int32, shape, len(shape) - 2) % 8 < 4


def to_rows(ref, rows_ref):
    for comp in range(3):
        for z in range(DEPTH):
            rows_ref[pl.ds((comp * DEPTH + z) * ROWS, ROWS), :] = ref[comp, pl.ds(z, ROWS, stride=DEPTH), :]


def prepare_body(
    orb_ref, pot_ref, e_ref, own_ref, swap_ref, weight_ref, core_ref, chip_ref, corex_ref, chipx_ref, e_rows_ref
):
    core, half = core_index(), half_index()
    to_rows(e_ref, e_rows_ref)
    for z in range(DEPTH):
        for part in range(2):
            own_ref[z, part], swap_ref[z, part] = split_rows(orb_ref[part, pl.ds(z, NX, stride=DEPTH), :], half)
        weight_ref[z] = split_rows(2.0 * pot_ref[pl.ds(z, NX, stride=DEPTH), :] + 6.0, half)[0]
    to_core = (1 - core) * (DEPTH - HALO)
    to_chip = core * (DEPTH - HALO)
    for i in range(HALO):
        for part in range(2):
            core_ref[2 * i + part] = own_ref[to_core + i, part]
            chip_ref[2 * i + part] = own_ref[to_chip + i, part]
            corex_ref[2 * i + part] = swap_ref[to_core + i, part]
            chipx_ref[2 * i + part] = swap_ref[to_chip + i, part]
    for i in range(MARGIN):
        core_ref[2 * HALO + i] = weight_ref[(1 - core) * (DEPTH - MARGIN) + i]
        chip_ref[2 * HALO + i] = weight_ref[core * (DEPTH - MARGIN) + i]


def prepare(orbitals, potential, e_field):
    planes = 2 * HALO + MARGIN
    return call(
        "prepare",
        prepare_body,
        [(DEPTH, 2, LOCAL, NY)] * 2
        + [(DEPTH, LOCAL, NY)]
        + [(planes, LOCAL, NY)] * 2
        + [(2 * HALO, LOCAL, NY)] * 2
        + [(PACK, NY)],
        [vmem()] * 3,
        limit=12,
    )(
        orbitals.reshape(2, NX * DEPTH, NY),
        potential.reshape(NX * DEPTH, NY),
        e_field.reshape(3, ROWS * DEPTH, NY),
    )


def edges_body(wide_ref, out_ref):
    half = half_index()
    for z in range(DEPTH):
        for k in range(4):
            low = wide_ref[z + 1, k, PAD + HALF - 8 : PAD + HALF, :]
            out_ref[z, k] = jnp.where(half == 0, low, wide_ref[z + 1, k, PAD + 8 : PAD + 16, :])


def edges(wide):
    return call("edges", edges_body, [(DEPTH, 4, 8, NY)], [vmem()])(wide)[0]


def rims_body(wide_ref, edge_ref, own_ref, other_ref, core_ref, chip_ref, corex_ref, chipx_ref):
    core, half = core_index(), half_index()
    for z in range(DEPTH):
        for slot, ref in enumerate((own_ref, other_ref)):
            for part in range(2):
                value = wide_ref[z + 1, 2 * slot + part, PAD : PAD + LOCAL, :]
                edge = edge_ref[z, 2 * (1 - slot) + part]
                ref[z, part, 0:8, :] = jnp.where(half == 0, value[0:8], edge)
                ref[z, part, 8:HALF, :] = value[8:HALF]
                ref[z, part, HALF:LOCAL, :] = jnp.where(half == 0, edge, value[HALF:LOCAL])
    to_core = (1 - core) * (DEPTH - HALO)
    to_chip = core * (DEPTH - HALO)
    for i in range(HALO):
        for part in range(2):
            core_ref[2 * i + part] = own_ref[to_core + i, part]
            chip_ref[2 * i + part] = own_ref[to_chip + i, part]
            corex_ref[2 * i + part] = other_ref[to_core + i, part]
            chipx_ref[2 * i + part] = other_ref[to_chip + i, part]


def rims(wide, edge):
    return call(
        "rims", rims_body, [(DEPTH, 2, LOCAL, NY)] * 2 + [(2 * HALO, LOCAL, NY)] * 4, [vmem()] * 2, limit=12
    )(wide, edge)


def spread_body(a_ref, copies_ref, a_rows_ref):
    to_rows(a_ref, a_rows_ref)
    value = a_rows_ref[...]
    for i in range(GROUP):
        copies_ref[i] = value


def spread(a_field):
    return call("spread", spread_body, [(GROUP, PACK, NY), (PACK, NY)], [vmem()])(
        a_field.reshape(3, ROWS * DEPTH, NY)
    )


def assemble_body(got_ref, field_ref, edge_ref, core_ref, chip_ref, corex_ref, chipx_ref):
    core, half = core_index(), half_index()
    low = half_rows((GROUP // 2, 8, NY))
    for comp in range(3):
        for pair in range(DEPTH // 2):
            rows = pl.ds((comp * DEPTH + 2 * pair) * ROWS, 8)
            first = got_ref[:, 0, rows, :]
            second = got_ref[:, 1, rows, :]
            even = jnp.where(low, first, pltpu.roll(second, 4, 1))
            odd = jnp.where(low, pltpu.roll(first, 4, 1), second)
            for z, value in ((2 * pair, even), (2 * pair + 1, odd)):
                field_ref[z, comp] = value.reshape(HALF, NY)
                edge_ref[z, comp] = jnp.where(half == 0, value[GROUP // 2 - 1], value[0])
    for i in range(MARGIN):
        to_core = (1 - core) * (DEPTH - MARGIN) + i
        to_chip = core * (DEPTH - MARGIN) + i
        for comp in range(3):
            core_ref[i, comp] = field_ref[to_core, comp]
            chip_ref[i, comp] = field_ref[to_chip, comp]
            corex_ref[i, comp] = edge_ref[to_core, comp]
            chipx_ref[i, comp] = edge_ref[to_chip, comp]


def assemble(got):
    return call(
        "assemble",
        assemble_body,
        [(DEPTH, 3, HALF, NY), (DEPTH, 3, 8, NY)]
        + [(MARGIN, 3, HALF, NY)] * 2
        + [(MARGIN, 3, 8, NY)] * 2,
        [vmem()],
    )(got.reshape(GROUP // 2, 2, PACK, NY))


def propagate_body(
    own_ref, other_ref, hcore_ref, hchip_ref, hcorex_ref, hchipx_ref, weight_ref, vcore_ref, vchip_ref,
    field_ref, edge_ref, acore_ref, achip_ref, acorex_ref, achipx_ref,
    out_ref, norm_ref, a_ref, base_ref, ping_ref, pong_ref, w_ref,
):
    core, half = core_index(), half_index()
    zeros = jnp.zeros((PAD, NY), F32)

    def clear(ref, count):
        @pl.loop(0, count)
        def _(j):
            for k in range(4):
                ref[j, k, 0:PAD, :] = zeros
                ref[j, k, PAD + LOCAL : XL, :] = zeros

    clear(base_ref, WIDE)
    clear(ping_ref, WIDE)
    clear(pong_ref, WIDE)
    clear(out_ref, DEPTH + 2)

    def put_field(j, fld_ref, edg_ref, i, base):
        total = base
        for comp in range(3):
            value, edge = fld_ref[i, comp], edg_ref[i, comp]
            joined = jnp.where(
                half == 0, jnp.concatenate([value, edge], axis=0), jnp.concatenate([edge, value], axis=0)
            )
            a_ref[j, comp] = joined
            total = total + joined * joined
        w_ref[j] = total

    @pl.loop(0, DEPTH)
    def _(z):
        for part in range(2):
            base_ref[z + HALO, part, PAD : PAD + LOCAL, :] = own_ref[z, part]
            base_ref[z + HALO, 2 + part, PAD : PAD + LOCAL, :] = other_ref[z, part]
        put_field(z + MARGIN, field_ref, edge_ref, z, weight_ref[z])

    def put_halo(above, orb_ref, orbx_ref, pot_ref, fld_ref, edg_ref):
        @pl.loop(0, HALO)
        def _(i):
            j = above * (DEPTH + HALO) + i
            for part in range(2):
                base_ref[j, part, PAD : PAD + LOCAL, :] = orb_ref[2 * i + part]
                base_ref[j, 2 + part, PAD : PAD + LOCAL, :] = orbx_ref[2 * i + part]

        @pl.loop(0, MARGIN)
        def _(i):
            put_field(above * (DEPTH + MARGIN) + i, fld_ref, edg_ref, i, pot_ref[2 * HALO + i])

    @pl.when(core == 1)
    def _():
        put_halo(0, hcore_ref, hcorex_ref, vcore_ref, acore_ref, acorex_ref)
        put_halo(1, hchip_ref, hchipx_ref, vchip_ref, achip_ref, achipx_ref)

    @pl.when(core == 0)
    def _():
        put_halo(1, hcore_ref, hcorex_ref, vcore_ref, acore_ref, acorex_ref)
        put_halo(0, hchip_ref, hchipx_ref, vchip_ref, achip_ref, achipx_ref)

    first = lax.axis_index("slab") * DEPTH - HALO
    sums = [jnp.zeros((8, NY), F32), jnp.zeros((8, NY), F32)]

    def plane(j, order, source, target, shift):
        depth = first + j
        inside = jnp.where((depth >= 0) & (depth < NZ), 1.0, 0.0).astype(F32)
        factor = inside * (0.5 * TIME_STEP / order)
        for r in range(0, LOCAL, CHUNK):
            here = pl.ds(PAD + r, CHUNK)
            fields = [a_ref[j - 1, comp, r : r + CHUNK, :] for comp in range(3)]
            weight = w_ref[j - 1, r : r + CHUNK, :]
            for slot in range(2):
                centre, total, drift = [], [], []
                for k in (2 * slot, 2 * slot + 1):
                    mid = source[j, k, here, :]
                    xp = source[j, k, pl.ds(PAD + r + 1, CHUNK), :]
                    xm = source[j, k, pl.ds(PAD + r - 1, CHUNK), :]
                    zp = source[j + 1, k, here, :]
                    zm = source[j - 1, k, here, :]
                    yp, ym = lane_shifts(mid)
                    centre.append(mid)
                    total.append((xp + xm) + (yp + ym) + (zp + zm))
                    drift.append(fields[0] * (xp - xm) + fields[1] * (yp - ym) + fields[2] * (zp - zm))
                real_h = weight * centre[0] - total[0] + drift[1]
                imag_h = weight * centre[1] - total[1] - drift[0]
                for part, change in enumerate((factor * imag_h, -factor * real_h)):
                    value = base_ref[j, 2 * slot + part, here, :] + change
                    target[j + shift, 2 * slot + part, here, :] = value
                    if order == 1 and HALO <= j < HALO + DEPTH:
                        square = value * value
                        if r == 0:
                            square = jnp.where(half == 0, square, 0.0)
                        if r == LOCAL - 8:
                            square = jnp.where(half == 1, square, 0.0)
                        sums[slot] = sums[slot] + square

    source = base_ref
    for done, order in enumerate(range(TERMS, 0, -1)):
        target = out_ref if order == 1 else (ping_ref, pong_ref)[done % 2]
        for j in range(done + 1, WIDE - done - 1):
            plane(j, order, source, target, 1 - HALO if order == 1 else 0)
        source = target
    norm_ref[0] = sums[0]
    norm_ref[1] = sums[1]


def propagate(orbs, weight, vcore, vchip, fields):
    return call(
        "propagate",
        propagate_body,
        [(DEPTH + 2, 4, XL, NY), (2, 8, NY), (DEPTH + 2 * MARGIN, 3, LOCAL, NY)],
        [vmem()] * 15,
        [
            pltpu.VMEM((WIDE, 4, XL, NY), F32),
            pltpu.VMEM((WIDE, 4, XL, NY), F32),
            pltpu.VMEM((WIDE, 4, XL, NY), F32),
            pltpu.VMEM((DEPTH + 2 * MARGIN, LOCAL, NY), F32),
        ],
        flops=60000000,
        limit=32,
    )(*orbs, weight, vcore, vchip, *fields)


def current_body(wide_ref, field_ref, flow_ref):
    low = half_rows((8, NY))

    @pl.loop(0, DEPTH // 2)
    def _(pair):
        for tile in range(TILES):
            r = 8 * tile
            here = pl.ds(PAD + r, 8)
            for slot in range(2):
                both = []
                for z in range(2):
                    j = 2 * pair + z + 1
                    mids, grads = [], []
                    for k in (2 * slot, 2 * slot + 1):
                        mid = wide_ref[j, k, here, :]
                        yp, ym = lane_shifts(mid)
                        mids.append(mid)
                        grads.append(
                            (
                                wide_ref[j, k, pl.ds(PAD + r + 1, 8), :] - wide_ref[j, k, pl.ds(PAD + r - 1, 8), :],
                                yp - ym,
                                wide_ref[j + 1, k, here, :] - wide_ref[j - 1, k, here, :],
                            )
                        )
                    u, w = mids
                    density = u * u + w * w
                    both.append(
                        [
                            0.5 * (u * grads[1][comp] - w * grads[0][comp])
                            + field_ref[j + MARGIN - 1, comp, r : r + 8, :] * density
                            for comp in range(3)
                        ]
                    )
                for comp in range(3):
                    even, odd = both[0][comp], both[1][comp]
                    rows = pl.ds(pl.multiple_of((comp * DEPTH + 2 * pair) * ROWS, 8), 8)
                    flow_ref[slot, tile, 0, rows, :] = jnp.where(low, even, pltpu.roll(odd, 4, 0))
                    flow_ref[slot, tile, 1, rows, :] = jnp.where(low, pltpu.roll(even, 4, 0), odd)


def current(wide, field):
    return call("current", current_body, [(2, TILES, 2, PACK, NY)], [vmem(), vmem()], flops=10000000, limit=10)(
        wide, field
    )[0]


def weigh_body(occ_ref, occx_ref, prior_ref, n_ref, nchip_ref, nhalf_ref, nboth_ref, flow_ref, out_ref, scale_ref):
    half = half_index()
    weights = []
    for slot, occ in enumerate((occ_ref, occx_ref)):
        sums = (n_ref[slot] + nchip_ref[slot]) + (nhalf_ref[1 - slot] + nboth_ref[1 - slot])
        norm = jnp.sum(jnp.sum(sums, axis=1, keepdims=True), axis=0, keepdims=True)
        prior = prior_ref[slot, 0:1, :]
        mean = prior * prior * (norm * (1.0 / CELLS)) + EPSILON
        scale = prior / jnp.sqrt(mean)
        scale_ref[slot] = jnp.broadcast_to(scale, (8, NY))
        weights.append(scale * scale * (occ[0] * (1.0 / ORBS)))

    @pl.loop(0, GROUP // 2)
    def _(i):
        for side in range(2):
            out_ref[i, side] = flow_ref[0, i + half, side] * weights[0] + flow_ref[1, i + half, side] * weights[1]


def weigh(occupations, prior, norms, flow):
    return call(
        "weigh", weigh_body, [(GROUP // 2, 2, PACK, NY), (2, 8, NY)], [smem()] * 2 + [vmem()] * 6, flops=500000
    )(*occupations, prior, *norms, flow)


def curl_body(field_ref, out_ref):
    owner = lax.axis_index("orb")
    place = lax.rem(owner, GROUP)
    tile = place // 2 + half_index()
    odd = lax.rem(place, 2)
    row = lax.broadcasted_iota(jnp.int32, (8, NY), 0)
    keep = ((owner > 0) | (row != 0)) & ((owner < ORBS - 1) | (row != ROWS + 1))
    starts = [pl.multiple_of(8 * jnp.clip(tile + k, 0, TILES - 1), 8) for k in (-1, 0, 1)]

    def window(z, comp):
        before, middle, after = [field_ref[z + MARGIN, comp, pl.ds(s, 8), :] for s in starts]
        first = jnp.where(odd == 1, middle, before)
        second = jnp.where(odd == 1, after, middle)
        shift_first = jnp.where(odd == 1, pltpu.roll(first, 5, 0), pltpu.roll(first, 1, 0))
        shift_second = jnp.where(odd == 1, pltpu.roll(second, 5, 0), pltpu.roll(second, 1, 0))
        split = jnp.where(odd == 1, 5, 1)
        return jnp.where(keep, jnp.where(row < split, shift_first, shift_second), 0.0)

    def x_plus(v):
        return pltpu.roll(v, 7, 0)

    def x_minus(v):
        return pltpu.roll(v, 1, 0)

    planes = [[window(z, comp) for comp in range(3)] for z in range(-1, DEPTH + 1)]
    for z in range(DEPTH):
        ax, ay, az = planes[z + 1]
        axm, aym, azm = planes[z]
        axp, ayp, azp = planes[z + 2]
        ax_up, ax_dn = lane_shifts(ax)
        ay_dn = lane_shifts(ay)[1]
        az_up, az_dn = lane_shifts(az)
        dy_ay = ay - ay_dn
        dx_ax = ax - x_minus(ax)
        inner_x = dy_ay + (az - azm)
        inner_y = dx_ax + (az - azm)
        inner_z = dx_ax + dy_ay
        up_inner_z = (axp - x_minus(axp)) + (ayp - lane_shifts(ayp)[1])
        out_x = (x_plus(inner_x) - inner_x) - (ax_up + ax_dn + axp + axm - 4.0 * ax)
        out_y = (lane_shifts(inner_y)[0] - inner_y) - (x_plus(ay) + x_minus(ay) + ayp + aym - 4.0 * ay)
        out_z = (up_inner_z - inner_z) - (x_plus(az) + x_minus(az) + az_up + az_dn - 4.0 * az)
        for comp, value in enumerate((out_x, out_y, out_z)):
            out_ref[pl.ds((comp * DEPTH + z) * ROWS, ROWS), :] = pltpu.roll(value, 7, 0)[0:ROWS]


def double_curl(field):
    return call("double_curl", curl_body, [(PACK, NY)], [vmem()], flops=1000000)(field)[0]


def update_body(last, got_ref, curl_ref, e_ref, a_ref, *outs):
    total = got_ref[0]
    for i in range(1, GROUP):
        total = total + got_ref[i]
    e_new = e_ref[...] + WAVE_STEP * (curl_ref[...] - total)
    a_new = a_ref[...] - WAVE_STEP * e_new
    if last:
        for ref, value in zip(outs, (e_new, a_new)):
            for comp in range(3):
                for z in range(DEPTH):
                    start = (comp * DEPTH + z) * ROWS
                    ref[comp, pl.ds(z, ROWS, stride=DEPTH), :] = value[start : start + ROWS]
    else:
        copies_ref, a_out_ref, e_out_ref = outs
        a_out_ref[...] = a_new
        e_out_ref[...] = e_new
        for i in range(GROUP):
            copies_ref[i] = a_new


def update(last, got, curl, e_rows, a_rows):
    if last:
        outs = [(3, ROWS * DEPTH, NY)] * 2
    else:
        outs = [(GROUP, PACK, NY), (PACK, NY), (PACK, NY)]
    return call("update", functools.partial(update_body, last), outs, [vmem()] * 4, flops=500000)(got, curl, e_rows, a_rows)


def hand_back_body(wide_ref, out_ref):
    half = half_index()
    for z in range(DEPTH):
        for part in range(2):
            out_ref[z, part] = own_rows(wide_ref[z + 1, 2 + part, PAD : PAD + LOCAL, :], half)


def hand_back(wide):
    return call("hand_back", hand_back_body, [(DEPTH, 2, HALF, NY)], [vmem()])(wide)[0]


def finish_body(scale_ref, wide_ref, theirs_ref, out_ref):
    half = half_index()
    scale = scale_ref[0, 0:1, :]
    for z in range(DEPTH):
        for part in range(2):
            mine = own_rows(wide_ref[z + 1, part, PAD : PAD + LOCAL, :], half) * scale
            theirs = theirs_ref[z, part] * scale
            out_ref[part, pl.ds(z, HALF, stride=DEPTH), :] = jnp.where(half == 0, mine, theirs)
            out_ref[part, pl.ds(HALF * DEPTH + z, HALF, stride=DEPTH), :] = jnp.where(half == 0, theirs, mine)


def finish(scale, wide, theirs):
    return call("finish", finish_body, [(2, NX * DEPTH, NY)], [vmem()] * 3)(scale, wide, theirs)[0]


def everyone(copies):
    return lax.all_to_all(copies, "orb", 0, 0, tiled=True, axis_index_groups=GROUPS)


def per_device(orbitals, potential, occupation, e_field, a_field):
    copies, a_rows = spread(a_field)
    got = everyone(copies)
    own, swap, weight, core, chip, corex, chipx, e_rows = prepare(orbitals, potential, e_field)
    other = send(swap, HALVES)
    vcore, vchip = send(core, CORE), send(chip, CHIP)
    orbs = (own, other, vcore, vchip, send(corex, CORE_ACROSS), send(chipx, CHIP_ACROSS))
    occupations = (occupation, send(occupation, HALVES))
    scale = jnp.ones((2, 8, NY), F32)
    for step in range(STEPS):
        last = step == STEPS - 1
        field, edge, acore, achip, acorex, achipx = assemble(got)
        fields = (
            field,
            send(edge, HALVES),
            send(acore, CORE),
            send(achip, CHIP),
            send(acorex, CORE_ACROSS),
            send(achipx, CHIP_ACROSS),
        )
        wide, norm, field = propagate(orbs, weight, vcore, vchip, fields)
        norm = norm + send(norm, CORE)
        norms = (norm, send(norm, CHIP_SUM), send(norm, HALVES), send(norm, BOTH_SUM))
        flow = current(wide, field)
        flow, scale = weigh(occupations, scale, norms, flow)
        flows = everyone(flow.reshape(GROUP, PACK, NY))
        curl = double_curl(field)
        if not last:
            edge = send(edges(wide), HALVES)
            own, other, core, chip, corex, chipx = rims(wide, edge)
            flows, core, chip, corex, chipx = lax.optimization_barrier((flows, core, chip, corex, chipx))
            orbs = (
                own,
                other,
                send(core, CORE),
                send(chip, CHIP),
                send(corex, CORE),
                send(chipx, CHIP),
            )
            copies, a_rows, e_rows = update(last, flows, curl, e_rows, a_rows)
            got = everyone(copies)
            got, orbs = lax.optimization_barrier((got, orbs))
        else:
            theirs = send(hand_back(wide), HALVES)
            e_new, a_new = update(last, flows, curl, e_rows, a_rows)
            orbitals = finish(scale, wide, theirs)
    return (
        orbitals.reshape(1, 2, NX, DEPTH, NY),
        e_new.reshape(3, ROWS, DEPTH, NY),
        a_new.reshape(3, ROWS, DEPTH, NY),
    )


def solution(mesh):
    return jax.shard_map(
        per_device,
        mesh=mesh,
        in_specs=(
            P("orb", None, None, "slab", None),
            P(None, "slab", None),
            P("orb"),
            P(None, "orb", "slab", None),
            P(None, "orb", "slab", None),
        ),
        out_specs=(
            P("orb", None, None, "slab", None),
            P(None, "orb", "slab", None),
            P(None, "orb", "slab", None),
        ),
        check_vma=False,
    )
```

```python
import functools

import jax
import jax.numpy as jnp
from jax import lax
from jax.experimental import pallas as pl
from jax.experimental.pallas import tpu as pltpu
from jax.sharding import PartitionSpec as P

TERMS = 4
STEPS = 2
TIME_STEP = 0.3
WAVE_STEP = 0.5
EPSILON = 1e-06

NX = 128
NY = 128
NZ = 32
ORBS = 32
SLABS = 4
CELLS = NX * NY * NZ
DEPTH = NZ // SLABS
ROWS = NX // ORBS
HALO = TERMS + 1
MARGIN = TERMS
WIDE = DEPTH + 2 * HALO
PAD = 8
PACK = 3 * DEPTH * ROWS
CHUNK = 8
F32 = jnp.float32

HALF = NX // 2
LOCAL = HALF + 8
XL = LOCAL + 2 * PAD
GROUP = ORBS // 2
TILES = LOCAL // 8
ALL = ("orb", "slab")
MEETING = (1, 2)


def pairs(flip, move):
    found = []
    for orb in range(ORBS):
        for slab in range(SLABS):
            to = move(slab)
            if to is not None:
                found.append((orb * SLABS + slab, (orb ^ flip) * SLABS + to))
    return found


def over_core(slab):
    return slab ^ 1


def over_chip(slab):
    return 3 - slab if slab in MEETING else None


HALVES = pairs(GROUP, lambda slab: slab)
CORE = pairs(0, over_core)
CHIP = pairs(0, over_chip)
CORE_ACROSS = pairs(GROUP, over_core)
CHIP_ACROSS = pairs(GROUP, over_chip)
CHIP_SUM = pairs(0, lambda slab: slab ^ 2)
BOTH_SUM = pairs(GROUP, lambda slab: slab ^ 2)
GROUPS = [list(range(GROUP)), list(range(GROUP, ORBS))]


def send(value, table):
    return lax.ppermute(value, ALL, table)


def vmem():
    return pl.BlockSpec(memory_space=pltpu.VMEM)


def smem():
    return pl.BlockSpec(memory_space=pltpu.SMEM)


def call(name, body, outs, ins, scratch=(), flops=1000000, limit=8):
    shapes = [jax.ShapeDtypeStruct(s, F32) for s in outs]
    size = sum(4 * s.size for s in shapes)
    return pl.pallas_call(
        body,
        name=name,
        out_shape=shapes,
        in_specs=ins,
        out_specs=[vmem()] * len(outs),
        scratch_shapes=list(scratch),
        compiler_params=pltpu.CompilerParams(vmem_limit_bytes=limit * 1024 * 1024),
        cost_estimate=pl.CostEstimate(flops=flops, bytes_accessed=2 * size, transcendentals=0),
    )


def core_index():
    return lax.rem(lax.axis_index("slab"), 2)


def half_index():
    return lax.axis_index("orb") // GROUP


def split_rows(value, half):
    low, high = value[0:LOCAL], value[NX - LOCAL : NX]
    return jnp.where(half == 0, low, high), jnp.where(half == 0, high, low)


def own_rows(value, half):
    return jnp.where(half == 0, value[0:HALF], value[8 : 8 + HALF])


def lane_shifts(value):
    lane = lax.broadcasted_iota(jnp.int32, value.shape, value.ndim - 1)
    plus = jnp.where(lane == NY - 1, 0.0, pltpu.roll(value, NY - 1, value.ndim - 1))
    minus = jnp.where(lane == 0, 0.0, pltpu.roll(value, 1, value.ndim - 1))
    return plus, minus


def half_rows(shape):
    return lax.broadcasted_iota(jnp.int32, shape, len(shape) - 2) % 8 < 4


def to_rows(ref, rows_ref):
    for comp in range(3):
        for z in range(DEPTH):
            rows_ref[pl.ds((comp * DEPTH + z) * ROWS, ROWS), :] = ref[comp, pl.ds(z, ROWS, stride=DEPTH), :]


def prepare_body(
    orb_ref, pot_ref, e_ref, own_ref, swap_ref, weight_ref, core_ref, chip_ref, corex_ref, chipx_ref, e_rows_ref
):
    core, half = core_index(), half_index()
    to_rows(e_ref, e_rows_ref)
    for z in range(DEPTH):
        for part in range(2):
            own_ref[z, part], swap_ref[z, part] = split_rows(orb_ref[part, pl.ds(z, NX, stride=DEPTH), :], half)
        weight_ref[z] = split_rows(2.0 * pot_ref[pl.ds(z, NX, stride=DEPTH), :] + 6.0, half)[0]
    to_core = (1 - core) * (DEPTH - HALO)
    to_chip = core * (DEPTH - HALO)
    for i in range(HALO):
        for part in range(2):
            core_ref[2 * i + part] = own_ref[to_core + i, part]
            chip_ref[2 * i + part] = own_ref[to_chip + i, part]
            corex_ref[2 * i + part] = swap_ref[to_core + i, part]
            chipx_ref[2 * i + part] = swap_ref[to_chip + i, part]
    for i in range(MARGIN):
        core_ref[2 * HALO + i] = weight_ref[(1 - core) * (DEPTH - MARGIN) + i]
        chip_ref[2 * HALO + i] = weight_ref[core * (DEPTH - MARGIN) + i]


def prepare(orbitals, potential, e_field):
    planes = 2 * HALO + MARGIN
    return call(
        "prepare",
        prepare_body,
        [(DEPTH, 2, LOCAL, NY)] * 2
        + [(DEPTH, LOCAL, NY)]
        + [(planes, LOCAL, NY)] * 2
        + [(2 * HALO, LOCAL, NY)] * 2
        + [(PACK, NY)],
        [vmem()] * 3,
        limit=12,
    )(
        orbitals.reshape(2, NX * DEPTH, NY),
        potential.reshape(NX * DEPTH, NY),
        e_field.reshape(3, ROWS * DEPTH, NY),
    )


def edges_body(wide_ref, out_ref):
    half = half_index()
    for z in range(DEPTH):
        for k in range(4):
            low = wide_ref[z + 1, k, PAD + HALF - 8 : PAD + HALF, :]
            out_ref[z, k] = jnp.where(half == 0, low, wide_ref[z + 1, k, PAD + 8 : PAD + 16, :])


def edges(wide):
    return call("edges", edges_body, [(DEPTH, 4, 8, NY)], [vmem()])(wide)[0]


def rims_body(wide_ref, edge_ref, own_ref, other_ref, core_ref, chip_ref):
    core, half = core_index(), half_index()
    for z in range(DEPTH):
        for slot, ref in enumerate((own_ref, other_ref)):
            for part in range(2):
                value = wide_ref[z + 1, 2 * slot + part, PAD : PAD + LOCAL, :]
                edge = edge_ref[z, 2 * (1 - slot) + part]
                ref[z, part, 0:8, :] = jnp.where(half == 0, value[0:8], edge)
                ref[z, part, 8:HALF, :] = value[8:HALF]
                ref[z, part, HALF:LOCAL, :] = jnp.where(half == 0, edge, value[HALF:LOCAL])
    to_core = (1 - core) * (DEPTH - HALO)
    to_chip = core * (DEPTH - HALO)
    for i in range(HALO):
        for slot, ref in enumerate((own_ref, other_ref)):
            for part in range(2):
                core_ref[2 * (HALO * slot + i) + part] = ref[to_core + i, part]
                chip_ref[2 * (HALO * slot + i) + part] = ref[to_chip + i, part]


def rims(wide, edge):
    return call(
        "rims", rims_body, [(DEPTH, 2, LOCAL, NY)] * 2 + [(4 * HALO, LOCAL, NY)] * 2, [vmem()] * 2, limit=12
    )(wide, edge)


def spread_body(a_ref, copies_ref, a_rows_ref):
    to_rows(a_ref, a_rows_ref)
    value = a_rows_ref[...]
    for i in range(GROUP):
        copies_ref[i] = value


def spread(a_field):
    return call("spread", spread_body, [(GROUP, PACK, NY), (PACK, NY)], [vmem()])(
        a_field.reshape(3, ROWS * DEPTH, NY)
    )


def assemble_body(got_ref, field_ref, edge_ref, core_ref, chip_ref, corex_ref, chipx_ref):
    core, half = core_index(), half_index()
    low = half_rows((GROUP // 2, 8, NY))
    for comp in range(3):
        for pair in range(DEPTH // 2):
            rows = pl.ds((comp * DEPTH + 2 * pair) * ROWS, 8)
            first = got_ref[:, 0, rows, :]
            second = got_ref[:, 1, rows, :]
            even = jnp.where(low, first, pltpu.roll(second, 4, 1))
            odd = jnp.where(low, pltpu.roll(first, 4, 1), second)
            for z, value in ((2 * pair, even), (2 * pair + 1, odd)):
                field_ref[z, comp] = value.reshape(HALF, NY)
                edge_ref[z, comp] = jnp.where(half == 0, value[GROUP // 2 - 1], value[0])
    for i in range(MARGIN):
        to_core = (1 - core) * (DEPTH - MARGIN) + i
        to_chip = core * (DEPTH - MARGIN) + i
        for comp in range(3):
            core_ref[i, comp] = field_ref[to_core, comp]
            chip_ref[i, comp] = field_ref[to_chip, comp]
            corex_ref[i, comp] = edge_ref[to_core, comp]
            chipx_ref[i, comp] = edge_ref[to_chip, comp]


def assemble(got):
    return call(
        "assemble",
        assemble_body,
        [(DEPTH, 3, HALF, NY), (DEPTH, 3, 8, NY)]
        + [(MARGIN, 3, HALF, NY)] * 2
        + [(MARGIN, 3, 8, NY)] * 2,
        [vmem()],
    )(got.reshape(GROUP // 2, 2, PACK, NY))


def clear(ref, count):
    zeros = jnp.zeros((PAD, NY), F32)

    @pl.loop(0, count)
    def _(j):
        for k in range(4):
            ref[j, k, 0:PAD, :] = zeros
            ref[j, k, PAD + LOCAL : XL, :] = zeros


def stage_body(
    first, own_ref, other_ref, hcore_ref, hchip_ref, hcorex_ref, hchipx_ref, weight_ref, vcore_ref, vchip_ref,
    base_ref, v_ref,
):
    core = core_index()
    clear(base_ref, WIDE)

    @pl.loop(0, DEPTH)
    def _(z):
        for part in range(2):
            base_ref[z + HALO, part, PAD : PAD + LOCAL, :] = own_ref[z, part]
            base_ref[z + HALO, 2 + part, PAD : PAD + LOCAL, :] = other_ref[z, part]
        v_ref[z + MARGIN] = weight_ref[z]

    def put_halo(above, orb_ref, orbx_ref, pot_ref):
        @pl.loop(0, HALO)
        def _(i):
            j = above * (DEPTH + HALO) + i
            for part in range(2):
                base_ref[j, part, PAD : PAD + LOCAL, :] = orb_ref[2 * i + part]
                base_ref[j, 2 + part, PAD : PAD + LOCAL, :] = orbx_ref[first + 2 * i + part]

        @pl.loop(0, MARGIN)
        def _(i):
            v_ref[above * (DEPTH + MARGIN) + i] = pot_ref[2 * HALO + i]

    @pl.when(core == 1)
    def _():
        put_halo(0, hcore_ref, hcorex_ref, vcore_ref)
        put_halo(1, hchip_ref, hchipx_ref, vchip_ref)

    @pl.when(core == 0)
    def _():
        put_halo(1, hcore_ref, hcorex_ref, vcore_ref)
        put_halo(0, hchip_ref, hchipx_ref, vchip_ref)


def stage(first, orbs, weight, vcore, vchip):
    return call(
        "stage",
        functools.partial(stage_body, first),
        [(WIDE, 4, XL, NY), (DEPTH + 2 * MARGIN, LOCAL, NY)],
        [vmem()] * 9,
        flops=1000000,
        limit=16,
    )(*orbs, weight, vcore, vchip)


def propagate_body(
    occ_ref, base_ref, v_ref, field_ref, edge_ref, acore_ref, achip_ref, acorex_ref, achipx_ref,
    out_ref, norm_ref, a_ref, ping_ref, pong_ref, w_ref,
):
    core, half = core_index(), half_index()
    clear(ping_ref, WIDE)
    clear(pong_ref, WIDE)
    clear(out_ref, DEPTH + 2)

    def put_field(j, fld_ref, edg_ref, i):
        total = v_ref[j]
        for comp in range(3):
            value, edge = fld_ref[i, comp], edg_ref[i, comp]
            joined = jnp.where(
                half == 0, jnp.concatenate([value, edge], axis=0), jnp.concatenate([edge, value], axis=0)
            )
            a_ref[j, comp] = joined
            total = total + joined * joined
        w_ref[j] = total

    @pl.loop(0, DEPTH)
    def _(z):
        put_field(z + MARGIN, field_ref, edge_ref, z)

    def put_halo(above, fld_ref, edg_ref):
        @pl.loop(0, MARGIN)
        def _(i):
            put_field(above * (DEPTH + MARGIN) + i, fld_ref, edg_ref, i)

    @pl.when(core == 1)
    def _():
        put_halo(0, acore_ref, acorex_ref)
        put_halo(1, achip_ref, achipx_ref)

    @pl.when(core == 0)
    def _():
        put_halo(1, acore_ref, acorex_ref)
        put_halo(0, achip_ref, achipx_ref)

    first = lax.axis_index("slab") * DEPTH - HALO
    sums = [jnp.zeros((8, NY), F32), jnp.zeros((8, NY), F32)]

    def plane(j, order, source, target, shift):
        depth = first + j
        inside = jnp.where((depth >= 0) & (depth < NZ), 1.0, 0.0).astype(F32)
        factor = inside * (0.5 * TIME_STEP / order)
        for r in range(0, LOCAL, CHUNK):
            here = pl.ds(PAD + r, CHUNK)
            fields = [a_ref[j - 1, comp, r : r + CHUNK, :] for comp in range(3)]
            weight = w_ref[j - 1, r : r + CHUNK, :]
            for slot in range(2):
                centre, total, drift = [], [], []
                for k in (2 * slot, 2 * slot + 1):
                    mid = source[j, k, here, :]
                    xp = source[j, k, pl.ds(PAD + r + 1, CHUNK), :]
                    xm = source[j, k, pl.ds(PAD + r - 1, CHUNK), :]
                    zp = source[j + 1, k, here, :]
                    zm = source[j - 1, k, here, :]
                    yp, ym = lane_shifts(mid)
                    centre.append(mid)
                    total.append((xp + xm) + (yp + ym) + (zp + zm))
                    drift.append(fields[0] * (xp - xm) + fields[1] * (yp - ym) + fields[2] * (zp - zm))
                real_h = weight * centre[0] - total[0] + drift[1]
                imag_h = weight * centre[1] - total[1] - drift[0]
                for part, change in enumerate((factor * imag_h, -factor * real_h)):
                    value = base_ref[j, 2 * slot + part, here, :] + change
                    target[j + shift, 2 * slot + part, here, :] = value
                    if order == 1 and HALO <= j < HALO + DEPTH:
                        square = value * value
                        if r == 0:
                            square = jnp.where(half == 0, square, 0.0)
                        if r == LOCAL - 8:
                            square = jnp.where(half == 1, square, 0.0)
                        sums[slot] = sums[slot] + square

    source = base_ref
    for done, order in enumerate(range(TERMS, 0, -1)):
        target = out_ref if order == 1 else (ping_ref, pong_ref)[done % 2]
        for j in range(done + 1, WIDE - done - 1):
            plane(j, order, source, target, 1 - HALO if order == 1 else 0)
        source = target
    norm_ref[0] = sums[0]
    norm_ref[1] = sums[1]
    norm_ref[2] = jnp.broadcast_to(occ_ref[0], (8, NY))


def propagate(occupation, base, v, fields):
    return call(
        "propagate",
        propagate_body,
        [(DEPTH + 2, 4, XL, NY), (3, 8, NY), (DEPTH + 2 * MARGIN, 3, LOCAL, NY)],
        [smem()] + [vmem()] * 8,
        [
            pltpu.VMEM((WIDE, 4, XL, NY), F32),
            pltpu.VMEM((WIDE, 4, XL, NY), F32),
            pltpu.VMEM((DEPTH + 2 * MARGIN, LOCAL, NY), F32),
        ],
        flops=60000000,
        limit=26,
    )(occupation, base, v, *fields)


def current_body(wide_ref, field_ref, flow_ref):
    low = half_rows((8, NY))

    @pl.loop(0, DEPTH // 2)
    def _(pair):
        for tile in range(TILES):
            r = 8 * tile
            here = pl.ds(PAD + r, 8)
            for slot in range(2):
                both = []
                for z in range(2):
                    j = 2 * pair + z + 1
                    mids, grads = [], []
                    for k in (2 * slot, 2 * slot + 1):
                        mid = wide_ref[j, k, here, :]
                        yp, ym = lane_shifts(mid)
                        mids.append(mid)
                        grads.append(
                            (
                                wide_ref[j, k, pl.ds(PAD + r + 1, 8), :] - wide_ref[j, k, pl.ds(PAD + r - 1, 8), :],
                                yp - ym,
                                wide_ref[j + 1, k, here, :] - wide_ref[j - 1, k, here, :],
                            )
                        )
                    u, w = mids
                    density = u * u + w * w
                    both.append(
                        [
                            0.5 * (u * grads[1][comp] - w * grads[0][comp])
                            + field_ref[j + MARGIN - 1, comp, r : r + 8, :] * density
                            for comp in range(3)
                        ]
                    )
                for comp in range(3):
                    even, odd = both[0][comp], both[1][comp]
                    rows = pl.ds(pl.multiple_of((comp * DEPTH + 2 * pair) * ROWS, 8), 8)
                    flow_ref[slot, tile, 0, rows, :] = jnp.where(low, even, pltpu.roll(odd, 4, 0))
                    flow_ref[slot, tile, 1, rows, :] = jnp.where(low, pltpu.roll(even, 4, 0), odd)


def current(wide, field):
    return call("current", current_body, [(2, TILES, 2, PACK, NY)], [vmem(), vmem()], flops=10000000, limit=10)(
        wide, field
    )[0]


def weigh_body(prior_ref, n_ref, nchip_ref, nhalf_ref, nboth_ref, flow_ref, out_ref, scale_ref):
    half = half_index()
    weights = []
    for slot, occ_ref in enumerate((n_ref, nhalf_ref)):
        sums = (n_ref[slot] + nchip_ref[slot]) + (nhalf_ref[1 - slot] + nboth_ref[1 - slot])
        norm = jnp.sum(jnp.sum(sums, axis=1, keepdims=True), axis=0, keepdims=True)
        prior = prior_ref[slot, 0:1, :]
        mean = prior * prior * (norm * (1.0 / CELLS)) + EPSILON
        scale = prior / jnp.sqrt(mean)
        scale_ref[slot] = jnp.broadcast_to(scale, (8, NY))
        weights.append(scale * scale * (occ_ref[2, 0:1, :] * (0.5 / ORBS)))

    @pl.loop(0, GROUP // 2)
    def _(i):
        for side in range(2):
            out_ref[i, side] = flow_ref[0, i + half, side] * weights[0] + flow_ref[1, i + half, side] * weights[1]


def weigh(prior, norms, flow):
    return call(
        "weigh", weigh_body, [(GROUP // 2, 2, PACK, NY), (2, 8, NY)], [vmem()] * 6, flops=500000
    )(prior, *norms, flow)


def curl_body(field_ref, out_ref):
    owner = lax.axis_index("orb")
    place = lax.rem(owner, GROUP)
    tile = place // 2 + half_index()
    odd = lax.rem(place, 2)
    row = lax.broadcasted_iota(jnp.int32, (8, NY), 0)
    keep = ((owner > 0) | (row != 0)) & ((owner < ORBS - 1) | (row != ROWS + 1))
    starts = [pl.multiple_of(8 * jnp.clip(tile + k, 0, TILES - 1), 8) for k in (-1, 0, 1)]

    def window(z, comp):
        before, middle, after = [field_ref[z + MARGIN, comp, pl.ds(s, 8), :] for s in starts]
        first = jnp.where(odd == 1, middle, before)
        second = jnp.where(odd == 1, after, middle)
        shift_first = jnp.where(odd == 1, pltpu.roll(first, 5, 0), pltpu.roll(first, 1, 0))
        shift_second = jnp.where(odd == 1, pltpu.roll(second, 5, 0), pltpu.roll(second, 1, 0))
        split = jnp.where(odd == 1, 5, 1)
        return jnp.where(keep, jnp.where(row < split, shift_first, shift_second), 0.0)

    def x_plus(v):
        return pltpu.roll(v, 7, 0)

    def x_minus(v):
        return pltpu.roll(v, 1, 0)

    planes = [[window(z, comp) for comp in range(3)] for z in range(-1, DEPTH + 1)]
    for z in range(DEPTH):
        ax, ay, az = planes[z + 1]
        axm, aym, azm = planes[z]
        axp, ayp, azp = planes[z + 2]
        ax_up, ax_dn = lane_shifts(ax)
        ay_dn = lane_shifts(ay)[1]
        az_up, az_dn = lane_shifts(az)
        dy_ay = ay - ay_dn
        dx_ax = ax - x_minus(ax)
        inner_x = dy_ay + (az - azm)
        inner_y = dx_ax + (az - azm)
        inner_z = dx_ax + dy_ay
        up_inner_z = (axp - x_minus(axp)) + (ayp - lane_shifts(ayp)[1])
        out_x = (x_plus(inner_x) - inner_x) - (ax_up + ax_dn + axp + axm - 4.0 * ax)
        out_y = (lane_shifts(inner_y)[0] - inner_y) - (x_plus(ay) + x_minus(ay) + ayp + aym - 4.0 * ay)
        out_z = (up_inner_z - inner_z) - (x_plus(az) + x_minus(az) + az_up + az_dn - 4.0 * az)
        for comp, value in enumerate((out_x, out_y, out_z)):
            out_ref[pl.ds((comp * DEPTH + z) * ROWS, ROWS), :] = pltpu.roll(value, 7, 0)[0:ROWS]


def double_curl(field):
    return call("double_curl", curl_body, [(PACK, NY)], [vmem()], flops=1000000)(field)[0]


def update_body(last, got_ref, curl_ref, e_ref, a_ref, *outs):
    total = got_ref[0]
    for i in range(1, GROUP):
        total = total + got_ref[i]
    e_new = e_ref[...] + WAVE_STEP * (curl_ref[...] - total)
    a_new = a_ref[...] - WAVE_STEP * e_new
    if last:
        for ref, value in zip(outs, (e_new, a_new)):
            for comp in range(3):
                for z in range(DEPTH):
                    start = (comp * DEPTH + z) * ROWS
                    ref[comp, pl.ds(z, ROWS, stride=DEPTH), :] = value[start : start + ROWS]
    else:
        copies_ref, a_out_ref, e_out_ref = outs
        a_out_ref[...] = a_new
        e_out_ref[...] = e_new
        for i in range(GROUP):
            copies_ref[i] = a_new


def update(last, got, curl, e_rows, a_rows):
    if last:
        outs = [(3, ROWS * DEPTH, NY)] * 2
    else:
        outs = [(GROUP, PACK, NY), (PACK, NY), (PACK, NY)]
    return call("update", functools.partial(update_body, last), outs, [vmem()] * 4, flops=500000)(got, curl, e_rows, a_rows)


def hand_back_body(wide_ref, out_ref):
    half = half_index()
    for z in range(DEPTH):
        for part in range(2):
            out_ref[z, part] = own_rows(wide_ref[z + 1, 2 + part, PAD : PAD + LOCAL, :], half)


def hand_back(wide):
    return call("hand_back", hand_back_body, [(DEPTH, 2, HALF, NY)], [vmem()])(wide)[0]


def finish_body(scale_ref, wide_ref, theirs_ref, out_ref):
    half = half_index()
    scale = scale_ref[0, 0:1, :]
    for z in range(DEPTH):
        for part in range(2):
            mine = own_rows(wide_ref[z + 1, part, PAD : PAD + LOCAL, :], half) * scale
            theirs = theirs_ref[z, part] * scale
            out_ref[part, pl.ds(z, HALF, stride=DEPTH), :] = jnp.where(half == 0, mine, theirs)
            out_ref[part, pl.ds(HALF * DEPTH + z, HALF, stride=DEPTH), :] = jnp.where(half == 0, theirs, mine)


def finish(scale, wide, theirs):
    return call("finish", finish_body, [(2, NX * DEPTH, NY)], [vmem()] * 3)(scale, wide, theirs)[0]


def everyone(copies):
    return lax.all_to_all(copies, "orb", 0, 0, tiled=True, axis_index_groups=GROUPS)


def per_device(orbitals, potential, occupation, e_field, a_field):
    own, swap, weight, core, chip, corex, chipx, e_rows = prepare(orbitals, potential, e_field)
    other = send(swap, HALVES)
    vcore, vchip = send(core, CORE), send(chip, CHIP)
    orbs = (own, other, vcore, vchip, send(corex, CORE_ACROSS), send(chipx, CHIP_ACROSS))
    a_field, swap = lax.optimization_barrier((a_field, swap))
    copies, a_rows = spread(a_field)
    got = everyone(copies)
    scale = jnp.ones((2, 8, NY), F32)
    for step in range(STEPS):
        last = step == STEPS - 1
        field, edge, acore, achip, acorex, achipx = assemble(got)
        fields = (
            field,
            send(edge, HALVES),
            send(acore, CORE),
            send(achip, CHIP),
            send(acorex, CORE_ACROSS),
            send(achipx, CHIP_ACROSS),
        )
        base, v = stage(2 * HALO * step, orbs, weight, vcore, vchip)
        wide, norm, field = propagate(occupation, base, v, fields)
        norm = norm + send(norm, CORE)
        norms = (norm, send(norm, CHIP_SUM), send(norm, HALVES), send(norm, BOTH_SUM))
        flow = current(wide, field)
        if last:
            theirs = hand_back(wide)
            flow, theirs = lax.optimization_barrier((flow, theirs))
            theirs = send(theirs, HALVES)
        else:
            edge = send(edges(wide), HALVES)
            flow, edge = lax.optimization_barrier((flow, edge))
        flow, scale = weigh(scale, norms, flow)
        flows = everyone(flow.reshape(GROUP, PACK, NY))
        curl = double_curl(field)
        if not last:
            own, other, core, chip = rims(wide, edge)
            flows, core, chip = lax.optimization_barrier((flows, core, chip))
            core, chip = send(core, CORE), send(chip, CHIP)
            copies, a_rows, e_rows = update(last, flows, curl, e_rows, a_rows)
            got = everyone(copies)
            got, core, chip = lax.optimization_barrier((got, core, chip))
            orbs = (own, other, core, chip, core, chip)
        else:
            e_new, a_new = update(last, flows, curl, e_rows, a_rows)
            orbitals = finish(scale, wide, theirs)
    return (
        orbitals.reshape(1, 2, NX, DEPTH, NY),
        e_new.reshape(3, ROWS, DEPTH, NY),
        a_new.reshape(3, ROWS, DEPTH, NY),
    )


def solution(mesh):
    return jax.shard_map(
        per_device,
        mesh=mesh,
        in_specs=(
            P("orb", None, None, "slab", None),
            P(None, "slab", None),
            P("orb"),
            P(None, "orb", "slab", None),
            P(None, "orb", "slab", None),
        ),
        out_specs=(
            P("orb", None, None, "slab", None),
            P(None, "orb", "slab", None),
            P(None, "orb", "slab", None),
        ),
        check_vma=False,
    )
```

```python
import functools

import jax
import jax.numpy as jnp
from jax import lax
from jax.experimental import pallas as pl
from jax.experimental.pallas import tpu as pltpu
from jax.sharding import PartitionSpec as P

TERMS = 4
STEPS = 2
TIME_STEP = 0.3
WAVE_STEP = 0.5
EPSILON = 1e-06

NX = 128
NY = 128
NZ = 32
ORBS = 32
SLABS = 4
CELLS = NX * NY * NZ
DEPTH = NZ // SLABS
ROWS = NX // ORBS
HALO = TERMS + 1
MARGIN = TERMS
WIDE = DEPTH + 2 * HALO
PAD = 8
PACK = 3 * DEPTH * ROWS
CHUNK = 8
F32 = jnp.float32

HALF = NX // 2
LOCAL = HALF + 8
XL = LOCAL + 2 * PAD
GROUP = ORBS // 2
TILES = LOCAL // 8
EARLY = 3
ALL = ("orb", "slab")
MEETING = (1, 2)


def pairs(flip, move):
    found = []
    for orb in range(ORBS):
        for slab in range(SLABS):
            to = move(slab)
            if to is not None:
                found.append((orb * SLABS + slab, (orb ^ flip) * SLABS + to))
    return found


def over_core(slab):
    return slab ^ 1


def over_chip(slab):
    return 3 - slab if slab in MEETING else None


HALVES = pairs(GROUP, lambda slab: slab)
CORE = pairs(0, over_core)
CHIP = pairs(0, over_chip)
CHIP_ACROSS = pairs(GROUP, over_chip)
CHIP_SUM = pairs(0, lambda slab: slab ^ 2)
BOTH_SUM = pairs(GROUP, lambda slab: slab ^ 2)
GROUPS = [list(range(GROUP)), list(range(GROUP, ORBS))]


def send(value, table):
    return lax.ppermute(value, ALL, table)


def vmem():
    return pl.BlockSpec(memory_space=pltpu.VMEM)


def smem():
    return pl.BlockSpec(memory_space=pltpu.SMEM)


def call(name, body, outs, ins, scratch=(), flops=1000000, limit=8):
    shapes = [jax.ShapeDtypeStruct(s, F32) for s in outs]
    size = sum(4 * s.size for s in shapes)
    return pl.pallas_call(
        body,
        name=name,
        out_shape=shapes,
        in_specs=ins,
        out_specs=[vmem()] * len(outs),
        scratch_shapes=list(scratch),
        compiler_params=pltpu.CompilerParams(vmem_limit_bytes=limit * 1024 * 1024),
        cost_estimate=pl.CostEstimate(flops=flops, bytes_accessed=2 * size, transcendentals=0),
    )


def core_index():
    return lax.rem(lax.axis_index("slab"), 2)


def half_index():
    return lax.axis_index("orb") // GROUP


def split_rows(value, half):
    low, high = value[0:LOCAL], value[NX - LOCAL : NX]
    return jnp.where(half == 0, low, high), jnp.where(half == 0, high, low)


def own_rows(value, half):
    return jnp.where(half == 0, value[0:HALF], value[8 : 8 + HALF])


def lane_shifts(value):
    lane = lax.broadcasted_iota(jnp.int32, value.shape, value.ndim - 1)
    plus = jnp.where(lane == NY - 1, 0.0, pltpu.roll(value, NY - 1, value.ndim - 1))
    minus = jnp.where(lane == 0, 0.0, pltpu.roll(value, 1, value.ndim - 1))
    return plus, minus


def half_rows(shape):
    return lax.broadcasted_iota(jnp.int32, shape, len(shape) - 2) % 8 < 4


def to_rows(ref, rows_ref):
    for comp in range(3):
        for z in range(DEPTH):
            rows_ref[pl.ds((comp * DEPTH + z) * ROWS, ROWS), :] = ref[comp, pl.ds(z, ROWS, stride=DEPTH), :]


def prepare_body(
    orb_ref, pot_ref, e_ref, own_ref, swap_ref, weight_ref, core_ref, chip_ref, chipx_ref, e_rows_ref
):
    core, half = core_index(), half_index()
    to_rows(e_ref, e_rows_ref)
    for z in range(DEPTH):
        for part in range(2):
            own_ref[z, part], swap_ref[z, part] = split_rows(orb_ref[part, pl.ds(z, NX, stride=DEPTH), :], half)
        weight_ref[z] = split_rows(2.0 * pot_ref[pl.ds(z, NX, stride=DEPTH), :] + 6.0, half)[0]
    to_core = (1 - core) * (DEPTH - HALO)
    to_chip = core * (DEPTH - HALO)
    for i in range(HALO):
        for part in range(2):
            core_ref[2 * i + part] = own_ref[to_core + i, part]
            chip_ref[2 * i + part] = own_ref[to_chip + i, part]
            chipx_ref[2 * i + part] = swap_ref[to_chip + i, part]
    for i in range(MARGIN):
        core_ref[2 * HALO + i] = weight_ref[(1 - core) * (DEPTH - MARGIN) + i]
        chip_ref[2 * HALO + i] = weight_ref[core * (DEPTH - MARGIN) + i]


def prepare(orbitals, potential, e_field):
    planes = 2 * HALO + MARGIN
    return call(
        "prepare",
        prepare_body,
        [(DEPTH, 2, LOCAL, NY)] * 2
        + [(DEPTH, LOCAL, NY)]
        + [(planes, LOCAL, NY)] * 2
        + [(2 * HALO, LOCAL, NY)]
        + [(PACK, NY)],
        [vmem()] * 3,
        limit=12,
    )(
        orbitals.reshape(2, NX * DEPTH, NY),
        potential.reshape(NX * DEPTH, NY),
        e_field.reshape(3, ROWS * DEPTH, NY),
    )


def lend_body(other_ref, out_ref):
    to_core = (1 - core_index()) * (DEPTH - HALO)
    for i in range(HALO):
        for part in range(2):
            out_ref[2 * i + part] = other_ref[to_core + i, part]


def lend(other):
    return call("lend", lend_body, [(2 * HALO, LOCAL, NY)], [vmem()])(other)[0]


def edges_body(wide_ref, out_ref):
    half = half_index()
    for z in range(DEPTH):
        for k in range(4):
            low = wide_ref[z + 1, k, PAD + HALF - 8 : PAD + HALF, :]
            out_ref[z, k] = jnp.where(half == 0, low, wide_ref[z + 1, k, PAD + 8 : PAD + 16, :])


def edges(wide):
    return call("edges", edges_body, [(DEPTH, 4, 8, NY)], [vmem()])(wide)[0]


def rims_body(wide_ref, edge_ref, own_ref, other_ref, core_ref, chip_ref, chipx_ref):
    core, half = core_index(), half_index()
    for z in range(DEPTH):
        for slot, ref in enumerate((own_ref, other_ref)):
            for part in range(2):
                value = wide_ref[z + 1, 2 * slot + part, PAD : PAD + LOCAL, :]
                edge = edge_ref[z, 2 * (1 - slot) + part]
                ref[z, part, 0:8, :] = jnp.where(half == 0, value[0:8], edge)
                ref[z, part, 8:HALF, :] = value[8:HALF]
                ref[z, part, HALF:LOCAL, :] = jnp.where(half == 0, edge, value[HALF:LOCAL])
    to_core = (1 - core) * (DEPTH - HALO)
    to_chip = core * (DEPTH - HALO)
    for i in range(HALO):
        for slot, ref in enumerate((own_ref, other_ref)):
            for part in range(2):
                core_ref[2 * (HALO * slot + i) + part] = ref[to_core + i, part]
                (chip_ref, chipx_ref)[slot][2 * i + part] = ref[to_chip + i, part]


def rims(wide, edge):
    return call(
        "rims", rims_body, [(DEPTH, 2, LOCAL, NY)] * 2 + [(4 * HALO, LOCAL, NY)] + [(2 * HALO, LOCAL, NY)] * 2, [vmem()] * 2, limit=12
    )(wide, edge)


def spread_body(a_ref, copies_ref, a_rows_ref):
    to_rows(a_ref, a_rows_ref)
    value = a_rows_ref[...]
    for i in range(GROUP):
        copies_ref[i] = value


def spread(a_field):
    return call("spread", spread_body, [(GROUP, PACK, NY), (PACK, NY)], [vmem()])(
        a_field.reshape(3, ROWS * DEPTH, NY)
    )


def assemble_body(got_ref, field_ref, edge_ref, core_ref, chip_ref, chipx_ref):
    core, half = core_index(), half_index()
    low = half_rows((GROUP // 2, 8, NY))
    for comp in range(3):
        for pair in range(DEPTH // 2):
            rows = pl.ds((comp * DEPTH + 2 * pair) * ROWS, 8)
            first = got_ref[:, 0, rows, :]
            second = got_ref[:, 1, rows, :]
            even = jnp.where(low, first, pltpu.roll(second, 4, 1))
            odd = jnp.where(low, pltpu.roll(first, 4, 1), second)
            for z, value in ((2 * pair, even), (2 * pair + 1, odd)):
                field_ref[z, comp] = value.reshape(HALF, NY)
                edge_ref[z, comp] = jnp.where(half == 0, value[GROUP // 2 - 1], value[0])
    for i in range(MARGIN):
        to_core = (1 - core) * (DEPTH - MARGIN) + i
        to_chip = core * (DEPTH - MARGIN) + i
        for comp in range(3):
            core_ref[i, comp] = field_ref[to_core, comp]
            chip_ref[i, comp] = field_ref[to_chip, comp]
            chipx_ref[i, comp] = edge_ref[to_chip, comp]


def assemble(got):
    return call(
        "assemble",
        assemble_body,
        [(DEPTH, 3, HALF, NY), (DEPTH, 3, 8, NY)]
        + [(MARGIN, 3, HALF, NY)] * 2
        + [(MARGIN, 3, 8, NY)],
        [vmem()],
    )(got.reshape(GROUP // 2, 2, PACK, NY))


def corners_body(edge_ref, core_ref, out_ref):
    core, half = core_index(), half_index()
    for comp in range(3):
        for z in range(DEPTH):
            out_ref[z + MARGIN * core, comp] = edge_ref[z, comp]
        for i in range(MARGIN):
            out_ref[(1 - core) * DEPTH + i, comp] = jnp.where(
                half == 0, core_ref[i, comp, HALF - 8 : HALF, :], core_ref[i, comp, 0:8, :]
            )


def corners(edge, acore):
    return call("corners", corners_body, [(DEPTH + MARGIN, 3, 8, NY)], [vmem()] * 2)(edge, acore)[0]


def clear(ref, count):
    zeros = jnp.zeros((PAD, NY), F32)

    @pl.loop(0, count)
    def _(j):
        for k in range(4):
            ref[j, k, 0:PAD, :] = zeros
            ref[j, k, PAD + LOCAL : XL, :] = zeros


def stage_body(
    first, own_ref, other_ref, hcore_ref, hchip_ref, hcorex_ref, hchipx_ref, weight_ref, vcore_ref, vchip_ref,
    base_ref, v_ref,
):
    core = core_index()
    clear(base_ref, WIDE)

    @pl.loop(0, DEPTH)
    def _(z):
        for part in range(2):
            base_ref[z + HALO, part, PAD : PAD + LOCAL, :] = own_ref[z, part]
            base_ref[z + HALO, 2 + part, PAD : PAD + LOCAL, :] = other_ref[z, part]
        v_ref[z + MARGIN] = weight_ref[z]

    def put_halo(above, orb_ref, orbx_ref, offset, pot_ref):
        @pl.loop(0, HALO)
        def _(i):
            j = above * (DEPTH + HALO) + i
            for part in range(2):
                base_ref[j, part, PAD : PAD + LOCAL, :] = orb_ref[2 * i + part]
                base_ref[j, 2 + part, PAD : PAD + LOCAL, :] = orbx_ref[offset + 2 * i + part]

        @pl.loop(0, MARGIN)
        def _(i):
            v_ref[above * (DEPTH + MARGIN) + i] = pot_ref[2 * HALO + i]

    @pl.when(core == 1)
    def _():
        put_halo(0, hcore_ref, hcorex_ref, first, vcore_ref)
        put_halo(1, hchip_ref, hchipx_ref, 0, vchip_ref)

    @pl.when(core == 0)
    def _():
        put_halo(1, hcore_ref, hcorex_ref, first, vcore_ref)
        put_halo(0, hchip_ref, hchipx_ref, 0, vchip_ref)


def stage(first, orbs, weight, vcore, vchip):
    return call(
        "stage",
        functools.partial(stage_body, first),
        [(WIDE, 4, XL, NY), (DEPTH + 2 * MARGIN, LOCAL, NY)],
        [vmem()] * 9,
        flops=1000000,
        limit=16,
    )(*orbs, weight, vcore, vchip)


def propagate_body(
    occ_ref, base_ref, v_ref, field_ref, edge_ref, acore_ref, achip_ref, achipx_ref,
    out_ref, norm_ref, a_ref, ping_ref, pong_ref, w_ref,
):
    core, half = core_index(), half_index()
    clear(ping_ref, WIDE)
    clear(pong_ref, WIDE)
    clear(out_ref, DEPTH + 2)

    def put_field(j, fld_ref, edg_ref, i, k):
        total = v_ref[j]
        for comp in range(3):
            value, edge = fld_ref[i, comp], edg_ref[k, comp]
            joined = jnp.where(
                half == 0, jnp.concatenate([value, edge], axis=0), jnp.concatenate([edge, value], axis=0)
            )
            a_ref[j, comp] = joined
            total = total + joined * joined
        w_ref[j] = total

    @pl.loop(0, DEPTH)
    def _(z):
        put_field(z + MARGIN, field_ref, edge_ref, z, z + MARGIN * core)

    @pl.loop(0, MARGIN)
    def _(i):
        put_field((1 - core) * (DEPTH + MARGIN) + i, acore_ref, edge_ref, i, (1 - core) * DEPTH + i)
        put_field(core * (DEPTH + MARGIN) + i, achip_ref, achipx_ref, i, i)

    first = lax.axis_index("slab") * DEPTH - HALO
    sums = [jnp.zeros((8, NY), F32), jnp.zeros((8, NY), F32)]

    def plane(j, order, source, target, shift):
        depth = first + j
        inside = jnp.where((depth >= 0) & (depth < NZ), 1.0, 0.0).astype(F32)
        factor = inside * (0.5 * TIME_STEP / order)
        for r in range(0, LOCAL, CHUNK):
            here = pl.ds(PAD + r, CHUNK)
            fields = [a_ref[j - 1, comp, r : r + CHUNK, :] for comp in range(3)]
            weight = w_ref[j - 1, r : r + CHUNK, :]
            for slot in range(2):
                centre, total, drift = [], [], []
                for k in (2 * slot, 2 * slot + 1):
                    mid = source[j, k, here, :]
                    xp = source[j, k, pl.ds(PAD + r + 1, CHUNK), :]
                    xm = source[j, k, pl.ds(PAD + r - 1, CHUNK), :]
                    zp = source[j + 1, k, here, :]
                    zm = source[j - 1, k, here, :]
                    yp, ym = lane_shifts(mid)
                    centre.append(mid)
                    total.append((xp + xm) + (yp + ym) + (zp + zm))
                    drift.append(fields[0] * (xp - xm) + fields[1] * (yp - ym) + fields[2] * (zp - zm))
                real_h = weight * centre[0] - total[0] + drift[1]
                imag_h = weight * centre[1] - total[1] - drift[0]
                for part, change in enumerate((factor * imag_h, -factor * real_h)):
                    value = base_ref[j, 2 * slot + part, here, :] + change
                    target[j + shift, 2 * slot + part, here, :] = value
                    if order == 1 and HALO <= j < HALO + DEPTH:
                        square = value * value
                        if r == 0:
                            square = jnp.where(half == 0, square, 0.0)
                        if r == LOCAL - 8:
                            square = jnp.where(half == 1, square, 0.0)
                        sums[slot] = sums[slot] + square

    source = base_ref
    for done, order in enumerate(range(TERMS, 0, -1)):
        target = out_ref if order == 1 else (ping_ref, pong_ref)[done % 2]
        for j in range(done + 1, WIDE - done - 1):
            plane(j, order, source, target, 1 - HALO if order == 1 else 0)
        source = target
    norm_ref[0] = sums[0]
    norm_ref[1] = sums[1]
    norm_ref[2] = jnp.broadcast_to(occ_ref[0], (8, NY))


def propagate(occupation, base, v, fields):
    return call(
        "propagate",
        propagate_body,
        [(DEPTH + 2, 4, XL, NY), (3, 8, NY), (DEPTH + 2 * MARGIN, 3, LOCAL, NY)],
        [smem()] + [vmem()] * 7,
        [
            pltpu.VMEM((WIDE, 4, XL, NY), F32),
            pltpu.VMEM((WIDE, 4, XL, NY), F32),
            pltpu.VMEM((DEPTH + 2 * MARGIN, LOCAL, NY), F32),
        ],
        flops=60000000,
        limit=26,
    )(occupation, base, v, *fields)


def current_body(wide_ref, field_ref, flow_ref):
    low = half_rows((8, NY))

    @pl.loop(0, DEPTH // 2)
    def _(pair):
        for tile in range(TILES):
            r = 8 * tile
            here = pl.ds(PAD + r, 8)
            for slot in range(2):
                both = []
                for z in range(2):
                    j = 2 * pair + z + 1
                    mids, grads = [], []
                    for k in (2 * slot, 2 * slot + 1):
                        mid = wide_ref[j, k, here, :]
                        yp, ym = lane_shifts(mid)
                        mids.append(mid)
                        grads.append(
                            (
                                wide_ref[j, k, pl.ds(PAD + r + 1, 8), :] - wide_ref[j, k, pl.ds(PAD + r - 1, 8), :],
                                yp - ym,
                                wide_ref[j + 1, k, here, :] - wide_ref[j - 1, k, here, :],
                            )
                        )
                    u, w = mids
                    density = u * u + w * w
                    both.append(
                        [
                            0.5 * (u * grads[1][comp] - w * grads[0][comp])
                            + field_ref[j + MARGIN - 1, comp, r : r + 8, :] * density
                            for comp in range(3)
                        ]
                    )
                for comp in range(3):
                    even, odd = both[0][comp], both[1][comp]
                    rows = pl.ds(pl.multiple_of((comp * DEPTH + 2 * pair) * ROWS, 8), 8)
                    flow_ref[slot, tile, 0, rows, :] = jnp.where(low, even, pltpu.roll(odd, 4, 0))
                    flow_ref[slot, tile, 1, rows, :] = jnp.where(low, pltpu.roll(even, 4, 0), odd)


def current(wide, field):
    return call("current", current_body, [(2, TILES, 2, PACK, NY)], [vmem(), vmem()], flops=10000000, limit=10)(
        wide, field
    )[0]


def weigh_body(prior_ref, n_ref, nchip_ref, nhalf_ref, nboth_ref, flow_ref, out_ref, scale_ref):
    half = half_index()
    weights = []
    for slot, occ_ref in enumerate((n_ref, nhalf_ref)):
        sums = (n_ref[slot] + nchip_ref[slot]) + (nhalf_ref[1 - slot] + nboth_ref[1 - slot])
        norm = jnp.sum(jnp.sum(sums, axis=1, keepdims=True), axis=0, keepdims=True)
        prior = prior_ref[slot, 0:1, :]
        mean = prior * prior * (norm * (1.0 / CELLS)) + EPSILON
        scale = prior / jnp.sqrt(mean)
        scale_ref[slot] = jnp.broadcast_to(scale, (8, NY))
        weights.append(scale * scale * (occ_ref[2, 0:1, :] * (0.5 / ORBS)))

    @pl.loop(0, GROUP // 2)
    def _(i):
        for side in range(2):
            out_ref[i, side] = flow_ref[0, i + half, side] * weights[0] + flow_ref[1, i + half, side] * weights[1]


def weigh(prior, norms, flow):
    return call(
        "weigh", weigh_body, [(GROUP // 2, 2, PACK, NY), (2, 8, NY)], [vmem()] * 6, flops=500000
    )(prior, *norms, flow)


def curl_body(field_ref, out_ref):
    owner = lax.axis_index("orb")
    place = lax.rem(owner, GROUP)
    tile = place // 2 + half_index()
    odd = lax.rem(place, 2)
    row = lax.broadcasted_iota(jnp.int32, (8, NY), 0)
    keep = ((owner > 0) | (row != 0)) & ((owner < ORBS - 1) | (row != ROWS + 1))
    starts = [pl.multiple_of(8 * jnp.clip(tile + k, 0, TILES - 1), 8) for k in (-1, 0, 1)]

    def window(z, comp):
        before, middle, after = [field_ref[z + MARGIN, comp, pl.ds(s, 8), :] for s in starts]
        first = jnp.where(odd == 1, middle, before)
        second = jnp.where(odd == 1, after, middle)
        shift_first = jnp.where(odd == 1, pltpu.roll(first, 5, 0), pltpu.roll(first, 1, 0))
        shift_second = jnp.where(odd == 1, pltpu.roll(second, 5, 0), pltpu.roll(second, 1, 0))
        split = jnp.where(odd == 1, 5, 1)
        return jnp.where(keep, jnp.where(row < split, shift_first, shift_second), 0.0)

    def x_plus(v):
        return pltpu.roll(v, 7, 0)

    def x_minus(v):
        return pltpu.roll(v, 1, 0)

    planes = [[window(z, comp) for comp in range(3)] for z in range(-1, DEPTH + 1)]
    for z in range(DEPTH):
        ax, ay, az = planes[z + 1]
        axm, aym, azm = planes[z]
        axp, ayp, azp = planes[z + 2]
        ax_up, ax_dn = lane_shifts(ax)
        ay_dn = lane_shifts(ay)[1]
        az_up, az_dn = lane_shifts(az)
        dy_ay = ay - ay_dn
        dx_ax = ax - x_minus(ax)
        inner_x = dy_ay + (az - azm)
        inner_y = dx_ax + (az - azm)
        inner_z = dx_ax + dy_ay
        up_inner_z = (axp - x_minus(axp)) + (ayp - lane_shifts(ayp)[1])
        out_x = (x_plus(inner_x) - inner_x) - (ax_up + ax_dn + axp + axm - 4.0 * ax)
        out_y = (lane_shifts(inner_y)[0] - inner_y) - (x_plus(ay) + x_minus(ay) + ayp + aym - 4.0 * ay)
        out_z = (up_inner_z - inner_z) - (x_plus(az) + x_minus(az) + az_up + az_dn - 4.0 * az)
        for comp, value in enumerate((out_x, out_y, out_z)):
            out_ref[pl.ds((comp * DEPTH + z) * ROWS, ROWS), :] = pltpu.roll(value, 7, 0)[0:ROWS]


def double_curl(field):
    return call("double_curl", curl_body, [(PACK, NY)], [vmem()], flops=1000000)(field)[0]


def update_body(last, got_ref, curl_ref, e_ref, a_ref, *outs):
    total = got_ref[0]
    for i in range(1, GROUP):
        total = total + got_ref[i]
    e_new = e_ref[...] + WAVE_STEP * (curl_ref[...] - total)
    a_new = a_ref[...] - WAVE_STEP * e_new
    if last:
        for ref, value in zip(outs, (e_new, a_new)):
            for comp in range(3):
                for z in range(DEPTH):
                    start = (comp * DEPTH + z) * ROWS
                    ref[comp, pl.ds(z, ROWS, stride=DEPTH), :] = value[start : start + ROWS]
    else:
        copies_ref, a_out_ref, e_out_ref = outs
        a_out_ref[...] = a_new
        e_out_ref[...] = e_new
        for i in range(GROUP):
            copies_ref[i] = a_new


def update(last, got, curl, e_rows, a_rows):
    if last:
        outs = [(3, ROWS * DEPTH, NY)] * 2
    else:
        outs = [(GROUP, PACK, NY), (PACK, NY), (PACK, NY)]
    return call("update", functools.partial(update_body, last), outs, [vmem()] * 4, flops=500000)(got, curl, e_rows, a_rows)


def hand_back_body(wide_ref, early_ref, late_ref):
    half = half_index()
    for z in range(DEPTH):
        for part in range(2):
            rows = own_rows(wide_ref[z + 1, 2 + part, PAD : PAD + LOCAL, :], half)
            if z < EARLY:
                early_ref[z, part] = rows
            else:
                late_ref[z - EARLY, part] = rows


def hand_back(wide):
    return call(
        "hand_back", hand_back_body, [(EARLY, 2, HALF, NY), (DEPTH - EARLY, 2, HALF, NY)], [vmem()]
    )(wide)


def finish_body(scale_ref, wide_ref, early_ref, late_ref, out_ref):
    half = half_index()
    scale = scale_ref[0, 0:1, :]
    for z in range(DEPTH):
        for part in range(2):
            mine = own_rows(wide_ref[z + 1, part, PAD : PAD + LOCAL, :], half) * scale
            theirs = (early_ref[z, part] if z < EARLY else late_ref[z - EARLY, part]) * scale
            out_ref[part, pl.ds(z, HALF, stride=DEPTH), :] = jnp.where(half == 0, mine, theirs)
            out_ref[part, pl.ds(HALF * DEPTH + z, HALF, stride=DEPTH), :] = jnp.where(half == 0, theirs, mine)


def finish(scale, wide, early, late):
    return call("finish", finish_body, [(2, NX * DEPTH, NY)], [vmem()] * 4)(scale, wide, early, late)[0]


def everyone(copies):
    return lax.all_to_all(copies, "orb", 0, 0, tiled=True, axis_index_groups=GROUPS)


def per_device(orbitals, potential, occupation, e_field, a_field):
    copies, a_rows = spread(a_field)
    got = everyone(copies)
    own, swap, weight, core, chip, chipx, e_rows = prepare(orbitals, potential, e_field)
    vcore, vchip, chipx = send(core, CORE), send(chip, CHIP), send(chipx, CHIP_ACROSS)
    other = send(swap, HALVES)
    got, vcore, vchip = lax.optimization_barrier((got, vcore, vchip))
    scale = jnp.ones((2, 8, NY), F32)
    for step in range(STEPS):
        last = step == STEPS - 1
        field, edge, acore, achip, achipx = assemble(got)
        acore = send(acore, CORE)
        achip = send(achip, CHIP)
        edge = corners(edge, acore)
        edge = send(edge, HALVES)
        if step == 0:
            edge, other = lax.optimization_barrier((edge, other))
        achipx = send(achipx, CHIP_ACROSS)
        if step == 0:
            orbs = (own, other, vcore, vchip, send(lend(other), CORE), chipx)
        base, v = stage(2 * HALO * step, orbs, weight, vcore, vchip)
        wide, norm, field = propagate(occupation, base, v, (field, edge, acore, achip, achipx))
        norm = norm + send(norm, CORE)
        norms = (norm, send(norm, CHIP_SUM), send(norm, HALVES), send(norm, BOTH_SUM))
        flow = current(wide, field)
        if last:
            early, late = hand_back(wide)
            early = send(early, HALVES)
            flow, early, late = lax.optimization_barrier((flow, early, late))
            late = send(late, HALVES)
        else:
            edge = send(edges(wide), HALVES)
            flow, edge = lax.optimization_barrier((flow, edge))
        flow, scale = weigh(scale, norms, flow)
        flows = everyone(flow.reshape(GROUP, PACK, NY))
        curl = double_curl(field)
        if not last:
            own, other, core, chip, chipx = rims(wide, edge)
            core, chip = send(core, CORE), send(chip, CHIP)
            flows, core, chip, chipx = lax.optimization_barrier((flows, core, chip, chipx))
            chipx = send(chipx, CHIP)
            copies, a_rows, e_rows = update(last, flows, curl, e_rows, a_rows)
            got = everyone(copies)
            got, chipx = lax.optimization_barrier((got, chipx))
            orbs = (own, other, core, chip, core, chipx)
        else:
            e_new, a_new = update(last, flows, curl, e_rows, a_rows)
            orbitals = finish(scale, wide, early, late)
    return (
        orbitals.reshape(1, 2, NX, DEPTH, NY),
        e_new.reshape(3, ROWS, DEPTH, NY),
        a_new.reshape(3, ROWS, DEPTH, NY),
    )


def solution(mesh):
    return jax.shard_map(
        per_device,
        mesh=mesh,
        in_specs=(
            P("orb", None, None, "slab", None),
            P(None, "slab", None),
            P("orb"),
            P(None, "orb", "slab", None),
            P(None, "orb", "slab", None),
        ),
        out_specs=(
            P("orb", None, None, "slab", None),
            P(None, "orb", "slab", None),
            P(None, "orb", "slab", None),
        ),
        check_vma=False,
    )
```

```python
import functools

import jax
import jax.numpy as jnp
from jax import lax
from jax.experimental import pallas as pl
from jax.experimental.pallas import tpu as pltpu
from jax.sharding import PartitionSpec as P

TERMS = 4
STEPS = 2
TIME_STEP = 0.3
WAVE_STEP = 0.5
EPSILON = 1e-06

NX = 128
NY = 128
NZ = 32
ORBS = 32
SLABS = 4
CELLS = NX * NY * NZ
DEPTH = NZ // SLABS
ROWS = NX // ORBS
HALO = TERMS + 1
MARGIN = TERMS
WIDE = DEPTH + 2 * HALO
PAD = 8
PACK = 3 * DEPTH * ROWS
CHUNK = 8
F32 = jnp.float32

HALF = NX // 2
LOCAL = HALF + 8
XL = LOCAL + 2 * PAD
GROUP = ORBS // 2
TILES = LOCAL // 8
EARLY = 3
ALL = ("orb", "slab")
MEETING = (1, 2)


def pairs(flip, move):
    found = []
    for orb in range(ORBS):
        for slab in range(SLABS):
            to = move(slab)
            if to is not None:
                found.append((orb * SLABS + slab, (orb ^ flip) * SLABS + to))
    return found


def over_core(slab):
    return slab ^ 1


def over_chip(slab):
    return 3 - slab if slab in MEETING else None


HALVES = pairs(GROUP, lambda slab: slab)
CORE = pairs(0, over_core)
CHIP = pairs(0, over_chip)
CHIP_ACROSS = pairs(GROUP, over_chip)
CHIP_SUM = pairs(0, lambda slab: slab ^ 2)
BOTH_SUM = pairs(GROUP, lambda slab: slab ^ 2)
GROUPS = [list(range(GROUP)), list(range(GROUP, ORBS))]


def send(value, table):
    return lax.ppermute(value, ALL, table)


def vmem():
    return pl.BlockSpec(memory_space=pltpu.VMEM)


def smem():
    return pl.BlockSpec(memory_space=pltpu.SMEM)


def call(name, body, outs, ins, scratch=(), flops=1000000, limit=8):
    shapes = [jax.ShapeDtypeStruct(s, F32) for s in outs]
    size = sum(4 * s.size for s in shapes)
    return pl.pallas_call(
        body,
        name=name,
        out_shape=shapes,
        in_specs=ins,
        out_specs=[vmem()] * len(outs),
        scratch_shapes=list(scratch),
        compiler_params=pltpu.CompilerParams(vmem_limit_bytes=limit * 1024 * 1024),
        cost_estimate=pl.CostEstimate(flops=flops, bytes_accessed=2 * size, transcendentals=0),
    )


def core_index():
    return lax.rem(lax.axis_index("slab"), 2)


def half_index():
    return lax.axis_index("orb") // GROUP


def split_rows(value, half):
    low, high = value[0:LOCAL], value[NX - LOCAL : NX]
    return jnp.where(half == 0, low, high), jnp.where(half == 0, high, low)


def own_rows(value, half):
    return jnp.where(half == 0, value[0:HALF], value[8 : 8 + HALF])


def lane_shifts(value):
    lane = lax.broadcasted_iota(jnp.int32, value.shape, value.ndim - 1)
    plus = jnp.where(lane == NY - 1, 0.0, pltpu.roll(value, NY - 1, value.ndim - 1))
    minus = jnp.where(lane == 0, 0.0, pltpu.roll(value, 1, value.ndim - 1))
    return plus, minus


def half_rows(shape):
    return lax.broadcasted_iota(jnp.int32, shape, len(shape) - 2) % 8 < 4


def to_rows(ref, rows_ref):
    for comp in range(3):
        for z in range(DEPTH):
            rows_ref[pl.ds((comp * DEPTH + z) * ROWS, ROWS), :] = ref[comp, pl.ds(z, ROWS, stride=DEPTH), :]


def prepare_body(
    orb_ref, pot_ref, a_ref, e_ref, own_ref, swap_ref, weight_ref, core_ref, chip_ref, chipx_ref, rows_ref
):
    core, half = core_index(), half_index()
    to_rows(a_ref, rows_ref.at[0])
    to_rows(e_ref, rows_ref.at[1])
    for z in range(DEPTH):
        for part in range(2):
            own_ref[z, part], swap_ref[z, part] = split_rows(orb_ref[part, pl.ds(z, NX, stride=DEPTH), :], half)
        weight_ref[z] = split_rows(2.0 * pot_ref[pl.ds(z, NX, stride=DEPTH), :] + 6.0, half)[0]
    to_core = (1 - core) * (DEPTH - HALO)
    to_chip = core * (DEPTH - HALO)
    for i in range(HALO):
        for part in range(2):
            core_ref[2 * i + part] = own_ref[to_core + i, part]
            chip_ref[2 * i + part] = own_ref[to_chip + i, part]
            chipx_ref[2 * i + part] = swap_ref[to_chip + i, part]
    for i in range(MARGIN):
        core_ref[2 * HALO + i] = weight_ref[(1 - core) * (DEPTH - MARGIN) + i]
        chip_ref[2 * HALO + i] = weight_ref[core * (DEPTH - MARGIN) + i]


def prepare(orbitals, potential, a_field, e_field):
    planes = 2 * HALO + MARGIN
    return call(
        "prepare",
        prepare_body,
        [(DEPTH, 2, LOCAL, NY)] * 2
        + [(DEPTH, LOCAL, NY)]
        + [(planes, LOCAL, NY)] * 2
        + [(2 * HALO, LOCAL, NY)]
        + [(2, PACK, NY)],
        [vmem()] * 4,
        limit=12,
    )(
        orbitals.reshape(2, NX * DEPTH, NY),
        potential.reshape(NX * DEPTH, NY),
        a_field.reshape(3, ROWS * DEPTH, NY),
        e_field.reshape(3, ROWS * DEPTH, NY),
    )


def lend_body(other_ref, out_ref):
    to_core = (1 - core_index()) * (DEPTH - HALO)
    for i in range(HALO):
        for part in range(2):
            out_ref[2 * i + part] = other_ref[to_core + i, part]


def lend(other):
    return call("lend", lend_body, [(2 * HALO, LOCAL, NY)], [vmem()])(other)[0]


def edges_body(wide_ref, out_ref):
    half = half_index()
    for z in range(DEPTH):
        for k in range(4):
            low = wide_ref[z + 1, k, PAD + HALF - 8 : PAD + HALF, :]
            out_ref[z, k] = jnp.where(half == 0, low, wide_ref[z + 1, k, PAD + 8 : PAD + 16, :])


def edges(wide):
    return call("edges", edges_body, [(DEPTH, 4, 8, NY)], [vmem()])(wide)[0]


def rims_body(wide_ref, edge_ref, own_ref, other_ref, core_ref, chip_ref, chipx_ref):
    core, half = core_index(), half_index()
    for z in range(DEPTH):
        for slot, ref in enumerate((own_ref, other_ref)):
            for part in range(2):
                value = wide_ref[z + 1, 2 * slot + part, PAD : PAD + LOCAL, :]
                edge = edge_ref[z, 2 * (1 - slot) + part]
                ref[z, part, 0:8, :] = jnp.where(half == 0, value[0:8], edge)
                ref[z, part, 8:HALF, :] = value[8:HALF]
                ref[z, part, HALF:LOCAL, :] = jnp.where(half == 0, edge, value[HALF:LOCAL])
    to_core = (1 - core) * (DEPTH - HALO)
    to_chip = core * (DEPTH - HALO)
    for i in range(HALO):
        for slot, ref in enumerate((own_ref, other_ref)):
            for part in range(2):
                core_ref[2 * (HALO * slot + i) + part] = ref[to_core + i, part]
                (chip_ref, chipx_ref)[slot][2 * i + part] = ref[to_chip + i, part]


def rims(wide, edge):
    return call(
        "rims", rims_body, [(DEPTH, 2, LOCAL, NY)] * 2 + [(4 * HALO, LOCAL, NY)] + [(2 * HALO, LOCAL, NY)] * 2, [vmem()] * 2, limit=12
    )(wide, edge)


def spread_body(a_ref, copies_ref, rows_ref):
    to_rows(a_ref, rows_ref)
    value = rows_ref[...]
    for i in range(GROUP):
        copies_ref[i] = value


def spread(a_field):
    return call("spread", spread_body, [(GROUP, PACK, NY)], [vmem()], [pltpu.VMEM((PACK, NY), F32)])(
        a_field.reshape(3, ROWS * DEPTH, NY)
    )[0]


def assemble_body(got_ref, field_ref, edge_ref, core_ref, chip_ref, chipx_ref):
    core, half = core_index(), half_index()
    low = half_rows((GROUP // 2, 8, NY))
    for comp in range(3):
        for pair in range(DEPTH // 2):
            rows = pl.ds((comp * DEPTH + 2 * pair) * ROWS, 8)
            first = got_ref[:, 0, rows, :]
            second = got_ref[:, 1, rows, :]
            even = jnp.where(low, first, pltpu.roll(second, 4, 1))
            odd = jnp.where(low, pltpu.roll(first, 4, 1), second)
            for z, value in ((2 * pair, even), (2 * pair + 1, odd)):
                field_ref[z, comp] = value.reshape(HALF, NY)
                edge_ref[z, comp] = jnp.where(half == 0, pltpu.roll(value[GROUP // 2 - 1], 4, 0), value[0])[0:ROWS]
    for i in range(MARGIN):
        to_core = (1 - core) * (DEPTH - MARGIN) + i
        to_chip = core * (DEPTH - MARGIN) + i
        for comp in range(3):
            core_ref[i, comp] = field_ref[to_core, comp]
            chip_ref[i, comp] = field_ref[to_chip, comp]
            chipx_ref[i, comp] = edge_ref[to_chip, comp]


def assemble(got):
    return call(
        "assemble",
        assemble_body,
        [(DEPTH, 3, HALF, NY), (DEPTH, 3, ROWS, NY)]
        + [(MARGIN, 3, HALF, NY)] * 2
        + [(MARGIN, 3, ROWS, NY)],
        [vmem()],
    )(got.reshape(GROUP // 2, 2, PACK, NY))


def corners_body(edge_ref, core_ref, out_ref):
    core, half = core_index(), half_index()
    for comp in range(3):
        for z in range(DEPTH):
            out_ref[z + MARGIN * core, comp] = edge_ref[z, comp]
        for i in range(MARGIN):
            out_ref[(1 - core) * DEPTH + i, comp] = jnp.where(
                half == 0, core_ref[i, comp, HALF - ROWS : HALF, :], core_ref[i, comp, 0:ROWS, :]
            )


def corners(edge, acore):
    return call("corners", corners_body, [(DEPTH + MARGIN, 3, ROWS, NY)], [vmem()] * 2)(edge, acore)[0]


def clear(ref, count):
    zeros = jnp.zeros((PAD, NY), F32)

    @pl.loop(0, count)
    def _(j):
        for k in range(4):
            ref[j, k, 0:PAD, :] = zeros
            ref[j, k, PAD + LOCAL : XL, :] = zeros


def stage_body(
    first, own_ref, other_ref, hcore_ref, hchip_ref, hcorex_ref, hchipx_ref, weight_ref, vcore_ref, vchip_ref,
    base_ref, v_ref,
):
    core = core_index()
    clear(base_ref, WIDE)

    @pl.loop(0, DEPTH)
    def _(z):
        for part in range(2):
            base_ref[z + HALO, part, PAD : PAD + LOCAL, :] = own_ref[z, part]
            base_ref[z + HALO, 2 + part, PAD : PAD + LOCAL, :] = other_ref[z, part]
        v_ref[z + MARGIN] = weight_ref[z]

    def put_halo(above, orb_ref, orbx_ref, offset, pot_ref):
        @pl.loop(0, HALO)
        def _(i):
            j = above * (DEPTH + HALO) + i
            for part in range(2):
                base_ref[j, part, PAD : PAD + LOCAL, :] = orb_ref[2 * i + part]
                base_ref[j, 2 + part, PAD : PAD + LOCAL, :] = orbx_ref[offset + 2 * i + part]

        @pl.loop(0, MARGIN)
        def _(i):
            v_ref[above * (DEPTH + MARGIN) + i] = pot_ref[2 * HALO + i]

    @pl.when(core == 1)
    def _():
        put_halo(0, hcore_ref, hcorex_ref, first, vcore_ref)
        put_halo(1, hchip_ref, hchipx_ref, 0, vchip_ref)

    @pl.when(core == 0)
    def _():
        put_halo(1, hcore_ref, hcorex_ref, first, vcore_ref)
        put_halo(0, hchip_ref, hchipx_ref, 0, vchip_ref)


def stage(first, orbs, weight, vcore, vchip):
    return call(
        "stage",
        functools.partial(stage_body, first),
        [(WIDE, 4, XL, NY), (DEPTH + 2 * MARGIN, LOCAL, NY)],
        [vmem()] * 9,
        flops=1000000,
        limit=16,
    )(*orbs, weight, vcore, vchip)


def propagate_body(
    occ_ref, base_ref, v_ref, field_ref, edge_ref, acore_ref, achip_ref, achipx_ref,
    out_ref, norm_ref, a_ref, ping_ref, pong_ref, w_ref,
):
    core, half = core_index(), half_index()
    clear(ping_ref, WIDE)
    clear(pong_ref, WIDE)
    clear(out_ref, DEPTH + 2)

    near = half_rows((8, NY)) == (half == 0)

    def put_field(j, fld_ref, edg_ref, i, k):
        total = v_ref[j]
        for comp in range(3):
            value, edge = fld_ref[i, comp], edg_ref[k, comp]
            edge = jnp.where(near, jnp.concatenate([edge, edge], axis=0), 0.0)
            joined = jnp.where(
                half == 0, jnp.concatenate([value, edge], axis=0), jnp.concatenate([edge, value], axis=0)
            )
            a_ref[j, comp] = joined
            total = total + joined * joined
        w_ref[j] = total

    @pl.loop(0, DEPTH)
    def _(z):
        put_field(z + MARGIN, field_ref, edge_ref, z, z + MARGIN * core)

    @pl.loop(0, MARGIN)
    def _(i):
        put_field((1 - core) * (DEPTH + MARGIN) + i, acore_ref, edge_ref, i, (1 - core) * DEPTH + i)
        put_field(core * (DEPTH + MARGIN) + i, achip_ref, achipx_ref, i, i)

    first = lax.axis_index("slab") * DEPTH - HALO
    sums = [jnp.zeros((8, NY), F32), jnp.zeros((8, NY), F32)]

    def plane(j, order, source, target, shift):
        depth = first + j
        inside = jnp.where((depth >= 0) & (depth < NZ), 1.0, 0.0).astype(F32)
        factor = inside * (0.5 * TIME_STEP / order)
        for r in range(0, LOCAL, CHUNK):
            here = pl.ds(PAD + r, CHUNK)
            fields = [a_ref[j - 1, comp, r : r + CHUNK, :] for comp in range(3)]
            weight = w_ref[j - 1, r : r + CHUNK, :]
            for slot in range(2):
                centre, total, drift = [], [], []
                for k in (2 * slot, 2 * slot + 1):
                    mid = source[j, k, here, :]
                    xp = source[j, k, pl.ds(PAD + r + 1, CHUNK), :]
                    xm = source[j, k, pl.ds(PAD + r - 1, CHUNK), :]
                    zp = source[j + 1, k, here, :]
                    zm = source[j - 1, k, here, :]
                    yp, ym = lane_shifts(mid)
                    centre.append(mid)
                    total.append((xp + xm) + (yp + ym) + (zp + zm))
                    drift.append(fields[0] * (xp - xm) + fields[1] * (yp - ym) + fields[2] * (zp - zm))
                real_h = weight * centre[0] - total[0] + drift[1]
                imag_h = weight * centre[1] - total[1] - drift[0]
                for part, change in enumerate((factor * imag_h, -factor * real_h)):
                    value = base_ref[j, 2 * slot + part, here, :] + change
                    target[j + shift, 2 * slot + part, here, :] = value
                    if order == 1 and HALO <= j < HALO + DEPTH:
                        square = value * value
                        if r == 0:
                            square = jnp.where(half == 0, square, 0.0)
                        if r == LOCAL - 8:
                            square = jnp.where(half == 1, square, 0.0)
                        sums[slot] = sums[slot] + square

    source = base_ref
    for done, order in enumerate(range(TERMS, 0, -1)):
        target = out_ref if order == 1 else (ping_ref, pong_ref)[done % 2]
        for j in range(done + 1, WIDE - done - 1):
            plane(j, order, source, target, 1 - HALO if order == 1 else 0)
        source = target
    norm_ref[0] = sums[0]
    norm_ref[1] = sums[1]
    norm_ref[2] = jnp.broadcast_to(occ_ref[0], (8, NY))


def propagate(occupation, base, v, fields):
    return call(
        "propagate",
        propagate_body,
        [(DEPTH + 2, 4, XL, NY), (3, 8, NY), (DEPTH + 2 * MARGIN, 3, LOCAL, NY)],
        [smem()] + [vmem()] * 7,
        [
            pltpu.VMEM((WIDE, 4, XL, NY), F32),
            pltpu.VMEM((WIDE, 4, XL, NY), F32),
            pltpu.VMEM((DEPTH + 2 * MARGIN, LOCAL, NY), F32),
        ],
        flops=60000000,
        limit=26,
    )(occupation, base, v, *fields)


def current_body(wide_ref, field_ref, flow_ref):
    low = half_rows((8, NY))

    @pl.loop(0, DEPTH // 2)
    def _(pair):
        for tile in range(TILES):
            r = 8 * tile
            here = pl.ds(PAD + r, 8)
            for slot in range(2):
                both = []
                for z in range(2):
                    j = 2 * pair + z + 1
                    mids, grads = [], []
                    for k in (2 * slot, 2 * slot + 1):
                        mid = wide_ref[j, k, here, :]
                        yp, ym = lane_shifts(mid)
                        mids.append(mid)
                        grads.append(
                            (
                                wide_ref[j, k, pl.ds(PAD + r + 1, 8), :] - wide_ref[j, k, pl.ds(PAD + r - 1, 8), :],
                                yp - ym,
                                wide_ref[j + 1, k, here, :] - wide_ref[j - 1, k, here, :],
                            )
                        )
                    u, w = mids
                    density = u * u + w * w
                    both.append(
                        [
                            0.5 * (u * grads[1][comp] - w * grads[0][comp])
                            + field_ref[j + MARGIN - 1, comp, r : r + 8, :] * density
                            for comp in range(3)
                        ]
                    )
                for comp in range(3):
                    even, odd = both[0][comp], both[1][comp]
                    rows = pl.ds(pl.multiple_of((comp * DEPTH + 2 * pair) * ROWS, 8), 8)
                    flow_ref[slot, tile, 0, rows, :] = jnp.where(low, even, pltpu.roll(odd, 4, 0))
                    flow_ref[slot, tile, 1, rows, :] = jnp.where(low, pltpu.roll(even, 4, 0), odd)


def current(wide, field):
    return call("current", current_body, [(2, TILES, 2, PACK, NY)], [vmem(), vmem()], flops=10000000, limit=10)(
        wide, field
    )[0]


def weigh_body(prior_ref, n_ref, nchip_ref, nhalf_ref, nboth_ref, flow_ref, out_ref, scale_ref):
    half = half_index()
    weights = []
    for slot, occ_ref in enumerate((n_ref, nhalf_ref)):
        sums = (n_ref[slot] + nchip_ref[slot]) + (nhalf_ref[1 - slot] + nboth_ref[1 - slot])
        norm = jnp.sum(jnp.sum(sums, axis=1, keepdims=True), axis=0, keepdims=True)
        prior = prior_ref[slot, 0:1, :]
        mean = prior * prior * (norm * (1.0 / CELLS)) + EPSILON
        scale = prior / jnp.sqrt(mean)
        scale_ref[slot] = jnp.broadcast_to(scale, (8, NY))
        weights.append(scale * scale * (occ_ref[2, 0:1, :] * (0.5 / ORBS)))

    @pl.loop(0, GROUP // 2)
    def _(i):
        for side in range(2):
            out_ref[i, side] = flow_ref[0, i + half, side] * weights[0] + flow_ref[1, i + half, side] * weights[1]


def weigh(prior, norms, flow):
    return call(
        "weigh", weigh_body, [(GROUP // 2, 2, PACK, NY), (2, 8, NY)], [vmem()] * 6, flops=500000
    )(prior, *norms, flow)


def curl_body(field_ref, rows_ref, out_ref):
    owner = lax.axis_index("orb")
    place = lax.rem(owner, GROUP)
    tile = place // 2 + half_index()
    odd = lax.rem(place, 2)
    row = lax.broadcasted_iota(jnp.int32, (8, NY), 0)
    keep = ((owner > 0) | (row != 0)) & ((owner < ORBS - 1) | (row != ROWS + 1))
    starts = [pl.multiple_of(8 * jnp.clip(tile + k, 0, TILES - 1), 8) for k in (-1, 0, 1)]

    def window(z, comp):
        before, middle, after = [field_ref[z + MARGIN, comp, pl.ds(s, 8), :] for s in starts]
        first = jnp.where(odd == 1, middle, before)
        second = jnp.where(odd == 1, after, middle)
        shift_first = jnp.where(odd == 1, pltpu.roll(first, 5, 0), pltpu.roll(first, 1, 0))
        shift_second = jnp.where(odd == 1, pltpu.roll(second, 5, 0), pltpu.roll(second, 1, 0))
        split = jnp.where(odd == 1, 5, 1)
        return jnp.where(keep, jnp.where(row < split, shift_first, shift_second), 0.0)

    def x_plus(v):
        return pltpu.roll(v, 7, 0)

    def x_minus(v):
        return pltpu.roll(v, 1, 0)

    planes = [[window(z, comp) for comp in range(3)] for z in range(-1, DEPTH + 1)]
    for z in range(DEPTH):
        ax, ay, az = planes[z + 1]
        axm, aym, azm = planes[z]
        axp, ayp, azp = planes[z + 2]
        ax_up, ax_dn = lane_shifts(ax)
        ay_dn = lane_shifts(ay)[1]
        az_up, az_dn = lane_shifts(az)
        dy_ay = ay - ay_dn
        dx_ax = ax - x_minus(ax)
        inner_x = dy_ay + (az - azm)
        inner_y = dx_ax + (az - azm)
        inner_z = dx_ax + dy_ay
        up_inner_z = (axp - x_minus(axp)) + (ayp - lane_shifts(ayp)[1])
        out_x = (x_plus(inner_x) - inner_x) - (ax_up + ax_dn + axp + axm - 4.0 * ax)
        out_y = (lane_shifts(inner_y)[0] - inner_y) - (x_plus(ay) + x_minus(ay) + ayp + aym - 4.0 * ay)
        out_z = (up_inner_z - inner_z) - (x_plus(az) + x_minus(az) + az_up + az_dn - 4.0 * az)
        for comp, value in enumerate((out_x, out_y, out_z)):
            out_ref[1, pl.ds((comp * DEPTH + z) * ROWS, ROWS), :] = pltpu.roll(value, 7, 0)[0:ROWS]
    e_part = rows_ref[1] + WAVE_STEP * out_ref[1]
    out_ref[1] = e_part
    out_ref[0] = rows_ref[0] - WAVE_STEP * e_part


def double_curl(field, rows):
    return call("double_curl", curl_body, [(2, PACK, NY)], [vmem()] * 2, flops=1000000)(field, rows)[0]


def update_body(last, got_ref, part_ref, *outs):
    total = got_ref[0]
    for i in range(1, GROUP):
        total = total + got_ref[i]
    e_new = part_ref[1] - WAVE_STEP * total
    a_new = part_ref[0] + WAVE_STEP * WAVE_STEP * total
    if last:
        for ref, value in zip(outs, (e_new, a_new)):
            for comp in range(3):
                for z in range(DEPTH):
                    start = (comp * DEPTH + z) * ROWS
                    ref[comp, pl.ds(z, ROWS, stride=DEPTH), :] = value[start : start + ROWS]
    else:
        copies_ref, rows_ref = outs
        rows_ref[0] = a_new
        rows_ref[1] = e_new
        for i in range(GROUP):
            copies_ref[i] = a_new


def update(last, got, part):
    if last:
        outs = [(3, ROWS * DEPTH, NY)] * 2
    else:
        outs = [(GROUP, PACK, NY), (2, PACK, NY)]
    return call("update", functools.partial(update_body, last), outs, [vmem()] * 2, flops=500000)(got, part)


def hand_back_body(wide_ref, early_ref, late_ref):
    half = half_index()
    for z in range(DEPTH):
        for part in range(2):
            rows = own_rows(wide_ref[z + 1, 2 + part, PAD : PAD + LOCAL, :], half)
            if z < EARLY:
                early_ref[z, part] = rows
            else:
                late_ref[z - EARLY, part] = rows


def hand_back(wide):
    return call(
        "hand_back", hand_back_body, [(EARLY, 2, HALF, NY), (DEPTH - EARLY, 2, HALF, NY)], [vmem()]
    )(wide)


def finish_body(scale_ref, wide_ref, early_ref, late_ref, out_ref):
    half = half_index()
    scale = scale_ref[0, 0:1, :]
    for z in range(DEPTH):
        for part in range(2):
            mine = own_rows(wide_ref[z + 1, part, PAD : PAD + LOCAL, :], half) * scale
            theirs = (early_ref[z, part] if z < EARLY else late_ref[z - EARLY, part]) * scale
            out_ref[part, pl.ds(z, HALF, stride=DEPTH), :] = jnp.where(half == 0, mine, theirs)
            out_ref[part, pl.ds(HALF * DEPTH + z, HALF, stride=DEPTH), :] = jnp.where(half == 0, theirs, mine)


def finish(scale, wide, early, late):
    return call("finish", finish_body, [(2, NX * DEPTH, NY)], [vmem()] * 4)(scale, wide, early, late)[0]


def everyone(copies):
    return lax.all_to_all(copies, "orb", 0, 0, tiled=True, axis_index_groups=GROUPS)


def per_device(orbitals, potential, occupation, e_field, a_field):
    got = everyone(spread(a_field))
    own, swap, weight, core, chip, chipx, rows = prepare(orbitals, potential, a_field, e_field)
    vcore, vchip, chipx = send(core, CORE), send(chip, CHIP), send(chipx, CHIP_ACROSS)
    other = send(swap, HALVES)
    got, vcore = lax.optimization_barrier((got, vcore))
    scale = jnp.ones((2, 8, NY), F32)
    for step in range(STEPS):
        last = step == STEPS - 1
        field, edge, acore, achip, achipx = assemble(got)
        acore = send(acore, CORE)
        achip = send(achip, CHIP)
        edge = corners(edge, acore)
        edge = send(edge, HALVES)
        if step == 0:
            edge, other = lax.optimization_barrier((edge, other))
        achipx = send(achipx, CHIP_ACROSS)
        if step == 0:
            orbs = (own, other, vcore, vchip, send(lend(other), CORE), chipx)
        base, v = stage(2 * HALO * step, orbs, weight, vcore, vchip)
        wide, norm, field = propagate(occupation, base, v, (field, edge, acore, achip, achipx))
        norm, late_wide = lax.optimization_barrier((norm + send(norm, CORE), wide))
        norms = (norm, send(norm, CHIP_SUM), send(norm, HALVES), send(norm, BOTH_SUM))
        flow = current(wide, field)
        if last:
            early, late = hand_back(late_wide)
            early = send(early, HALVES)
            flow, early, late = lax.optimization_barrier((flow, early, late))
            late = send(late, HALVES)
        else:
            edge = send(edges(late_wide), HALVES)
            flow, edge = lax.optimization_barrier((flow, edge))
        flow, scale = weigh(scale, norms, flow)
        flows = everyone(flow.reshape(GROUP, PACK, NY))
        part = double_curl(field, rows)
        if not last:
            own, other, core, chip, chipx = rims(wide, edge)
            core, chip = send(core, CORE), send(chip, CHIP)
            flows, core, chip, chipx = lax.optimization_barrier((flows, core, chip, chipx))
            chipx = send(chipx, CHIP)
            copies, rows = update(last, flows, part)
            got = everyone(copies)
            got, chipx = lax.optimization_barrier((got, chipx))
            orbs = (own, other, core, chip, core, chipx)
        else:
            e_new, a_new = update(last, flows, part)
            orbitals = finish(scale, wide, early, late)
    return (
        orbitals.reshape(1, 2, NX, DEPTH, NY),
        e_new.reshape(3, ROWS, DEPTH, NY),
        a_new.reshape(3, ROWS, DEPTH, NY),
    )


def solution(mesh):
    return jax.shard_map(
        per_device,
        mesh=mesh,
        in_specs=(
            P("orb", None, None, "slab", None),
            P(None, "slab", None),
            P("orb"),
            P(None, "orb", "slab", None),
            P(None, "orb", "slab", None),
        ),
        out_specs=(
            P("orb", None, None, "slab", None),
            P(None, "orb", "slab", None),
            P(None, "orb", "slab", None),
        ),
        check_vma=False,
    )
```

```python
import functools

import jax
import jax.numpy as jnp
from jax import lax
from jax.experimental import pallas as pl
from jax.experimental.pallas import tpu as pltpu
from jax.sharding import PartitionSpec as P

TERMS = 4
STEPS = 2
TIME_STEP = 0.3
WAVE_STEP = 0.5
EPSILON = 1e-06

NX = 128
NY = 128
NZ = 32
ORBS = 32
SLABS = 4
CELLS = NX * NY * NZ
DEPTH = NZ // SLABS
ROWS = NX // ORBS
HALO = TERMS + 1
MARGIN = TERMS
WIDE = DEPTH + 2 * HALO
PAD = 8
PACK = 3 * DEPTH * ROWS
CHUNK = 8
F32 = jnp.float32

HALF = NX // 2
LOCAL = HALF + 8
XL = LOCAL + 2 * PAD
GROUP = ORBS // 2
TILES = LOCAL // 8
EARLY = 3
ALL = ("orb", "slab")
MEETING = (1, 2)


def pairs(flip, move):
    found = []
    for orb in range(ORBS):
        for slab in range(SLABS):
            to = move(slab)
            if to is not None:
                found.append((orb * SLABS + slab, (orb ^ flip) * SLABS + to))
    return found


def over_core(slab):
    return slab ^ 1


def over_chip(slab):
    return 3 - slab if slab in MEETING else None


HALVES = pairs(GROUP, lambda slab: slab)
CORE = pairs(0, over_core)
CHIP = pairs(0, over_chip)
CHIP_ACROSS = pairs(GROUP, over_chip)
CHIP_SUM = pairs(0, lambda slab: slab ^ 2)
BOTH_SUM = pairs(GROUP, lambda slab: slab ^ 2)
GROUPS = [list(range(GROUP)), list(range(GROUP, ORBS))]


def send(value, table):
    return lax.ppermute(value, ALL, table)


def vmem():
    return pl.BlockSpec(memory_space=pltpu.VMEM)


def smem():
    return pl.BlockSpec(memory_space=pltpu.SMEM)


def call(name, body, outs, ins, scratch=(), flops=1000000, limit=8):
    shapes = [jax.ShapeDtypeStruct(s, F32) for s in outs]
    size = sum(4 * s.size for s in shapes)
    return pl.pallas_call(
        body,
        name=name,
        out_shape=shapes,
        in_specs=ins,
        out_specs=[vmem()] * len(outs),
        scratch_shapes=list(scratch),
        compiler_params=pltpu.CompilerParams(vmem_limit_bytes=limit * 1024 * 1024),
        cost_estimate=pl.CostEstimate(flops=flops, bytes_accessed=2 * size, transcendentals=0),
    )


def core_index():
    return lax.rem(lax.axis_index("slab"), 2)


def half_index():
    return lax.axis_index("orb") // GROUP


def split_rows(value, half):
    low, high = value[0:LOCAL], value[NX - LOCAL : NX]
    return jnp.where(half == 0, low, high), jnp.where(half == 0, high, low)


def own_rows(value, half):
    return jnp.where(half == 0, value[0:HALF], value[8 : 8 + HALF])


def lane_shifts(value):
    lane = lax.broadcasted_iota(jnp.int32, value.shape, value.ndim - 1)
    plus = jnp.where(lane == NY - 1, 0.0, pltpu.roll(value, NY - 1, value.ndim - 1))
    minus = jnp.where(lane == 0, 0.0, pltpu.roll(value, 1, value.ndim - 1))
    return plus, minus


def half_rows(shape):
    return lax.broadcasted_iota(jnp.int32, shape, len(shape) - 2) % 8 < 4


def to_rows(ref, rows_ref):
    for comp in range(3):
        for z in range(DEPTH):
            rows_ref[pl.ds((comp * DEPTH + z) * ROWS, ROWS), :] = ref[comp, pl.ds(z, ROWS, stride=DEPTH), :]


def prepare_body(
    orb_ref, pot_ref, a_ref, e_ref, own_ref, swap_ref, weight_ref, core_ref, chip_ref, chipx_ref, rows_ref
):
    core, half = core_index(), half_index()
    to_rows(a_ref, rows_ref.at[0])
    to_rows(e_ref, rows_ref.at[1])
    for z in range(DEPTH):
        for part in range(2):
            own_ref[z, part], swap_ref[z, part] = split_rows(orb_ref[part, pl.ds(z, NX, stride=DEPTH), :], half)
        weight_ref[z] = split_rows(2.0 * pot_ref[pl.ds(z, NX, stride=DEPTH), :] + 6.0, half)[0]
    to_core = (1 - core) * (DEPTH - HALO)
    to_chip = core * (DEPTH - HALO)
    for i in range(HALO):
        for part in range(2):
            core_ref[2 * i + part] = own_ref[to_core + i, part]
            chip_ref[2 * i + part] = own_ref[to_chip + i, part]
            chipx_ref[2 * i + part] = swap_ref[to_chip + i, part]
    for i in range(MARGIN):
        core_ref[2 * HALO + i] = weight_ref[(1 - core) * (DEPTH - MARGIN) + i]
        chip_ref[2 * HALO + i] = weight_ref[core * (DEPTH - MARGIN) + i]


def prepare(orbitals, potential, a_field, e_field):
    planes = 2 * HALO + MARGIN
    return call(
        "prepare",
        prepare_body,
        [(DEPTH, 2, LOCAL, NY)] * 2
        + [(DEPTH, LOCAL, NY)]
        + [(planes, LOCAL, NY)] * 2
        + [(2 * HALO, LOCAL, NY)]
        + [(2, PACK, NY)],
        [vmem()] * 4,
        limit=12,
    )(
        orbitals.reshape(2, NX * DEPTH, NY),
        potential.reshape(NX * DEPTH, NY),
        a_field.reshape(3, ROWS * DEPTH, NY),
        e_field.reshape(3, ROWS * DEPTH, NY),
    )


def lend_body(other_ref, out_ref):
    to_core = (1 - core_index()) * (DEPTH - HALO)
    for i in range(HALO):
        for part in range(2):
            out_ref[2 * i + part] = other_ref[to_core + i, part]


def lend(other):
    return call("lend", lend_body, [(2 * HALO, LOCAL, NY)], [vmem()])(other)[0]


def edges_body(wide_ref, out_ref):
    half = half_index()
    for z in range(DEPTH):
        for k in range(4):
            low = wide_ref[z + 1, k, PAD + HALF - 8 : PAD + HALF, :]
            out_ref[z, k] = jnp.where(half == 0, low, wide_ref[z + 1, k, PAD + 8 : PAD + 16, :])


def edges(wide):
    return call("edges", edges_body, [(DEPTH, 4, 8, NY)], [vmem()])(wide)[0]


def rims_body(wide_ref, edge_ref, own_ref, other_ref, core_ref, chip_ref, chipx_ref):
    core, half = core_index(), half_index()
    for z in range(DEPTH):
        for slot, ref in enumerate((own_ref, other_ref)):
            for part in range(2):
                value = wide_ref[z + 1, 2 * slot + part, PAD : PAD + LOCAL, :]
                edge = edge_ref[z, 2 * (1 - slot) + part]
                ref[z, part, 0:8, :] = jnp.where(half == 0, value[0:8], edge)
                ref[z, part, 8:HALF, :] = value[8:HALF]
                ref[z, part, HALF:LOCAL, :] = jnp.where(half == 0, edge, value[HALF:LOCAL])
    to_core = (1 - core) * (DEPTH - HALO)
    to_chip = core * (DEPTH - HALO)
    for i in range(HALO):
        for slot, ref in enumerate((own_ref, other_ref)):
            for part in range(2):
                core_ref[2 * (HALO * slot + i) + part] = ref[to_core + i, part]
                (chip_ref, chipx_ref)[slot][2 * i + part] = ref[to_chip + i, part]


def rims(wide, edge):
    return call(
        "rims", rims_body, [(DEPTH, 2, LOCAL, NY)] * 2 + [(4 * HALO, LOCAL, NY)] + [(2 * HALO, LOCAL, NY)] * 2, [vmem()] * 2, limit=12
    )(wide, edge)


def spread_body(a_ref, copies_ref, rows_ref):
    to_rows(a_ref, rows_ref)
    value = rows_ref[...]
    for i in range(GROUP):
        copies_ref[i] = value


def spread(a_field):
    return call("spread", spread_body, [(GROUP, PACK, NY)], [vmem()], [pltpu.VMEM((PACK, NY), F32)])(
        a_field.reshape(3, ROWS * DEPTH, NY)
    )[0]


def assemble_body(got_ref, field_ref, edge_ref, core_ref, chip_ref, chipx_ref):
    core, half = core_index(), half_index()
    low = half_rows((GROUP // 2, 8, NY))
    for comp in range(3):
        for pair in range(DEPTH // 2):
            rows = pl.ds((comp * DEPTH + 2 * pair) * ROWS, 8)
            first = got_ref[:, 0, rows, :]
            second = got_ref[:, 1, rows, :]
            even = jnp.where(low, first, pltpu.roll(second, 4, 1))
            odd = jnp.where(low, pltpu.roll(first, 4, 1), second)
            for z, value in ((2 * pair, even), (2 * pair + 1, odd)):
                field_ref[z, comp] = value.reshape(HALF, NY)
                edge_ref[z, comp] = jnp.where(half == 0, pltpu.roll(value[GROUP // 2 - 1], 4, 0), value[0])[0:ROWS]
    for i in range(MARGIN):
        to_core = (1 - core) * (DEPTH - MARGIN) + i
        to_chip = core * (DEPTH - MARGIN) + i
        for comp in range(3):
            core_ref[i, comp] = field_ref[to_core, comp]
            chip_ref[i, comp] = field_ref[to_chip, comp]
            chipx_ref[i, comp] = edge_ref[to_chip, comp]


def assemble(got):
    return call(
        "assemble",
        assemble_body,
        [(DEPTH, 3, HALF, NY), (DEPTH, 3, ROWS, NY)]
        + [(MARGIN, 3, HALF, NY)] * 2
        + [(MARGIN, 3, ROWS, NY)],
        [vmem()],
    )(got.reshape(GROUP // 2, 2, PACK, NY))


def corners_body(edge_ref, core_ref, out_ref):
    core, half = core_index(), half_index()
    for comp in range(3):
        for z in range(DEPTH):
            out_ref[z + MARGIN * core, comp] = edge_ref[z, comp]
        for i in range(MARGIN):
            out_ref[(1 - core) * DEPTH + i, comp] = jnp.where(
                half == 0, core_ref[i, comp, HALF - ROWS : HALF, :], core_ref[i, comp, 0:ROWS, :]
            )


def corners(edge, acore):
    return call("corners", corners_body, [(DEPTH + MARGIN, 3, ROWS, NY)], [vmem()] * 2)(edge, acore)[0]


def clear(ref, count):
    zeros = jnp.zeros((PAD, NY), F32)

    @pl.loop(0, count)
    def _(j):
        for k in range(4):
            ref[j, k, 0:PAD, :] = zeros
            ref[j, k, PAD + LOCAL : XL, :] = zeros


def stage_body(
    first, own_ref, other_ref, hcore_ref, hchip_ref, hcorex_ref, hchipx_ref, weight_ref, vcore_ref, vchip_ref,
    base_ref, v_ref,
):
    core = core_index()
    clear(base_ref, WIDE)

    @pl.loop(0, DEPTH)
    def _(z):
        for part in range(2):
            base_ref[z + HALO, part, PAD : PAD + LOCAL, :] = own_ref[z, part]
            base_ref[z + HALO, 2 + part, PAD : PAD + LOCAL, :] = other_ref[z, part]
        v_ref[z + MARGIN] = weight_ref[z]

    def put_halo(above, orb_ref, orbx_ref, offset, pot_ref):
        @pl.loop(0, HALO)
        def _(i):
            j = above * (DEPTH + HALO) + i
            for part in range(2):
                base_ref[j, part, PAD : PAD + LOCAL, :] = orb_ref[2 * i + part]
                base_ref[j, 2 + part, PAD : PAD + LOCAL, :] = orbx_ref[offset + 2 * i + part]

        @pl.loop(0, MARGIN)
        def _(i):
            v_ref[above * (DEPTH + MARGIN) + i] = pot_ref[2 * HALO + i]

    @pl.when(core == 1)
    def _():
        put_halo(0, hcore_ref, hcorex_ref, first, vcore_ref)
        put_halo(1, hchip_ref, hchipx_ref, 0, vchip_ref)

    @pl.when(core == 0)
    def _():
        put_halo(1, hcore_ref, hcorex_ref, first, vcore_ref)
        put_halo(0, hchip_ref, hchipx_ref, 0, vchip_ref)


def stage(first, orbs, weight, vcore, vchip):
    return call(
        "stage",
        functools.partial(stage_body, first),
        [(WIDE, 4, XL, NY), (DEPTH + 2 * MARGIN, LOCAL, NY)],
        [vmem()] * 9,
        flops=1000000,
        limit=16,
    )(*orbs, weight, vcore, vchip)


def propagate_body(
    occ_ref, base_ref, v_ref, field_ref, edge_ref, acore_ref, achip_ref, achipx_ref,
    out_ref, norm_ref, a_ref, ping_ref, pong_ref, w_ref,
):
    core, half = core_index(), half_index()
    clear(ping_ref, WIDE)
    clear(pong_ref, WIDE)
    clear(out_ref, DEPTH + 2)

    near = half_rows((8, NY)) == (half == 0)

    def put_field(j, fld_ref, edg_ref, i, k):
        total = v_ref[j]
        for comp in range(3):
            value, edge = fld_ref[i, comp], edg_ref[k, comp]
            edge = jnp.where(near, jnp.concatenate([edge, edge], axis=0), 0.0)
            joined = jnp.where(
                half == 0, jnp.concatenate([value, edge], axis=0), jnp.concatenate([edge, value], axis=0)
            )
            a_ref[j, comp] = joined
            total = total + joined * joined
        w_ref[j] = total

    @pl.loop(0, DEPTH)
    def _(z):
        put_field(z + MARGIN, field_ref, edge_ref, z, z + MARGIN * core)

    @pl.loop(0, MARGIN)
    def _(i):
        put_field((1 - core) * (DEPTH + MARGIN) + i, acore_ref, edge_ref, i, (1 - core) * DEPTH + i)
        put_field(core * (DEPTH + MARGIN) + i, achip_ref, achipx_ref, i, i)

    first = lax.axis_index("slab") * DEPTH - HALO
    sums = [jnp.zeros((8, NY), F32), jnp.zeros((8, NY), F32)]

    def plane(j, order, source, target, shift):
        depth = first + j
        inside = jnp.where((depth >= 0) & (depth < NZ), 1.0, 0.0).astype(F32)
        factor = inside * (0.5 * TIME_STEP / order)
        for r in range(0, LOCAL, CHUNK):
            here = pl.ds(PAD + r, CHUNK)
            fields = [a_ref[j - 1, comp, r : r + CHUNK, :] for comp in range(3)]
            weight = w_ref[j - 1, r : r + CHUNK, :]
            for slot in range(2):
                centre, total, drift = [], [], []
                for k in (2 * slot, 2 * slot + 1):
                    mid = source[j, k, here, :]
                    xp = source[j, k, pl.ds(PAD + r + 1, CHUNK), :]
                    xm = source[j, k, pl.ds(PAD + r - 1, CHUNK), :]
                    zp = source[j + 1, k, here, :]
                    zm = source[j - 1, k, here, :]
                    yp, ym = lane_shifts(mid)
                    centre.append(mid)
                    total.append((xp + xm) + (yp + ym) + (zp + zm))
                    drift.append(fields[0] * (xp - xm) + fields[1] * (yp - ym) + fields[2] * (zp - zm))
                real_h = weight * centre[0] - total[0] + drift[1]
                imag_h = weight * centre[1] - total[1] - drift[0]
                for part, change in enumerate((factor * imag_h, -factor * real_h)):
                    value = base_ref[j, 2 * slot + part, here, :] + change
                    target[j + shift, 2 * slot + part, here, :] = value
                    if order == 1 and HALO <= j < HALO + DEPTH:
                        square = value * value
                        if r == 0:
                            square = jnp.where(half == 0, square, 0.0)
                        if r == LOCAL - 8:
                            square = jnp.where(half == 1, square, 0.0)
                        sums[slot] = sums[slot] + square

    source = base_ref
    for done, order in enumerate(range(TERMS, 0, -1)):
        target = out_ref if order == 1 else (ping_ref, pong_ref)[done % 2]
        for j in range(done + 1, WIDE - done - 1):
            plane(j, order, source, target, 1 - HALO if order == 1 else 0)
        source = target
    norm_ref[0] = sums[0]
    norm_ref[1] = sums[1]
    norm_ref[2] = jnp.broadcast_to(occ_ref[0], (8, NY))


def propagate(occupation, base, v, fields):
    return call(
        "propagate",
        propagate_body,
        [(DEPTH + 2, 4, XL, NY), (3, 8, NY), (DEPTH + 2 * MARGIN, 3, LOCAL, NY)],
        [smem()] + [vmem()] * 7,
        [
            pltpu.VMEM((WIDE, 4, XL, NY), F32),
            pltpu.VMEM((WIDE, 4, XL, NY), F32),
            pltpu.VMEM((DEPTH + 2 * MARGIN, LOCAL, NY), F32),
        ],
        flops=60000000,
        limit=26,
    )(occupation, base, v, *fields)


def current_body(wide_ref, field_ref, flow_ref):
    low = half_rows((8, NY))

    @pl.loop(0, DEPTH // 2)
    def _(pair):
        for tile in range(TILES):
            r = 8 * tile
            here = pl.ds(PAD + r, 8)
            for slot in range(2):
                both = []
                for z in range(2):
                    j = 2 * pair + z + 1
                    mids, grads = [], []
                    for k in (2 * slot, 2 * slot + 1):
                        mid = wide_ref[j, k, here, :]
                        yp, ym = lane_shifts(mid)
                        mids.append(mid)
                        grads.append(
                            (
                                wide_ref[j, k, pl.ds(PAD + r + 1, 8), :] - wide_ref[j, k, pl.ds(PAD + r - 1, 8), :],
                                yp - ym,
                                wide_ref[j + 1, k, here, :] - wide_ref[j - 1, k, here, :],
                            )
                        )
                    u, w = mids
                    density = u * u + w * w
                    both.append(
                        [
                            0.5 * (u * grads[1][comp] - w * grads[0][comp])
                            + field_ref[j + MARGIN - 1, comp, r : r + 8, :] * density
                            for comp in range(3)
                        ]
                    )
                for comp in range(3):
                    even, odd = both[0][comp], both[1][comp]
                    rows = pl.ds(pl.multiple_of((comp * DEPTH + 2 * pair) * ROWS, 8), 8)
                    flow_ref[slot, tile, 0, rows, :] = jnp.where(low, even, pltpu.roll(odd, 4, 0))
                    flow_ref[slot, tile, 1, rows, :] = jnp.where(low, pltpu.roll(even, 4, 0), odd)


def current(wide, field):
    return call("current", current_body, [(2, TILES, 2, PACK, NY)], [vmem(), vmem()], flops=10000000, limit=10)(
        wide, field
    )[0]


def weigh_body(prior_ref, n_ref, nchip_ref, nhalf_ref, nboth_ref, flow_ref, out_ref, scale_ref):
    half = half_index()
    weights = []
    for slot, occ_ref in enumerate((n_ref, nhalf_ref)):
        sums = (n_ref[slot] + nchip_ref[slot]) + (nhalf_ref[1 - slot] + nboth_ref[1 - slot])
        norm = jnp.sum(jnp.sum(sums, axis=1, keepdims=True), axis=0, keepdims=True)
        prior = prior_ref[slot, 0:1, :]
        mean = prior * prior * (norm * (1.0 / CELLS)) + EPSILON
        scale = prior / jnp.sqrt(mean)
        scale_ref[slot] = jnp.broadcast_to(scale, (8, NY))
        weights.append(scale * scale * (occ_ref[2, 0:1, :] * (0.5 / ORBS)))

    @pl.loop(0, GROUP // 2)
    def _(i):
        for side in range(2):
            out_ref[i, side] = flow_ref[0, i + half, side] * weights[0] + flow_ref[1, i + half, side] * weights[1]


def weigh(prior, norms, flow):
    return call(
        "weigh", weigh_body, [(GROUP // 2, 2, PACK, NY), (2, 8, NY)], [vmem()] * 6, flops=500000
    )(prior, *norms, flow)


def curl_body(field_ref, rows_ref, out_ref):
    owner = lax.axis_index("orb")
    place = lax.rem(owner, GROUP)
    tile = place // 2 + half_index()
    odd = lax.rem(place, 2)
    row = lax.broadcasted_iota(jnp.int32, (8, NY), 0)
    keep = ((owner > 0) | (row != 0)) & ((owner < ORBS - 1) | (row != ROWS + 1))
    starts = [pl.multiple_of(8 * jnp.clip(tile + k, 0, TILES - 1), 8) for k in (-1, 0, 1)]

    def window(z, comp):
        before, middle, after = [field_ref[z + MARGIN, comp, pl.ds(s, 8), :] for s in starts]
        first = jnp.where(odd == 1, middle, before)
        second = jnp.where(odd == 1, after, middle)
        shift_first = jnp.where(odd == 1, pltpu.roll(first, 5, 0), pltpu.roll(first, 1, 0))
        shift_second = jnp.where(odd == 1, pltpu.roll(second, 5, 0), pltpu.roll(second, 1, 0))
        split = jnp.where(odd == 1, 5, 1)
        return jnp.where(keep, jnp.where(row < split, shift_first, shift_second), 0.0)

    def x_plus(v):
        return pltpu.roll(v, 7, 0)

    def x_minus(v):
        return pltpu.roll(v, 1, 0)

    planes = [[window(z, comp) for comp in range(3)] for z in range(-1, DEPTH + 1)]
    for z in range(DEPTH):
        ax, ay, az = planes[z + 1]
        axm, aym, azm = planes[z]
        axp, ayp, azp = planes[z + 2]
        ax_up, ax_dn = lane_shifts(ax)
        ay_dn = lane_shifts(ay)[1]
        az_up, az_dn = lane_shifts(az)
        dy_ay = ay - ay_dn
        dx_ax = ax - x_minus(ax)
        inner_x = dy_ay + (az - azm)
        inner_y = dx_ax + (az - azm)
        inner_z = dx_ax + dy_ay
        up_inner_z = (axp - x_minus(axp)) + (ayp - lane_shifts(ayp)[1])
        out_x = (x_plus(inner_x) - inner_x) - (ax_up + ax_dn + axp + axm - 4.0 * ax)
        out_y = (lane_shifts(inner_y)[0] - inner_y) - (x_plus(ay) + x_minus(ay) + ayp + aym - 4.0 * ay)
        out_z = (up_inner_z - inner_z) - (x_plus(az) + x_minus(az) + az_up + az_dn - 4.0 * az)
        for comp, value in enumerate((out_x, out_y, out_z)):
            out_ref[1, pl.ds((comp * DEPTH + z) * ROWS, ROWS), :] = pltpu.roll(value, 7, 0)[0:ROWS]
    e_part = rows_ref[1] + WAVE_STEP * out_ref[1]
    out_ref[1] = e_part
    out_ref[0] = rows_ref[0] - WAVE_STEP * e_part


def double_curl(field, rows):
    return call("double_curl", curl_body, [(2, PACK, NY)], [vmem()] * 2, flops=1000000)(field, rows)[0]


def update_body(last, got_ref, part_ref, *outs):
    total = got_ref[0]
    for i in range(1, GROUP):
        total = total + got_ref[i]
    e_new = part_ref[1] - WAVE_STEP * total
    a_new = part_ref[0] + WAVE_STEP * WAVE_STEP * total
    if last:
        for ref, value in zip(outs, (e_new, a_new)):
            for comp in range(3):
                for z in range(DEPTH):
                    start = (comp * DEPTH + z) * ROWS
                    ref[comp, pl.ds(z, ROWS, stride=DEPTH), :] = value[start : start + ROWS]
    else:
        copies_ref, rows_ref = outs
        rows_ref[0] = a_new
        rows_ref[1] = e_new
        for i in range(GROUP):
            copies_ref[i] = a_new


def update(last, got, part):
    if last:
        outs = [(3, ROWS * DEPTH, NY)] * 2
    else:
        outs = [(GROUP, PACK, NY), (2, PACK, NY)]
    return call("update", functools.partial(update_body, last), outs, [vmem()] * 2, flops=500000)(got, part)


def hand_back_body(wide_ref, early_ref, late_ref):
    half = half_index()
    for z in range(DEPTH):
        for part in range(2):
            rows = own_rows(wide_ref[z + 1, 2 + part, PAD : PAD + LOCAL, :], half)
            if z < EARLY:
                early_ref[z, part] = rows
            else:
                late_ref[z - EARLY, part] = rows


def hand_back(wide):
    return call(
        "hand_back", hand_back_body, [(EARLY, 2, HALF, NY), (DEPTH - EARLY, 2, HALF, NY)], [vmem()]
    )(wide)


def finish_body(scale_ref, wide_ref, early_ref, late_ref, out_ref):
    half = half_index()
    scale = scale_ref[0, 0:1, :]
    for z in range(DEPTH):
        for part in range(2):
            mine = own_rows(wide_ref[z + 1, part, PAD : PAD + LOCAL, :], half) * scale
            theirs = (early_ref[z, part] if z < EARLY else late_ref[z - EARLY, part]) * scale
            out_ref[part, pl.ds(z, HALF, stride=DEPTH), :] = jnp.where(half == 0, mine, theirs)
            out_ref[part, pl.ds(HALF * DEPTH + z, HALF, stride=DEPTH), :] = jnp.where(half == 0, theirs, mine)


def finish(scale, wide, early, late):
    return call("finish", finish_body, [(2, NX * DEPTH, NY)], [vmem()] * 4)(scale, wide, early, late)[0]


def everyone(copies):
    return lax.all_to_all(copies, "orb", 0, 0, tiled=True, axis_index_groups=GROUPS)


def per_device(orbitals, potential, occupation, e_field, a_field):
    got = everyone(spread(a_field))
    own, swap, weight, core, chip, chipx, rows = prepare(orbitals, potential, a_field, e_field)
    vcore, vchip, chipx = send(core, CORE), send(chip, CHIP), send(chipx, CHIP_ACROSS)
    other = send(swap, HALVES)
    got, vcore = lax.optimization_barrier((got, vcore))
    scale = jnp.ones((2, 8, NY), F32)
    for step in range(STEPS):
        last = step == STEPS - 1
        field, edge, acore, achip, achipx = assemble(got)
        acore = send(acore, CORE)
        achip = send(achip, CHIP)
        edge = send(corners(edge, acore), HALVES)
        achipx = send(achipx, CHIP_ACROSS)
        if step == 0:
            edge, achipx, other = lax.optimization_barrier((edge, achipx, other))
        if step == 0:
            orbs = (own, other, vcore, vchip, send(lend(other), CORE), chipx)
        base, v = stage(2 * HALO * step, orbs, weight, vcore, vchip)
        wide, norm, field = propagate(occupation, base, v, (field, edge, acore, achip, achipx))
        norm, late_wide = lax.optimization_barrier((norm + send(norm, CORE), wide))
        norms = (norm, send(norm, CHIP_SUM), send(norm, HALVES), send(norm, BOTH_SUM))
        flow = current(wide, field)
        if last:
            early, late = hand_back(late_wide)
            early = send(early, HALVES)
        else:
            edge = send(edges(late_wide), HALVES)
            flow, edge = lax.optimization_barrier((flow, edge))
        flow, scale = weigh(scale, norms, flow)
        if last:
            flow, early, late = lax.optimization_barrier((flow, early, late))
            late = send(late, HALVES)
        flows = everyone(flow.reshape(GROUP, PACK, NY))
        part = double_curl(field, rows)
        if not last:
            own, other, core, chip, chipx = rims(wide, edge)
            core, chip = send(core, CORE), send(chip, CHIP)
            flows, core, chip, chipx = lax.optimization_barrier((flows, core, chip, chipx))
            chipx = send(chipx, CHIP)
            copies, rows = update(last, flows, part)
            got = everyone(copies)
            got, chipx = lax.optimization_barrier((got, chipx))
            orbs = (own, other, core, chip, core, chipx)
        else:
            e_new, a_new = update(last, flows, part)
            orbitals = finish(scale, wide, early, late)
    return (
        orbitals.reshape(1, 2, NX, DEPTH, NY),
        e_new.reshape(3, ROWS, DEPTH, NY),
        a_new.reshape(3, ROWS, DEPTH, NY),
    )


def solution(mesh):
    return jax.shard_map(
        per_device,
        mesh=mesh,
        in_specs=(
            P("orb", None, None, "slab", None),
            P(None, "slab", None),
            P("orb"),
            P(None, "orb", "slab", None),
            P(None, "orb", "slab", None),
        ),
        out_specs=(
            P("orb", None, None, "slab", None),
            P(None, "orb", "slab", None),
            P(None, "orb", "slab", None),
        ),
        check_vma=False,
    )
```

```python
import functools

import jax
import jax.numpy as jnp
from jax import lax
from jax.experimental import pallas as pl
from jax.experimental.pallas import tpu as pltpu
from jax.sharding import PartitionSpec as P

TERMS = 4
STEPS = 2
TIME_STEP = 0.3
WAVE_STEP = 0.5
EPSILON = 1e-06

NX = 128
NY = 128
NZ = 32
ORBS = 32
SLABS = 4
CELLS = NX * NY * NZ
DEPTH = NZ // SLABS
ROWS = NX // ORBS
HALO = TERMS + 1
MARGIN = TERMS
WIDE = DEPTH + 2 * HALO
PAD = 8
PACK = 3 * DEPTH * ROWS
CHUNK = 8
F32 = jnp.float32

HALF = NX // 2
LOCAL = HALF + 8
XL = LOCAL + 2 * PAD
GROUP = ORBS // 2
TILES = LOCAL // 8
EARLY = 3
ALL = ("orb", "slab")
MEETING = (1, 2)


def pairs(flip, move):
    found = []
    for orb in range(ORBS):
        for slab in range(SLABS):
            to = move(slab)
            if to is not None:
                found.append((orb * SLABS + slab, (orb ^ flip) * SLABS + to))
    return found


def over_core(slab):
    return slab ^ 1


def over_chip(slab):
    return 3 - slab if slab in MEETING else None


HALVES = pairs(GROUP, lambda slab: slab)
CORE = pairs(0, over_core)
CHIP = pairs(0, over_chip)
CHIP_ACROSS = pairs(GROUP, over_chip)
CHIP_SUM = pairs(0, lambda slab: slab ^ 2)
BOTH_SUM = pairs(GROUP, lambda slab: slab ^ 2)
GROUPS = [list(range(GROUP)), list(range(GROUP, ORBS))]


def send(value, table):
    return lax.ppermute(value, ALL, table)


def vmem():
    return pl.BlockSpec(memory_space=pltpu.VMEM)


def smem():
    return pl.BlockSpec(memory_space=pltpu.SMEM)


def call(name, body, outs, ins, scratch=(), flops=1000000, limit=8):
    shapes = [jax.ShapeDtypeStruct(s, F32) for s in outs]
    size = sum(4 * s.size for s in shapes)
    return pl.pallas_call(
        body,
        name=name,
        out_shape=shapes,
        in_specs=ins,
        out_specs=[vmem()] * len(outs),
        scratch_shapes=list(scratch),
        compiler_params=pltpu.CompilerParams(vmem_limit_bytes=limit * 1024 * 1024),
        cost_estimate=pl.CostEstimate(flops=flops, bytes_accessed=2 * size, transcendentals=0),
    )


def core_index():
    return lax.rem(lax.axis_index("slab"), 2)


def half_index():
    return lax.axis_index("orb") // GROUP


def split_rows(value, half):
    low, high = value[0:LOCAL], value[NX - LOCAL : NX]
    return jnp.where(half == 0, low, high), jnp.where(half == 0, high, low)


def own_rows(value, half):
    return jnp.where(half == 0, value[0:HALF], value[8 : 8 + HALF])


def lane_shifts(value):
    lane = lax.broadcasted_iota(jnp.int32, value.shape, value.ndim - 1)
    plus = jnp.where(lane == NY - 1, 0.0, pltpu.roll(value, NY - 1, value.ndim - 1))
    minus = jnp.where(lane == 0, 0.0, pltpu.roll(value, 1, value.ndim - 1))
    return plus, minus


def half_rows(shape):
    return lax.broadcasted_iota(jnp.int32, shape, len(shape) - 2) % 8 < 4


def to_rows(ref, rows_ref):
    for comp in range(3):
        for z in range(DEPTH):
            rows_ref[pl.ds((comp * DEPTH + z) * ROWS, ROWS), :] = ref[comp, pl.ds(z, ROWS, stride=DEPTH), :]


def prepare_body(
    orb_ref, pot_ref, a_ref, e_ref, own_ref, swap_ref, weight_ref, core_ref, chip_ref, chipx_ref, rows_ref
):
    core, half = core_index(), half_index()
    to_rows(a_ref, rows_ref.at[0])
    to_rows(e_ref, rows_ref.at[1])
    for z in range(DEPTH):
        for part in range(2):
            own_ref[z, part], swap_ref[z, part] = split_rows(orb_ref[part, pl.ds(z, NX, stride=DEPTH), :], half)
        weight_ref[z] = split_rows(2.0 * pot_ref[pl.ds(z, NX, stride=DEPTH), :] + 6.0, half)[0]
    to_core = (1 - core) * (DEPTH - HALO)
    to_chip = core * (DEPTH - HALO)
    for i in range(HALO):
        for part in range(2):
            core_ref[2 * i + part] = own_ref[to_core + i, part]
            chip_ref[2 * i + part] = own_ref[to_chip + i, part]
            chipx_ref[2 * i + part] = swap_ref[to_chip + i, part]
    for i in range(MARGIN):
        core_ref[2 * HALO + i] = weight_ref[(1 - core) * (DEPTH - MARGIN) + i]
        chip_ref[2 * HALO + i] = weight_ref[core * (DEPTH - MARGIN) + i]


def prepare(orbitals, potential, a_field, e_field):
    planes = 2 * HALO + MARGIN
    return call(
        "prepare",
        prepare_body,
        [(DEPTH, 2, LOCAL, NY)] * 2
        + [(DEPTH, LOCAL, NY)]
        + [(planes, LOCAL, NY)] * 2
        + [(2 * HALO, LOCAL, NY)]
        + [(2, PACK, NY)],
        [vmem()] * 4,
        limit=12,
    )(
        orbitals.reshape(2, NX * DEPTH, NY),
        potential.reshape(NX * DEPTH, NY),
        a_field.reshape(3, ROWS * DEPTH, NY),
        e_field.reshape(3, ROWS * DEPTH, NY),
    )


def lend_body(other_ref, out_ref):
    to_core = (1 - core_index()) * (DEPTH - HALO)
    for i in range(HALO):
        for part in range(2):
            out_ref[2 * i + part] = other_ref[to_core + i, part]


def lend(other):
    return call("lend", lend_body, [(2 * HALO, LOCAL, NY)], [vmem()])(other)[0]


def edges_body(wide_ref, out_ref):
    half = half_index()
    for z in range(DEPTH):
        for k in range(4):
            low = wide_ref[z + 1, k, PAD + HALF - 8 : PAD + HALF, :]
            out_ref[z, k] = jnp.where(half == 0, low, wide_ref[z + 1, k, PAD + 8 : PAD + 16, :])


def edges(wide):
    return call("edges", edges_body, [(DEPTH, 4, 8, NY)], [vmem()])(wide)[0]


def rims_body(wide_ref, edge_ref, own_ref, other_ref, core_ref, chip_ref, chipx_ref):
    core, half = core_index(), half_index()
    for z in range(DEPTH):
        for slot, ref in enumerate((own_ref, other_ref)):
            for part in range(2):
                value = wide_ref[z + 1, 2 * slot + part, PAD : PAD + LOCAL, :]
                edge = edge_ref[z, 2 * (1 - slot) + part]
                ref[z, part, 0:8, :] = jnp.where(half == 0, value[0:8], edge)
                ref[z, part, 8:HALF, :] = value[8:HALF]
                ref[z, part, HALF:LOCAL, :] = jnp.where(half == 0, edge, value[HALF:LOCAL])
    to_core = (1 - core) * (DEPTH - HALO)
    to_chip = core * (DEPTH - HALO)
    for i in range(HALO):
        for slot, ref in enumerate((own_ref, other_ref)):
            for part in range(2):
                core_ref[2 * (HALO * slot + i) + part] = ref[to_core + i, part]
                (chip_ref, chipx_ref)[slot][2 * i + part] = ref[to_chip + i, part]


def rims(wide, edge):
    return call(
        "rims", rims_body, [(DEPTH, 2, LOCAL, NY)] * 2 + [(4 * HALO, LOCAL, NY)] + [(2 * HALO, LOCAL, NY)] * 2, [vmem()] * 2, limit=12
    )(wide, edge)


def spread_body(a_ref, copies_ref, rows_ref):
    to_rows(a_ref, rows_ref)
    value = rows_ref[...]
    for i in range(GROUP):
        copies_ref[i] = value


def spread(a_field):
    return call("spread", spread_body, [(GROUP, PACK, NY)], [vmem()], [pltpu.VMEM((PACK, NY), F32)])(
        a_field.reshape(3, ROWS * DEPTH, NY)
    )[0]


def assemble_body(got_ref, field_ref, edge_ref, core_ref, chip_ref, chipx_ref):
    core, half = core_index(), half_index()
    low = half_rows((GROUP // 2, 8, NY))
    for comp in range(3):
        for pair in range(DEPTH // 2):
            rows = pl.ds((comp * DEPTH + 2 * pair) * ROWS, 8)
            first = got_ref[:, 0, rows, :]
            second = got_ref[:, 1, rows, :]
            even = jnp.where(low, first, pltpu.roll(second, 4, 1))
            odd = jnp.where(low, pltpu.roll(first, 4, 1), second)
            for z, value in ((2 * pair, even), (2 * pair + 1, odd)):
                field_ref[z, comp] = value.reshape(HALF, NY)
                edge_ref[z, comp] = jnp.where(half == 0, pltpu.roll(value[GROUP // 2 - 1], 4, 0), value[0])[0:ROWS]
    for i in range(MARGIN):
        to_core = (1 - core) * (DEPTH - MARGIN) + i
        to_chip = core * (DEPTH - MARGIN) + i
        for comp in range(3):
            core_ref[i, comp] = field_ref[to_core, comp]
            chip_ref[i, comp] = field_ref[to_chip, comp]
            chipx_ref[i, comp] = edge_ref[to_chip, comp]


def assemble(got):
    return call(
        "assemble",
        assemble_body,
        [(DEPTH, 3, HALF, NY), (DEPTH, 3, ROWS, NY)]
        + [(MARGIN, 3, HALF, NY)] * 2
        + [(MARGIN, 3, ROWS, NY)],
        [vmem()],
    )(got.reshape(GROUP // 2, 2, PACK, NY))


def corners_body(edge_ref, core_ref, out_ref):
    core, half = core_index(), half_index()
    for comp in range(3):
        for z in range(DEPTH):
            out_ref[z + MARGIN * core, comp] = edge_ref[z, comp]
        for i in range(MARGIN):
            out_ref[(1 - core) * DEPTH + i, comp] = jnp.where(
                half == 0, core_ref[i, comp, HALF - ROWS : HALF, :], core_ref[i, comp, 0:ROWS, :]
            )


def corners(edge, acore):
    return call("corners", corners_body, [(DEPTH + MARGIN, 3, ROWS, NY)], [vmem()] * 2)(edge, acore)[0]


def clear(ref, count):
    zeros = jnp.zeros((PAD, NY), F32)

    @pl.loop(0, count)
    def _(j):
        for k in range(4):
            ref[j, k, 0:PAD, :] = zeros
            ref[j, k, PAD + LOCAL : XL, :] = zeros


def stage_body(
    first, own_ref, other_ref, hcore_ref, hchip_ref, hcorex_ref, hchipx_ref, weight_ref, vcore_ref, vchip_ref,
    base_ref, v_ref,
):
    core = core_index()
    clear(base_ref, WIDE)

    @pl.loop(0, DEPTH)
    def _(z):
        for part in range(2):
            base_ref[z + HALO, part, PAD : PAD + LOCAL, :] = own_ref[z, part]
            base_ref[z + HALO, 2 + part, PAD : PAD + LOCAL, :] = other_ref[z, part]
        v_ref[z + MARGIN] = weight_ref[z]

    def put_halo(above, orb_ref, orbx_ref, offset, pot_ref):
        @pl.loop(0, HALO)
        def _(i):
            j = above * (DEPTH + HALO) + i
            for part in range(2):
                base_ref[j, part, PAD : PAD + LOCAL, :] = orb_ref[2 * i + part]
                base_ref[j, 2 + part, PAD : PAD + LOCAL, :] = orbx_ref[offset + 2 * i + part]

        @pl.loop(0, MARGIN)
        def _(i):
            v_ref[above * (DEPTH + MARGIN) + i] = pot_ref[2 * HALO + i]

    @pl.when(core == 1)
    def _():
        put_halo(0, hcore_ref, hcorex_ref, first, vcore_ref)
        put_halo(1, hchip_ref, hchipx_ref, 0, vchip_ref)

    @pl.when(core == 0)
    def _():
        put_halo(1, hcore_ref, hcorex_ref, first, vcore_ref)
        put_halo(0, hchip_ref, hchipx_ref, 0, vchip_ref)


def stage(first, orbs, weight, vcore, vchip):
    return call(
        "stage",
        functools.partial(stage_body, first),
        [(WIDE, 4, XL, NY), (DEPTH + 2 * MARGIN, LOCAL, NY)],
        [vmem()] * 9,
        flops=1000000,
        limit=16,
    )(*orbs, weight, vcore, vchip)


def propagate_body(
    occ_ref, base_ref, v_ref, field_ref, edge_ref, acore_ref, achip_ref, achipx_ref,
    out_ref, norm_ref, a_ref, ping_ref, pong_ref, w_ref,
):
    core, half = core_index(), half_index()
    clear(ping_ref, WIDE)
    clear(pong_ref, WIDE)
    clear(out_ref, DEPTH + 2)

    near = half_rows((8, NY)) == (half == 0)

    def put_field(j, fld_ref, edg_ref, i, k):
        total = v_ref[j]
        for comp in range(3):
            value, edge = fld_ref[i, comp], edg_ref[k, comp]
            edge = jnp.where(near, jnp.concatenate([edge, edge], axis=0), 0.0)
            joined = jnp.where(
                half == 0, jnp.concatenate([value, edge], axis=0), jnp.concatenate([edge, value], axis=0)
            )
            a_ref[j, comp] = joined
            total = total + joined * joined
        w_ref[j] = total

    @pl.loop(0, DEPTH)
    def _(z):
        put_field(z + MARGIN, field_ref, edge_ref, z, z + MARGIN * core)

    @pl.loop(0, MARGIN)
    def _(i):
        put_field((1 - core) * (DEPTH + MARGIN) + i, acore_ref, edge_ref, i, (1 - core) * DEPTH + i)
        put_field(core * (DEPTH + MARGIN) + i, achip_ref, achipx_ref, i, i)

    first = lax.axis_index("slab") * DEPTH - HALO
    sums = [jnp.zeros((8, NY), F32), jnp.zeros((8, NY), F32)]

    def plane(j, order, source, target, shift):
        depth = first + j
        inside = jnp.where((depth >= 0) & (depth < NZ), 1.0, 0.0).astype(F32)
        factor = inside * (0.5 * TIME_STEP / order)
        for r in range(0, LOCAL, CHUNK):
            here = pl.ds(PAD + r, CHUNK)
            fields = [a_ref[j - 1, comp, r : r + CHUNK, :] for comp in range(3)]
            weight = w_ref[j - 1, r : r + CHUNK, :]
            for slot in range(2):
                centre, total, drift = [], [], []
                for k in (2 * slot, 2 * slot + 1):
                    mid = source[j, k, here, :]
                    xp = source[j, k, pl.ds(PAD + r + 1, CHUNK), :]
                    xm = source[j, k, pl.ds(PAD + r - 1, CHUNK), :]
                    zp = source[j + 1, k, here, :]
                    zm = source[j - 1, k, here, :]
                    yp, ym = lane_shifts(mid)
                    centre.append(mid)
                    total.append((xp + xm) + (yp + ym) + (zp + zm))
                    drift.append(fields[0] * (xp - xm) + fields[1] * (yp - ym) + fields[2] * (zp - zm))
                real_h = weight * centre[0] - total[0] + drift[1]
                imag_h = weight * centre[1] - total[1] - drift[0]
                for part, change in enumerate((factor * imag_h, -factor * real_h)):
                    value = base_ref[j, 2 * slot + part, here, :] + change
                    target[j + shift, 2 * slot + part, here, :] = value
                    if order == 1 and HALO <= j < HALO + DEPTH:
                        square = value * value
                        if r == 0:
                            square = jnp.where(half == 0, square, 0.0)
                        if r == LOCAL - 8:
                            square = jnp.where(half == 1, square, 0.0)
                        sums[slot] = sums[slot] + square

    source = base_ref
    for done, order in enumerate(range(TERMS, 0, -1)):
        target = out_ref if order == 1 else (ping_ref, pong_ref)[done % 2]
        for j in range(done + 1, WIDE - done - 1):
            plane(j, order, source, target, 1 - HALO if order == 1 else 0)
        source = target
    norm_ref[0] = sums[0]
    norm_ref[1] = sums[1]
    norm_ref[2] = jnp.broadcast_to(occ_ref[0], (8, NY))


def propagate(occupation, base, v, fields):
    return call(
        "propagate",
        propagate_body,
        [(DEPTH + 2, 4, XL, NY), (3, 8, NY), (DEPTH + 2 * MARGIN, 3, LOCAL, NY)],
        [smem()] + [vmem()] * 7,
        [
            pltpu.VMEM((WIDE, 4, XL, NY), F32),
            pltpu.VMEM((WIDE, 4, XL, NY), F32),
            pltpu.VMEM((DEPTH + 2 * MARGIN, LOCAL, NY), F32),
        ],
        flops=60000000,
        limit=26,
    )(occupation, base, v, *fields)


def current_body(wide_ref, field_ref, flow_ref):
    low = half_rows((8, NY))

    @pl.loop(0, DEPTH // 2)
    def _(pair):
        for tile in range(TILES):
            r = 8 * tile
            here = pl.ds(PAD + r, 8)
            for slot in range(2):
                both = []
                for z in range(2):
                    j = 2 * pair + z + 1
                    mids, grads = [], []
                    for k in (2 * slot, 2 * slot + 1):
                        mid = wide_ref[j, k, here, :]
                        yp, ym = lane_shifts(mid)
                        mids.append(mid)
                        grads.append(
                            (
                                wide_ref[j, k, pl.ds(PAD + r + 1, 8), :] - wide_ref[j, k, pl.ds(PAD + r - 1, 8), :],
                                yp - ym,
                                wide_ref[j + 1, k, here, :] - wide_ref[j - 1, k, here, :],
                            )
                        )
                    u, w = mids
                    density = u * u + w * w
                    both.append(
                        [
                            0.5 * (u * grads[1][comp] - w * grads[0][comp])
                            + field_ref[j + MARGIN - 1, comp, r : r + 8, :] * density
                            for comp in range(3)
                        ]
                    )
                for comp in range(3):
                    even, odd = both[0][comp], both[1][comp]
                    rows = pl.ds(pl.multiple_of((comp * DEPTH + 2 * pair) * ROWS, 8), 8)
                    flow_ref[slot, tile, 0, rows, :] = jnp.where(low, even, pltpu.roll(odd, 4, 0))
                    flow_ref[slot, tile, 1, rows, :] = jnp.where(low, pltpu.roll(even, 4, 0), odd)


def current(wide, field):
    return call("current", current_body, [(2, TILES, 2, PACK, NY)], [vmem(), vmem()], flops=10000000, limit=10)(
        wide, field
    )[0]


def weigh_body(prior_ref, n_ref, nchip_ref, nhalf_ref, nboth_ref, flow_ref, out_ref, scale_ref):
    half = half_index()
    weights = []
    for slot, occ_ref in enumerate((n_ref, nhalf_ref)):
        sums = (n_ref[slot] + nchip_ref[slot]) + (nhalf_ref[1 - slot] + nboth_ref[1 - slot])
        norm = jnp.sum(jnp.sum(sums, axis=1, keepdims=True), axis=0, keepdims=True)
        prior = prior_ref[slot, 0:1, :]
        mean = prior * prior * (norm * (1.0 / CELLS)) + EPSILON
        scale = prior / jnp.sqrt(mean)
        scale_ref[slot] = jnp.broadcast_to(scale, (8, NY))
        weights.append(scale * scale * (occ_ref[2, 0:1, :] * (0.5 / ORBS)))

    @pl.loop(0, GROUP // 2)
    def _(i):
        for side in range(2):
            out_ref[i, side] = flow_ref[0, i + half, side] * weights[0] + flow_ref[1, i + half, side] * weights[1]


def weigh(prior, norms, flow):
    return call(
        "weigh", weigh_body, [(GROUP // 2, 2, PACK, NY), (2, 8, NY)], [vmem()] * 6, flops=500000
    )(prior, *norms, flow)


def curl_body(field_ref, rows_ref, out_ref):
    owner = lax.axis_index("orb")
    place = lax.rem(owner, GROUP)
    tile = place // 2 + half_index()
    odd = lax.rem(place, 2)
    row = lax.broadcasted_iota(jnp.int32, (8, NY), 0)
    keep = ((owner > 0) | (row != 0)) & ((owner < ORBS - 1) | (row != ROWS + 1))
    starts = [pl.multiple_of(8 * jnp.clip(tile + k, 0, TILES - 1), 8) for k in (-1, 0, 1)]

    def window(z, comp):
        before, middle, after = [field_ref[z + MARGIN, comp, pl.ds(s, 8), :] for s in starts]
        first = jnp.where(odd == 1, middle, before)
        second = jnp.where(odd == 1, after, middle)
        shift_first = jnp.where(odd == 1, pltpu.roll(first, 5, 0), pltpu.roll(first, 1, 0))
        shift_second = jnp.where(odd == 1, pltpu.roll(second, 5, 0), pltpu.roll(second, 1, 0))
        split = jnp.where(odd == 1, 5, 1)
        return jnp.where(keep, jnp.where(row < split, shift_first, shift_second), 0.0)

    def x_plus(v):
        return pltpu.roll(v, 7, 0)

    def x_minus(v):
        return pltpu.roll(v, 1, 0)

    planes = [[window(z, comp) for comp in range(3)] for z in range(-1, DEPTH + 1)]
    for z in range(DEPTH):
        ax, ay, az = planes[z + 1]
        axm, aym, azm = planes[z]
        axp, ayp, azp = planes[z + 2]
        ax_up, ax_dn = lane_shifts(ax)
        ay_dn = lane_shifts(ay)[1]
        az_up, az_dn = lane_shifts(az)
        dy_ay = ay - ay_dn
        dx_ax = ax - x_minus(ax)
        inner_x = dy_ay + (az - azm)
        inner_y = dx_ax + (az - azm)
        inner_z = dx_ax + dy_ay
        up_inner_z = (axp - x_minus(axp)) + (ayp - lane_shifts(ayp)[1])
        out_x = (x_plus(inner_x) - inner_x) - (ax_up + ax_dn + axp + axm - 4.0 * ax)
        out_y = (lane_shifts(inner_y)[0] - inner_y) - (x_plus(ay) + x_minus(ay) + ayp + aym - 4.0 * ay)
        out_z = (up_inner_z - inner_z) - (x_plus(az) + x_minus(az) + az_up + az_dn - 4.0 * az)
        for comp, value in enumerate((out_x, out_y, out_z)):
            out_ref[1, pl.ds((comp * DEPTH + z) * ROWS, ROWS), :] = pltpu.roll(value, 7, 0)[0:ROWS]
    e_part = rows_ref[1] + WAVE_STEP * out_ref[1]
    out_ref[1] = e_part
    out_ref[0] = rows_ref[0] - WAVE_STEP * e_part


def double_curl(field, rows):
    return call("double_curl", curl_body, [(2, PACK, NY)], [vmem()] * 2, flops=1000000)(field, rows)[0]


def update_body(last, got_ref, part_ref, *outs):
    total = got_ref[0]
    for i in range(1, GROUP):
        total = total + got_ref[i]
    e_new = part_ref[1] - WAVE_STEP * total
    a_new = part_ref[0] + WAVE_STEP * WAVE_STEP * total
    if last:
        for ref, value in zip(outs, (e_new, a_new)):
            for comp in range(3):
                for z in range(DEPTH):
                    start = (comp * DEPTH + z) * ROWS
                    ref[comp, pl.ds(z, ROWS, stride=DEPTH), :] = value[start : start + ROWS]
    else:
        copies_ref, rows_ref = outs
        rows_ref[0] = a_new
        rows_ref[1] = e_new
        for i in range(GROUP):
            copies_ref[i] = a_new


def update(last, got, part):
    if last:
        outs = [(3, ROWS * DEPTH, NY)] * 2
    else:
        outs = [(GROUP, PACK, NY), (2, PACK, NY)]
    return call("update", functools.partial(update_body, last), outs, [vmem()] * 2, flops=500000)(got, part)


def hand_back_body(wide_ref, early_ref, late_ref):
    half = half_index()
    for z in range(DEPTH):
        for part in range(2):
            rows = own_rows(wide_ref[z + 1, 2 + part, PAD : PAD + LOCAL, :], half)
            if z < EARLY:
                early_ref[z, part] = rows
            else:
                late_ref[z - EARLY, part] = rows


def hand_back(wide):
    return call(
        "hand_back", hand_back_body, [(EARLY, 2, HALF, NY), (DEPTH - EARLY, 2, HALF, NY)], [vmem()]
    )(wide)


def finish_body(scale_ref, wide_ref, early_ref, late_ref, out_ref):
    half = half_index()
    scale = scale_ref[0, 0:1, :]
    for z in range(DEPTH):
        for part in range(2):
            mine = own_rows(wide_ref[z + 1, part, PAD : PAD + LOCAL, :], half) * scale
            theirs = (early_ref[z, part] if z < EARLY else late_ref[z - EARLY, part]) * scale
            out_ref[part, pl.ds(z, HALF, stride=DEPTH), :] = jnp.where(half == 0, mine, theirs)
            out_ref[part, pl.ds(HALF * DEPTH + z, HALF, stride=DEPTH), :] = jnp.where(half == 0, theirs, mine)


def finish(scale, wide, early, late):
    return call("finish", finish_body, [(2, NX * DEPTH, NY)], [vmem()] * 4)(scale, wide, early, late)[0]


def everyone(copies):
    return lax.all_to_all(copies, "orb", 0, 0, tiled=True, axis_index_groups=GROUPS)


def per_device(orbitals, potential, occupation, e_field, a_field):
    got = everyone(spread(a_field))
    own, swap, weight, core, chip, chipx, rows = prepare(orbitals, potential, a_field, e_field)
    vcore, vchip, chipx = send(core, CORE), send(chip, CHIP), send(chipx, CHIP_ACROSS)
    other = send(swap, HALVES)
    got, vcore = lax.optimization_barrier((got, vcore))
    scale = jnp.ones((2, 8, NY), F32)
    for step in range(STEPS):
        last = step == STEPS - 1
        field, edge, acore, achip, achipx = assemble(got)
        acore = send(acore, CORE)
        achip = send(achip, CHIP)
        edge = corners(edge, acore)
        edge = send(edge, HALVES)
        if step == 0:
            edge, other = lax.optimization_barrier((edge, other))
        achipx = send(achipx, CHIP_ACROSS)
        if step == 0:
            orbs = (own, other, vcore, vchip, send(lend(other), CORE), chipx)
        base, v = stage(2 * HALO * step, orbs, weight, vcore, vchip)
        wide, norm, field = propagate(occupation, base, v, (field, edge, acore, achip, achipx))
        norm, late_wide = lax.optimization_barrier((norm + send(norm, CORE), wide))
        norms = (norm, send(norm, CHIP_SUM), send(norm, HALVES), send(norm, BOTH_SUM))
        flow = current(wide, field)
        if last:
            early, late = hand_back(late_wide)
            early = send(early, HALVES)
        else:
            edge = send(edges(late_wide), HALVES)
            flow, edge = lax.optimization_barrier((flow, edge))
        flow, scale = weigh(scale, norms, flow)
        if last:
            flow, early, late = lax.optimization_barrier((flow, early, late))
            late = send(late, HALVES)
        flows = everyone(flow.reshape(GROUP, PACK, NY))
        part = double_curl(field, rows)
        if not last:
            own, other, core, chip, chipx = rims(wide, edge)
            core, chip = send(core, CORE), send(chip, CHIP)
            flows, core, chip, chipx = lax.optimization_barrier((flows, core, chip, chipx))
            chipx = send(chipx, CHIP)
            copies, rows = update(last, flows, part)
            got = everyone(copies)
            got, chipx = lax.optimization_barrier((got, chipx))
            orbs = (own, other, core, chip, core, chipx)
        else:
            e_new, a_new = update(last, flows, part)
            orbitals = finish(scale, wide, early, late)
    return (
        orbitals.reshape(1, 2, NX, DEPTH, NY),
        e_new.reshape(3, ROWS, DEPTH, NY),
        a_new.reshape(3, ROWS, DEPTH, NY),
    )


def solution(mesh):
    return jax.shard_map(
        per_device,
        mesh=mesh,
        in_specs=(
            P("orb", None, None, "slab", None),
            P(None, "slab", None),
            P("orb"),
            P(None, "orb", "slab", None),
            P(None, "orb", "slab", None),
        ),
        out_specs=(
            P("orb", None, None, "slab", None),
            P(None, "orb", "slab", None),
            P(None, "orb", "slab", None),
        ),
        check_vma=False,
    )
```
